256 devices in a mesh: xs: 8 (over z), al: 32 (over x, y, core).
Axes of the slice: x: 4, y: 4, z: 8, core: 2. Of those that a mesh axis runs over, the one named last changes fastest.
Arguments:
- wave_state: float32 [3, 1024, 16384], P(None, 'xs', 'al'), as said below
- depth_class: int32 [1024, 16384], P('xs', 'al'), may hold values from 0 to 7
- onset_flag: int32 [1024, 16384], P('xs', 'al'), may hold values 0 or 1
- cessation: int32 [1024, 16384], P('xs', 'al'), may hold values 0 or 1
- class_depth: float32 [8], replicated, may hold values from 2 to 6
Outputs:
- tendency: float32 [3, 1024, 16384], P(None, 'xs', 'al')
The draws below stay inside these ranges and needn't reach their ends.
Inputs may be any that keep to these rules, and one draw needn't show every extreme that they name: wave_state[0], the surface elevation, stays within -0.9 to 0.9.
All inputs are finite; a program needn't handle non-finite values. No bound on the sum of `onset_flag` or of `cessation` on one device may be relied on, other than what follows from the above.
Results may differ from the reference program's by a relative error of at most 0.00011.
Values sent between devices are 32-bit elements; how exact they have to be, the bound alone decides.
A program may use at most 64 MiB of HBM per device.

```python
import math
import jax
import jax.numpy as jnp
from jax import lax

CLASSES = 8
ITERS = 8
NX = 1024
NY = 16384


def draw_wave_state(key, part):
    key = jax.random.fold_in(key, 11)
    cross = jnp.arange(NX, dtype=jnp.float32) / max(NX - 1, 1)
    envelope = jnp.exp(math.log(3.0) * cross)[:, None] * jnp.ones((1, NY), jnp.float32)
    scales = jnp.array([0.1, 0.6, 0.6], jnp.float32)[:, None, None]
    noise = jnp.clip(jax.random.normal(key, (3, NX, NY), jnp.float32), -3.0, 3.0)
    return noise * scales * envelope[None]


def set_ends(entries, stream_key, low, top_value):
    place = [jax.random.randint(jax.random.fold_in(stream_key, axis), (), 0, length) for axis, length in enumerate(entries.shape)]
    longest = entries.shape.index(max(entries.shape))
    next_to = place[:longest] + [(place[longest] + 1) % entries.shape[longest]] + place[longest + 1:]
    return entries.at[tuple(place)].set(low).at[tuple(next_to)].set(top_value)


def setup_inputs(seed: int = 0) -> dict:
    key_list = jax.random.split(jax.random.key(seed), 6)
    wave_state = draw_wave_state(jax.random.fold_in(key_list[5], 71), 0)
    depth_class = set_ends(jax.random.randint(key_list[1], (NX, NY), 0, CLASSES), jax.random.fold_in(key_list[1], 1), 0, CLASSES - 1).astype(jnp.int32)
    onset_flag = set_ends((jax.random.randint(key_list[2], (NX, NY), 0, 2) < 1).astype(jnp.int32), jax.random.fold_in(key_list[2], 1), 0, 1)
    cessation = set_ends((jax.random.randint(key_list[3], (NX, NY), 0, 4) < 1).astype(jnp.int32), jax.random.fold_in(key_list[3], 1), 0, 1)
    class_depth = jnp.clip(jax.random.uniform(key_list[4], (CLASSES,), jnp.float32, 2.0, 6.0), 2.0, 6.0)
    return dict(wave_state=wave_state, depth_class=depth_class, onset_flag=onset_flag, cessation=cessation, class_depth=class_depth)


pade_alpha = 1.0 / 3.0
stencil_near = 14.0 / 9.0
stencil_far = 1.0 / 9.0
gravity = 1.0
breaking_coef = 0.05
dispersion_coef = 1.0 / 3.0

def cross_derivative(quantity):
    padded = jnp.pad(quantity, ((2, 2), (0, 0)))
    source = 0.5 * stencil_near * (padded[3:-1] - padded[1:-3]) + 0.25 * stencil_far * (padded[4:] - padded[:-4])
    length = quantity.shape[0]
    position = jnp.arange(length)
    lower_band = jnp.where(position > 0, pade_alpha, 0.0).astype(quantity.dtype)
    upper_band = jnp.where(position < length - 1, pade_alpha, 0.0).astype(quantity.dtype)
    diagonal = jnp.ones((length,), quantity.dtype)
    return lax.linalg.tridiagonal_solve(lower_band, diagonal, upper_band, source)

def along_derivative(quantity):
    padded = jnp.concatenate([quantity[:, -2:], quantity, quantity[:, :2]], axis=1)
    source = 0.5 * stencil_near * (padded[:, 3:-1] - padded[:, 1:-3]) + 0.25 * stencil_far * (padded[:, 4:] - padded[:, :-4])
    turned = jnp.transpose(source)
    length = turned.shape[0]
    position = jnp.arange(length)
    lower_band = jnp.where(position > 0, pade_alpha, 0.0).astype(quantity.dtype)
    upper_band = jnp.where(position < length - 1, pade_alpha, 0.0).astype(quantity.dtype)
    diagonal = jnp.where(position == 0, 2.0, jnp.where(position == length - 1, 1.0 + pade_alpha * pade_alpha, 1.0)).astype(quantity.dtype)
    correction = jnp.where(position == 0, -1.0, jnp.where(position == length - 1, pade_alpha, 0.0)).astype(quantity.dtype)
    stacked = jnp.concatenate([turned, correction[:, None]], axis=1)
    solved = lax.linalg.tridiagonal_solve(lower_band, diagonal, upper_band, stacked)
    plain = solved[:, :-1]
    helper = solved[:, -1]
    numer = plain[0] - pade_alpha * plain[-1]
    denom = 1.0 + helper[0] - pade_alpha * helper[-1]
    result = plain - (numer / denom)[None, :] * helper[:, None]
    return jnp.transpose(result)

def dispersive_operator(flow_x, flow_y, coefficient):
    next_x = jnp.concatenate([flow_x[1:], jnp.zeros_like(flow_x[:1])], axis=0)
    next_y = jnp.roll(flow_y, -1, axis=1)
    potential = coefficient * (next_x - flow_x + (next_y - flow_y))
    prior_x = jnp.concatenate([jnp.zeros_like(potential[:1]), potential[:-1]], axis=0)
    prior_y = jnp.roll(potential, 1, axis=1)
    return (flow_x - (potential - prior_x), flow_y - (potential - prior_y))

def reference(wave_state, depth_class, onset_flag, cessation, class_depth):
    surface = wave_state[0]
    flux_x = wave_state[1]
    flux_y = wave_state[2]
    still_depth = jnp.zeros_like(surface)
    for class_id in range(CLASSES):
        still_depth = still_depth + jnp.where(depth_class == class_id, class_depth[class_id], 0.0)
    total_depth = still_depth + surface
    velocity_x = flux_x / total_depth
    velocity_y = flux_y / total_depth
    surface_dx = cross_derivative(surface)
    flux_xx = cross_derivative(flux_x)
    speed_ux = cross_derivative(velocity_x)
    speed_vx = cross_derivative(velocity_y)
    advect_uux = cross_derivative(flux_x * velocity_x)
    advect_uvx = cross_derivative(flux_x * velocity_y)
    surface_dy = along_derivative(surface)
    flux_yy = along_derivative(flux_y)
    speed_uy = along_derivative(velocity_x)
    speed_vy = along_derivative(velocity_y)
    advect_uvy = along_derivative(flux_x * velocity_y)
    advect_vvy = along_derivative(flux_y * velocity_y)
    surface_rate = -(flux_xx + flux_yy)
    active = (onset_flag * (1 - cessation)).astype(jnp.float32)
    viscosity = breaking_coef * active * total_depth * jnp.abs(surface_rate)
    stress_xx = 2.0 * viscosity * total_depth * speed_ux
    stress_xy = viscosity * total_depth * (speed_uy + speed_vx)
    stress_yy = 2.0 * viscosity * total_depth * speed_vy
    force_x = -advect_uux - advect_uvy - gravity * total_depth * surface_dx + cross_derivative(stress_xx) + along_derivative(stress_xy)
    force_y = -advect_uvx - advect_vvy - gravity * total_depth * surface_dy + cross_derivative(stress_xy) + along_derivative(stress_yy)
    coefficient = dispersion_coef * total_depth * total_depth
    solved_x = jnp.zeros_like(force_x)
    solved_y = jnp.zeros_like(force_y)
    residual_x, residual_y = (force_x, force_y)
    search_x, search_y = (force_x, force_y)
    norm_now = jnp.sum(residual_x * residual_x) + jnp.sum(residual_y * residual_y)
    for iteration in range(ITERS):
        image_x, image_y = dispersive_operator(search_x, search_y, coefficient)
        step_size = norm_now / (jnp.sum(search_x * image_x) + jnp.sum(search_y * image_y))
        solved_x = solved_x + step_size * search_x
        solved_y = solved_y + step_size * search_y
        residual_x = residual_x - step_size * image_x
        residual_y = residual_y - step_size * image_y
        norm_next = jnp.sum(residual_x * residual_x) + jnp.sum(residual_y * residual_y)
        growth = norm_next / norm_now
        search_x = residual_x + growth * search_x
        search_y = residual_y + growth * search_y
        norm_now = norm_next
    return jnp.stack([surface_rate, solved_x, solved_y])
```

```python
import functools

import jax
import jax.numpy as jnp
import numpy as np
from jax import lax
from jax.experimental import pallas as pl
from jax.experimental.pallas import tpu as pltpu
from jax.sharding import PartitionSpec as P

MESH = pl.DeviceIdType.MESH
CLASSES = 8
ITERS = 8
ROWS, COLS = 128, 512
HALO = 8
EROWS, ECOLS = ROWS + 2 * HALO, COLS + 128
FPAD = 16
Q = 1.0 / 3.0
A2 = 0.5 * 14.0 / 9.0
B4 = 0.25 / 9.0
BREAKING = 0.05
F32, BF16 = jnp.float32, jnp.bfloat16


def tridiagonal_inverse(length):
    band = np.eye(length) + Q * (np.eye(length, k=1) + np.eye(length, k=-1))
    return np.linalg.inv(band)


CORNER = float(tridiagonal_inverse(ROWS)[0, 0])
NEXT = (1.0 - CORNER) / Q
LINK = Q * CORNER
COUPLE = 1.0 / (1.0 - LINK * LINK)


def halves(matrix):
    matrix = matrix.astype(np.float32)
    high = matrix.astype(jnp.bfloat16)
    low = (matrix - high.astype(np.float32)).astype(jnp.bfloat16)
    return high, low


def split_bf16(value):
    high = value.astype(BF16)
    return high, (value - high.astype(F32)).astype(BF16)


def two_sum(a, b):
    s = a + b
    t = s - a
    return s, (a - (s - t)) + (b - t)


def quick_sum(a, b):
    s = a + b
    return s, b - (s - a)


def cut(a):
    t = 4097.0 * a
    high = t - (t - a)
    return high, a - high


def two_prod(a, b):
    p = a * b
    ah, al = cut(a)
    bh, bl = cut(b)
    return p, ((ah * bh - p) + ah * bl + al * bh) + al * bl


def dd_add(a, b):
    s, e = two_sum(a[0], b[0])
    t, f = two_sum(a[1], b[1])
    s, e = quick_sum(s, e + t)
    return quick_sum(s, e + f)


def dd_neg(a):
    return -a[0], -a[1]


def dd_mul(a, b):
    p, e = two_prod(a[0], b[0])
    return quick_sum(p, e + (a[0] * b[1] + a[1] * b[0]))


def dd_scale(a, b):
    p, e = two_prod(a[0], b)
    return quick_sum(p, e + a[1] * b)


def dd_half(a):
    return 0.5 * a[0], 0.5 * a[1]


def dd_div(a, b):
    first = a[0] / b[0]
    rest = dd_add(a, dd_neg(dd_scale(b, first)))
    return quick_sum(first, rest[0] / b[0])


def rolled(value, shift, axis):
    size = value.shape[axis]
    return pltpu.roll(value, shift % size, axis)


def iota(shape, axis):
    return lax.broadcasted_iota(jnp.int32, shape, axis)


def lane_source(field):
    d = rolled(field, -1, 1) - rolled(field, 1, 1)
    s = A2 * d + B4 * (rolled(d, -1, 1) + rolled(d, 1, 1))
    lane = iota(field.shape, 1)
    return jnp.where((lane >= 2) & (lane < COLS - 2), s, 0.0)


def row_source(around, start):
    d = rolled(around, -1, 0) - rolled(around, 1, 0)
    s = (A2 * d + B4 * (rolled(d, -1, 0) + rolled(d, 1, 0)))[8:24]
    row = iota(s.shape, 0) + start
    return jnp.where((row >= 2) & (row < ROWS - 2), s, 0.0)


def edge_items(f):
    return A2 * f[1] + B4 * f[2], A2 * (f[2] - f[0]) + B4 * f[3]


def kernel(nz, na, ws, dc, on, ce, cd, xh, xl, yh, yl, exl, exr, ey, out,
           wv, dv, ov, cv, xhv, xlv, yhv, ylv, exlv, exrv, eyv,
           fld, dep, sxh, sxl, syh, syl, hx, hy, er, ec, stress, part, ratev, solv,
           rowmsg, rowgot, colmsg, colgot, bx, by, cext, cs, cright, cleft, fright, fleft, fmsg, tau, crec,
           stmsg, stz, sta, dtmsg, dtz, dta, nsc,
           insem, outsem, ssem, rowsem, colsem, crowsem, ccolsem, ccorsem, frowsem, fcolsem, fcorsem,
           stzs, stas, dtzs, dtas, stzr, star, dtzr, dtar):
    z, a = lax.axis_index("xs"), lax.axis_index("al")
    up, down = lax.rem(z + nz - 1, nz), lax.rem(z + 1, nz)
    left, right = lax.rem(a + na - 1, na), lax.rem(a + 1, na)
    has_up = (z > 0).astype(F32)
    has_down = (z < nz - 1).astype(F32)

    barrier = pltpu.get_barrier_semaphore()
    zpeers = [lax.rem(z + k, nz) for k in range(1, nz)]
    apeers = [lax.rem(a + k, na) for k in range(1, na)]
    corners = [(up, left), (up, right), (down, left), (down, right)]
    greet = [(p, a) for p in zpeers] + [(z, p) for p in apeers] + corners
    for who in greet:
        pl.semaphore_signal(barrier, inc=1, device_id=who, device_id_type=MESH)

    loads = [pltpu.make_async_copy(s, d, insem.at[k]) for k, (s, d) in enumerate(
        [(ws, wv), (dc, dv), (on, ov), (ce, cv), (xh, xhv), (xl, xlv), (yh, yhv), (yl, ylv), (exl, exlv), (exr, exrv), (ey, eyv)])]
    for load in loads:
        load.start()

    sends = []

    def send(src, dst, sem_index, recv, who):
        copy = pltpu.make_async_remote_copy(src_ref=src, dst_ref=dst, send_sem=ssem.at[sem_index], recv_sem=recv,
                                            device_id=who, device_id_type=MESH)
        copy.start()
        sends.append(copy)
        return copy

    for load in loads[:2]:
        load.wait()
    SUR, FX, FY, U, V, FXU, FXV, FYV = range(8)
    ACROSS = (SUR, FX, U, V, FXU, FXV)
    ALONG = (SUR, FY, U, V, FXV, FYV)

    def first(i, sums):
        rows = pl.ds(pl.multiple_of(i * 16, 16), 16)
        inner = pl.ds(pl.multiple_of(i * 16 + FPAD, 16), 16)
        kind = dv[rows, :]
        still = jnp.full((16, COLS), cd[0], F32)
        for k in range(1, CLASSES):
            still = jnp.where(kind == k, cd[k], still)
        surface, px, py = wv[0, rows, :], wv[1, rows, :], wv[2, rows, :]
        depth = still + surface
        u, v = px / depth, py / depth
        fields = [surface, px, py, u, v, px * u, px * v, py * v]
        for k, f in enumerate(fields):
            fld[k, inner, :] = f
        dep[rows, :] = depth
        c = depth * depth * (1.0 / 3.0)
        cext[pl.ds(pl.multiple_of(i * 16 + HALO, 8), 16), 0:COLS] = c
        for k, f in enumerate(ALONG):
            high, low = split_bf16(lane_source(fields[f]))
            syh[k, rows, :] = high
            syl[k, rows, :] = low
        energy = surface * surface + px * px + py * py
        return sums[0] + c * energy, sums[1] + energy

    nil = jnp.zeros((16, COLS), F32)
    stat = lax.fori_loop(0, ROWS // 16, first, (nil, nil))

    def across_sources(ref, which):
        def body(i, _):
            rows = pl.ds(pl.multiple_of(i * 16, 16), 16)
            for k, f in enumerate(which):
                around = ref[f, pl.ds(pl.multiple_of(i * 16 + FPAD - 8, 8), 32), :]
                high, low = split_bf16(row_source(around, i * 16))
                sxh[k, rows, :] = high
                sxl[k, rows, :] = low
            return 0
        lax.fori_loop(0, ROWS // 16, body, 0)

    def solves(count):
        def body(k, _):
            dot = functools.partial(jnp.dot, preferred_element_type=F32)
            hx[k] = dot(xhv[...], sxh[k]) + (dot(xhv[...], sxl[k]) + dot(xlv[...], sxh[k]))
            hy[k] = dot(syh[k], yhv[...]) + (dot(syl[k], yhv[...]) + dot(syh[k], ylv[...]))
            return 0
        lax.fori_loop(0, count, body, 0)

    lane128 = iota((ROWS, 128), 1)

    def edges_out(ref, across, along, stage):
        for k, f in enumerate(across):
            for j in range(4):
                er[j, k:k + 1, :] = ref[f, FPAD + j:FPAD + j + 1, :]
                er[4 + j, k:k + 1, :] = ref[f, FPAD + ROWS - 1 - j:FPAD + ROWS - j, :]
            er[8, k:k + 1, :] = hx[k, 0:1, :]
            er[9, k:k + 1, :] = hx[k, ROWS - 1:ROWS, :]
        for k, f in enumerate(along):
            fl = ref[f, FPAD:FPAD + ROWS, 0:128]
            fr = ref[f, FPAD:FPAD + ROWS, COLS - 128:COLS]
            tile = jnp.where(lane128 < 32, fl, jnp.where(lane128 < 64, rolled(hy[k, :, 0:128], 32, 1), jnp.where(
                lane128 < 96, rolled(hy[k, :, COLS - 128:COLS], -32, 1), fr)))
            turned = tile.T
            for j in range(4):
                ec[j, k:k + 1, :] = turned[j:j + 1, :]
                ec[4 + j, k:k + 1, :] = turned[127 - j:128 - j, :]
            ec[8, k:k + 1, :] = turned[32:33, :]
            ec[9, k:k + 1, :] = turned[95:96, :]
        for e, msg in ((er, rowmsg), (ec, colmsg)):
            s0, s1 = edge_items([e[j] for j in range(4)])
            msg[stage, 0, 0] = e[0]
            msg[stage, 0, 1] = e[1]
            msg[stage, 0, 2] = e[8] + CORNER * s0 + NEXT * s1
            t0, t1 = edge_items([e[4 + j] for j in range(4)])
            msg[stage, 1, 0] = e[4]
            msg[stage, 1, 1] = e[5]
            msg[stage, 1, 2] = e[9] - CORNER * t0 - NEXT * t1

    def edges_send(stage):
        base = 4 * stage
        return [
            send(rowmsg.at[stage, 0], rowgot.at[stage, 1], base, rowsem.at[stage, 1], (up, a)),
            send(rowmsg.at[stage, 1], rowgot.at[stage, 0], base + 1, rowsem.at[stage, 0], (down, a)),
            send(colmsg.at[stage, 0], colgot.at[stage, 1], base + 2, colsem.at[stage, 1], (z, left)),
            send(colmsg.at[stage, 1], colgot.at[stage, 0], base + 3, colsem.at[stage, 0], (z, right)),
        ]

    def closing(e, got, keep_low, keep_high):
        f0, f1 = e[0], e[1]
        p1, p2, ph = got[0, 0] * keep_low, got[0, 1] * keep_low, got[0, 2]
        s0, s1 = edge_items([e[j] for j in range(4)])
        s0 = s0 - A2 * p1 - B4 * p2
        s1 = s1 - B4 * p1
        own = e[8] + CORNER * s0 + NEXT * s1
        theirs = ph + CORNER * (A2 * f0 + B4 * f1) + NEXT * (B4 * f0)
        gp = (theirs - LINK * own) * COUPLE * keep_low
        low, low_end = s0 - s1 * (1.0 / Q) - Q * gp, s1 * (1.0 / Q)
        l0, l1 = e[4], e[5]
        n1, n2, nh = got[1, 0] * keep_high, got[1, 1] * keep_high, got[1, 2]
        t0, t1 = edge_items([e[4 + j] for j in range(4)])
        t0 = A2 * n1 + B4 * n2 - t0
        t1 = B4 * n1 - t1
        own = e[9] + CORNER * t0 + NEXT * t1
        theirs = nh - CORNER * (A2 * l0 + B4 * l1) - NEXT * (B4 * l0)
        gn = (theirs - LINK * own) * COUPLE * keep_high
        return low, t0 - t1 * (1.0 / Q) - Q * gn, low_end, t1 * (1.0 / Q)

    def close_across(count, stage):
        low, high, low_end, high_end = closing(er, rowgot.at[stage], has_up, has_down)
        for k in range(count):
            hx[k, 0:1, :] = hx[k, 0:1, :] + low_end[k:k + 1, :]
            hx[k, ROWS - 1:ROWS, :] = hx[k, ROWS - 1:ROWS, :] + high_end[k:k + 1, :]
        return low, high

    def close_along(count, stage):
        terms = closing(ec, colgot.at[stage], 1.0, 1.0)
        block = jnp.concatenate(list(terms) + [jnp.zeros((96, 128), F32)], axis=0)
        turned = block.T
        for k in range(count):
            col = [jnp.broadcast_to(turned[:, 8 * j + k:8 * j + k + 1], (ROWS, 128)) for j in range(4)]
            hy[k, :, 0:128] = hy[k, :, 0:128] + col[0] * eyv[0:1, :] + jnp.where(lane128 == 0, col[2], 0.0)
            hy[k, :, COLS - 128:COLS] = (hy[k, :, COLS - 128:COLS] + col[1] * eyv[1:2, :]
                                         + jnp.where(lane128 == 127, col[3], 0.0))

    across_sources(fld, ACROSS)
    for load in loads[4:]:
        load.wait()
    solves(6)
    edges_out(fld, ACROSS, ALONG, 0)

    stat_c, stat_e = [t[0:8] + t[8:16] for t in stat]
    stat_c, stat_e = [sum(t[:, 128 * j:128 * (j + 1)] for j in range(4)) for t in (stat_c, stat_e)]
    sub8, lane8 = iota((8, 128), 0), iota((8, 128), 1)
    mixed = jnp.where(sub8 < 4, stat_c + rolled(stat_c, 4, 0), stat_e + rolled(stat_e, 4, 0))
    for s in (64, 32, 16, 8, 4, 2, 1):
        mixed = mixed + rolled(mixed, s, 1)
    mixed = mixed + jnp.where(sub8 % 4 < 2, rolled(mixed, -2, 0), rolled(mixed, 2, 0))
    mixed = mixed + jnp.where(sub8 % 2 < 1, rolled(mixed, -1, 0), rolled(mixed, 1, 0))
    stmsg[0] = mixed

    pl.semaphore_wait(barrier, len(greet))

    first_edges = edges_send(0)

    def spread_z(msg, slots, ss, rs):
        copies = []
        for k, p in enumerate(zpeers):
            copy = pltpu.make_async_remote_copy(src_ref=msg, dst_ref=slots.at[z], send_sem=ss.at[k], recv_sem=rs.at[z],
                                                device_id=(p, a), device_id_type=MESH)
            copy.start()
            copies.append(copy)
        slots[z] = msg[...]
        return copies

    def spread_a(msg, slots, ss, rs):
        copies = []
        for k, p in enumerate(apeers):
            copy = pltpu.make_async_remote_copy(src_ref=msg, dst_ref=slots.at[a], send_sem=ss.at[k], recv_sem=rs.at[a],
                                                device_id=(z, p), device_id_type=MESH)
            copy.start()
            copies.append(copy)
        slots[a] = msg[...]
        return copies

    def arrived(msg, slots, ss, rs, peers):
        for k, p in enumerate(peers):
            pltpu.make_async_remote_copy(src_ref=msg, dst_ref=slots.at[p], send_sem=ss.at[k], recv_sem=rs.at[p],
                                         device_id=(z, right), device_id_type=MESH).wait_recv()

    stz_copies = spread_z(stmsg.at[0], stz, stzs, stzr)

    top, bottom = pl.ds(0, HALO), pl.ds(EROWS - HALO, HALO)
    inner = pl.ds(HALO, ROWS)
    first_rows, last_rows = pl.ds(HALO, HALO), pl.ds(ROWS, HALO)
    low_cols, high_cols = pl.ds(0, 128), pl.ds(COLS - 128, 128)
    whole_cols = pl.ds(0, COLS)
    c_copies = [
        send(cext.at[first_rows, whole_cols], cext.at[bottom, whole_cols], 8, crowsem.at[1], (up, a)),
        send(cext.at[last_rows, whole_cols], cext.at[top, whole_cols], 9, crowsem.at[0], (down, a)),
        send(cext.at[inner, low_cols], cright.at[inner, :], 10, ccolsem.at[1], (z, left)),
        send(cext.at[inner, high_cols], cleft.at[inner, :], 11, ccolsem.at[0], (z, right)),
        send(cext.at[first_rows, low_cols], cright.at[bottom, :], 12, ccorsem.at[0], (up, left)),
        send(cext.at[first_rows, high_cols], cleft.at[bottom, :], 13, ccorsem.at[1], (up, right)),
        send(cext.at[last_rows, low_cols], cright.at[top, :], 14, ccorsem.at[2], (down, left)),
        send(cext.at[last_rows, high_cols], cleft.at[top, :], 15, ccorsem.at[3], (down, right)),
    ]

    for copy in first_edges:
        copy.wait_recv()
    xlow, xhigh = close_across(6, 0)
    close_along(6, 0)
    for load in loads[2:4]:
        load.wait()

    def wide(tile):
        return jnp.concatenate([tile] * 4, axis=1)

    er[0] = xlow
    er[1] = xhigh

    def second(i, _):
        rows = pl.ds(pl.multiple_of(i * 16, 16), 16)
        inner16 = pl.ds(pl.multiple_of(i * 16 + FPAD, 16), 16)
        wl, wr = wide(exlv[rows, :]), wide(exrv[rows, :])
        gx = [hx[k, rows, :] + (wl * er[0, k:k + 1, :] + wr * er[1, k:k + 1, :]) for k in range(6)]
        gy = [hy[k, rows, :] for k in range(6)]
        depth = dep[rows, :]
        rate = -(gx[1] + gy[1])
        active = (ov[rows, :] * (1 - cv[rows, :])).astype(F32)
        weight = BREAKING * active * depth * jnp.abs(rate) * depth
        sxx = 2.0 * weight * gx[2]
        sxy = weight * (gy[2] + gx[3])
        syy = 2.0 * weight * gy[3]
        ratev[rows, :] = rate
        stress[0, inner16, :] = sxx
        stress[1, inner16, :] = sxy
        stress[2, inner16, :] = syy
        part[0, rows, :] = -gx[4] - gy[4] - depth * gx[0]
        part[1, rows, :] = -gx[5] - gy[5] - depth * gy[0]
        for k, f in enumerate((sxy, syy)):
            high, low = split_bf16(lane_source(f))
            syh[k, rows, :] = high
            syl[k, rows, :] = low
        return 0

    lax.fori_loop(0, ROWS // 16, second, 0)
    rate_out = pltpu.make_async_copy(ratev, out.at[0], outsem.at[0])
    rate_out.start()
    across_sources(stress, (0, 1))
    solves(2)
    edges_out(stress, (0, 1), (1, 2), 1)
    second_edges = edges_send(1)

    arrived(stmsg.at[0], stz, stzs, stzr, zpeers)
    stmsg[1] = functools.reduce(lambda s, k: s + stz[k], range(1, nz), stz[0])
    sta_copies = spread_a(stmsg.at[1], sta, stas, star)

    for copy in second_edges:
        copy.wait_recv()
    xlow, xhigh = close_across(2, 1)
    close_along(2, 1)
    er[0] = xlow
    er[1] = xhigh

    def third(i, _):
        rows = pl.ds(pl.multiple_of(i * 16, 16), 16)
        ext = pl.ds(pl.multiple_of(i * 16 + HALO, 8), 16)
        wl, wr = wide(exlv[rows, :]), wide(exrv[rows, :])
        gx = [hx[k, rows, :] + (wl * er[0, k:k + 1, :] + wr * er[1, k:k + 1, :]) for k in range(2)]
        fx = part[0, rows, :] + gx[0] + hy[0, rows, :]
        fy = part[1, rows, :] + gx[1] + hy[1, rows, :]
        bx[ext, 0:COLS] = fx
        by[ext, 0:COLS] = fy
        lane = iota((16, 128), 1)
        fmsg[0, rows, :] = jnp.where(lane < 64, fx[:, 0:128], rolled(fy[:, 0:128], 64, 1))
        fmsg[1, rows, :] = jnp.where(lane < 64, rolled(fy[:, COLS - 128:], 64, 1), fx[:, COLS - 128:])
        return 0

    lax.fori_loop(0, ROWS // 16, third, 0)
    lo8, hi8 = pl.ds(0, HALO), pl.ds(ROWS - HALO, HALO)
    f_copies = [
        send(bx.at[first_rows, whole_cols], bx.at[bottom, whole_cols], 16, frowsem.at[0], (up, a)),
        send(bx.at[last_rows, whole_cols], bx.at[top, whole_cols], 17, frowsem.at[1], (down, a)),
        send(by.at[first_rows, whole_cols], by.at[bottom, whole_cols], 18, frowsem.at[2], (up, a)),
        send(by.at[last_rows, whole_cols], by.at[top, whole_cols], 19, frowsem.at[3], (down, a)),
        send(fmsg.at[0], fright.at[inner, :], 20, fcolsem.at[1], (z, left)),
        send(fmsg.at[1], fleft.at[inner, :], 21, fcolsem.at[0], (z, right)),
        send(fmsg.at[0, lo8, :], fright.at[bottom, :], 22, fcorsem.at[0], (up, left)),
        send(fmsg.at[1, lo8, :], fleft.at[bottom, :], 23, fcorsem.at[1], (up, right)),
        send(fmsg.at[0, hi8, :], fright.at[top, :], 24, fcorsem.at[2], (down, left)),
        send(fmsg.at[1, hi8, :], fleft.at[top, :], 25, fcorsem.at[3], (down, right)),
    ]

    arrived(stmsg.at[1], sta, stas, star, apeers)
    total = functools.reduce(lambda s, k: s + sta[k], range(1, na), sta[0])
    weight_c = jnp.broadcast_to(total[0:1, 0:1], (8, 128))
    weight_e = jnp.broadcast_to(total[4:5, 0:1], (8, 128))
    top_value = jnp.where(weight_e > 0.0, 10.0 * weight_c / weight_e, 100.0)
    half_top = 0.5 * top_value
    shrink = 1.0 / half_top
    for copy in c_copies:
        copy.wait_recv()

    def wide5(tile):
        return jnp.concatenate([tile] * 5, axis=1)

    sub = iota((8, ECOLS), 0)
    lanes = iota((8, 128), 1)
    shrink5 = wide5(shrink)

    def scaled_c(i, _):
        rows = pl.ds(pl.multiple_of(i * 8, 8), 8)
        side = jnp.where(lanes < 64, cright[rows, :], cleft[rows, :])
        c = jnp.concatenate([cext[rows, 0:COLS], side], axis=1) * shrink5
        c = c * jnp.where(i == 0, has_up, jnp.where(i == EROWS // 8 - 1, has_down, 1.0))
        cs[rows, :] = c
        crec[rows, :] = 1.0 / c
        return 0

    lax.fori_loop(0, EROWS // 8, scaled_c, 0)
    for copy in f_copies:
        copy.wait_recv()

    def sides(i, _):
        rows = pl.ds(pl.multiple_of(i * 8, 8), 8)
        from_right, from_left = fright[rows, :], fleft[rows, :]
        bx[rows, COLS:ECOLS] = jnp.where(lanes < 64, from_right, from_left)
        by[rows, COLS:ECOLS] = jnp.where(lanes < 64, rolled(from_right, 64, 1), rolled(from_left, 64, 1))
        return 0

    lax.fori_loop(0, EROWS // 8, sides, 0)
    bx[bottom, :] = bx[bottom, :] * has_down

    def tile_at(ref, i):
        return ref[pl.ds(pl.multiple_of(i * 8, 8), 8), :]

    def below_of(x, nxt):
        return jnp.where(sub == 7, rolled(nxt, -1, 0), rolled(x, -1, 0))

    def above_of(x, prv):
        return jnp.where(sub == 0, rolled(prv, 1, 0), rolled(x, 1, 0))

    TILES = EROWS // 8

    def start_tile(i):
        wx, wy = tile_at(bx, i), tile_at(by, i)
        nxt = tile_at(bx, jnp.minimum(i + 1, TILES - 1))
        div = (below_of(wx, nxt) - wx) + (rolled(wy, -1, 1) - wy)
        t = tile_at(cs, i) * div
        tau[0, pl.ds(pl.multiple_of(i * 8, 8), 8), :] = t
        return wx, wy, t

    def inside(t):
        return t[:, 0:COLS]

    def start_body(i, sums):
        wx, wy, t = start_tile(i)
        wx, wy, t = inside(wx), inside(wy), inside(t)
        return sums[0] + (wx * wx + wy * wy), sums[1] + t * (t * inside(tile_at(crec, i)))

    nil8 = jnp.zeros((8, COLS), F32)
    start_tile(0)
    start_tile(TILES - 1)
    norm, dot0 = lax.fori_loop(1, TILES - 1, start_body, (nil8, nil8))
    dots = [dot0]

    def step_tile(k, i):
        rows = pl.ds(pl.multiple_of(i * 8, 8), 8)
        x = tile_at(tau.at[k], i)
        prv = tile_at(tau.at[k], jnp.maximum(i - 1, 0))
        nxt = tile_at(tau.at[k], jnp.minimum(i + 1, TILES - 1))
        around = (above_of(x, prv) + below_of(x, nxt)) + (rolled(x, -1, 1) + rolled(x, 1, 1))
        last = (i == TILES - 2) & (z == nz - 1)
        diag = jnp.where((sub == 7) & last, 3.0, 4.0)
        t = tile_at(cs, i) * (diag * x - around) - x
        if k > 0:
            t = 2.0 * t - tile_at(tau.at[k - 1], i)
        tau[k + 1, rows, :] = t
        return x, t

    for k in range(ITERS - 1):
        def step_body(i, sums, k=k):
            x, t = step_tile(k, i)
            x, t = inside(x), inside(t)
            q = t * inside(tile_at(crec, i))
            return sums[0] + x * q, sums[1] + t * q

        if k < ITERS - 2:
            step_tile(k, 0)
            step_tile(k, TILES - 1)
        dots += list(lax.fori_loop(1, TILES - 1, step_body, (nil8, nil8)))
    dots.append(norm)

    def fold(t):
        s0 = dd_add(two_sum(t[:, 0:128], t[:, 128:256]), two_sum(t[:, 256:384], t[:, 384:512]))
        return s0

    level = [fold(t) for t in dots]
    for width, span in ((8, 4), (4, 2), (2, 1)):
        mask = sub8 % (2 * span) < span

        def merge(p, q, mask=mask, span=span):
            def parts(g, h):
                w = jnp.where(mask, h, g)
                return jnp.where(mask, g, h), jnp.where(mask, rolled(w, -span, 0), rolled(w, span, 0))
            xh_, yh_ = parts(p[0], q[0])
            xl_, yl_ = parts(p[1], q[1])
            return dd_add((xh_, xl_), (yh_, yl_))

        level = [merge(level[i], level[i + width]) for i in range(width)]
    for s in (64, 32, 16, 8, 4, 2, 1):
        level = [dd_add(p, (rolled(p[0], s, 1), rolled(p[1], s, 1))) for p in level]
    even, odd = level

    dtmsg[0] = jnp.where(lane8 < 32, even[0], jnp.where(lane8 < 64, odd[0], jnp.where(lane8 < 96, even[1], odd[1])))
    dtz_copies = spread_z(dtmsg.at[0], dtz, dtzs, dtzr)
    arrived(dtmsg.at[0], dtz, dtzs, dtzr, zpeers)

    def gathered(slots, count):
        level = [(slots[k], rolled(slots[k], 64, 1)) for k in range(count)]
        while len(level) > 1:
            level = [dd_add(level[2 * i], level[2 * i + 1]) for i in range(len(level) // 2)]
        return level[0]

    sums = gathered(dtz, nz)
    dtmsg[1] = jnp.where(lane8 < 64, sums[0], rolled(sums[1], 64, 1))
    dta_copies = spread_a(dtmsg.at[1], dta, dtas, dtar)
    arrived(dtmsg.at[1], dta, dtas, dtar, apeers)
    sums = gathered(dta, na)

    def pick(value, lane):
        return jnp.broadcast_to(value[:, lane:lane + 1], (8, 128))

    def row_of(value, r):
        return tuple(jnp.broadcast_to(part_[r:r + 1, :], (8, 128)) for part_ in value)

    even = pick(sums[0], 0), pick(sums[1], 0)
    odd = pick(sums[0], 32), pick(sums[1], 32)
    square = row_of(odd, 7)
    even = dd_add((2.0 * even[0], 2.0 * even[1]), dd_neg(row_of(even, 0)))
    odd = dd_add((2.0 * odd[0], 2.0 * odd[1]), dd_neg(row_of(odd, 0)))

    MOM, SEC, GRAM, MIX = range(4)
    nsc[...] = jnp.zeros(nsc.shape, F32)
    for part_ in range(2):
        for j in range(15):
            value = (even, odd)[j % 2][part_][j // 2:j // 2 + 1, :]
            nsc[MOM, part_, 8 + j:9 + j, :] = value
            if j == 1:
                nsc[MOM, part_, 7:8, :] = value

    def entries(which, start, count=8):
        return nsc[which, 0, start:start + count, :], nsc[which, 1, start:start + count, :]

    def widened(which, start):
        return dd_add(entries(which, start), dd_half(dd_add(entries(which, start + 1), entries(which, start - 1))))

    for start in (8, 16):
        value = widened(MOM, start)
        nsc[SEC, 0, start:start + 8, :], nsc[SEC, 1, start:start + 8, :] = value
        mix = dd_add(entries(MOM, start), dd_scale(value, half_top))
        nsc[MIX, 0, start:start + 8, :], nsc[MIX, 1, start:start + 8, :] = mix
    for part_ in range(2):
        nsc[SEC, part_, 7:8, :] = nsc[SEC, part_, 9:10, :]
    for start in (8, 16):
        value = dd_add(entries(SEC, start), dd_scale(widened(SEC, start), half_top))
        nsc[GRAM, 0, start:start + 8, :], nsc[GRAM, 1, start:start + 8, :] = value
    for part_ in range(2):
        for j in range(1, 8):
            nsc[GRAM, part_, 8 - j:9 - j, :] = nsc[GRAM, part_, 8 + j:9 + j, :]

    def with_first(value, head):
        return tuple(jnp.where(sub8 == 0, h, v) for v, h in zip(value, head))

    moment0 = row_of(entries(MOM, 8), 0)
    matrix = [with_first(entries(MIX, 7), dd_add(square, dd_scale(moment0, half_top)))]
    for l in range(ITERS - 1):
        column = dd_half(dd_add(entries(GRAM, 7 + l), entries(GRAM, 7 - l)))
        matrix.append(with_first(column, row_of(entries(MIX, 8 + l), 0)))
    right_side = with_first(entries(MOM, 7), square)
    diagonal = jnp.zeros((8, 128), F32)
    first_diagonal = [row_of(matrix[k], k)[0] for k in range(ITERS)]
    for k in range(ITERS):
        pivot = row_of(matrix[k], k)
        usable = pivot[0] > 1e-11 * first_diagonal[k]
        safe = jnp.where(usable, pivot[0], 1.0), jnp.where(usable, pivot[1], 0.0)
        factor = dd_div(matrix[k], safe)
        skip = (sub8 == k) | jnp.logical_not(usable)
        factor = tuple(jnp.where(skip, 0.0, f) for f in factor)
        diagonal = jnp.where((sub8 == k) & usable, pivot[0], diagonal)
        for l in range(k + 1, ITERS):
            matrix[l] = dd_add(matrix[l], dd_neg(dd_mul(factor, row_of(matrix[l], k))))
        right_side = dd_add(right_side, dd_neg(dd_mul(factor, row_of(right_side, k))))
    answer = jnp.where(diagonal > 0.0, right_side[0] / jnp.where(diagonal > 0.0, diagonal, 1.0), 0.0)
    nsc[MOM, 0, 0:8, :] = answer

    def finish(i, _):
        rows = pl.ds(pl.multiple_of(i * 8, 8), 8)
        weights = [wide5(jnp.broadcast_to(nsc[MOM, 0, k:k + 1, :], (8, 128))) for k in range(ITERS)]

        def combined(j):
            return functools.reduce(lambda s, t: s + t, [weights[l + 1] * tile_at(tau.at[l], j) for l in range(ITERS - 1)])

        here, prv = combined(i + 1), combined(i)
        inner_rows = pl.ds(pl.multiple_of(i * 8 + HALO, 8), 8)
        gain = weights[0][:, 0:COLS]
        solv[0, rows, :] = gain * bx[inner_rows, 0:COLS] - inside(here - above_of(here, prv))
        solv[1, rows, :] = gain * by[inner_rows, 0:COLS] - inside(here - rolled(here, 1, 1))
        return 0

    lax.fori_loop(0, ROWS // 8, finish, 0)
    solved_out = pltpu.make_async_copy(solv, out.at[pl.ds(1, 2)], outsem.at[1])
    solved_out.start()
    for copy in sends + stz_copies + sta_copies + dtz_copies + dta_copies:
        copy.wait_send()
    rate_out.wait()
    solved_out.wait()


def per_device(nz, na, wave_state, depth_class, onset_flag, cessation, class_depth):
    across, along = tridiagonal_inverse(ROWS), tridiagonal_inverse(COLS)
    xh, xl = halves(across)
    yh, yl = halves(along)
    exl = np.repeat(across[:, :1], 128, axis=1).astype(np.float32)
    exr = np.repeat(across[:, -1:], 128, axis=1).astype(np.float32)
    ey = np.zeros((8, 128), np.float32)
    ey[0] = along[0, :128]
    ey[1] = along[-1, -128:]
    consts = [jnp.asarray(t) for t in (xh, xl, yh, yl, exl, exr, ey)]
    dma = pltpu.SemaphoreType.DMA

    def vm(*shape, dtype=F32):
        return pltpu.VMEM(shape, dtype)

    scratch = [
        vm(3, ROWS, COLS), vm(ROWS, COLS, dtype=jnp.int32), vm(ROWS, COLS, dtype=jnp.int32), vm(ROWS, COLS, dtype=jnp.int32),
        vm(ROWS, ROWS, dtype=BF16), vm(ROWS, ROWS, dtype=BF16), vm(COLS, COLS, dtype=BF16), vm(COLS, COLS, dtype=BF16),
        vm(ROWS, 128), vm(ROWS, 128), vm(8, 128),
        vm(8, ROWS + 2 * FPAD, COLS), vm(ROWS, COLS),
        vm(6, ROWS, COLS, dtype=BF16), vm(6, ROWS, COLS, dtype=BF16), vm(6, ROWS, COLS, dtype=BF16), vm(6, ROWS, COLS, dtype=BF16),
        vm(6, ROWS, COLS), vm(6, ROWS, COLS), vm(10, 8, COLS), vm(10, 8, 128),
        vm(3, ROWS + 2 * FPAD, COLS), vm(2, ROWS, COLS), vm(ROWS, COLS), vm(2, ROWS, COLS),
        vm(2, 2, 3, 8, COLS), vm(2, 2, 3, 8, COLS), vm(2, 2, 3, 8, 128), vm(2, 2, 3, 8, 128),
        vm(EROWS, ECOLS), vm(EROWS, ECOLS), vm(EROWS, ECOLS), vm(EROWS, ECOLS),
        vm(EROWS, 128), vm(EROWS, 128), vm(EROWS, 128), vm(EROWS, 128), vm(2, ROWS, 128),
        vm(ITERS, EROWS, ECOLS), vm(EROWS, ECOLS),
        vm(2, 8, 128), vm(nz, 8, 128), vm(na, 8, 128), vm(2, 8, 128), vm(nz, 8, 128), vm(na, 8, 128), vm(4, 2, 32, 128),
        dma((11,)), dma((2,)), dma((26,)), dma((2, 2)), dma((2, 2)), dma((2,)), dma((2,)), dma((4,)), dma((4,)), dma((2,)), dma((4,)),
        dma((nz - 1,)), dma((na - 1,)), dma((nz - 1,)), dma((na - 1,)), dma((nz,)), dma((na,)), dma((nz,)), dma((na,)),
    ]
    anywhere = pl.BlockSpec(memory_space=pl.ANY)
    return pl.pallas_call(
        functools.partial(kernel, nz, na),
        out_shape=jax.ShapeDtypeStruct((3, ROWS, COLS), F32),
        in_specs=[anywhere] * 4 + [pl.BlockSpec(memory_space=pltpu.SMEM)] + [anywhere] * 7,
        out_specs=anywhere,
        scratch_shapes=scratch,
        compiler_params=pltpu.CompilerParams(collective_id=0, has_side_effects=True, vmem_limit_bytes=50 * 2**20),
    )(wave_state, depth_class, onset_flag, cessation, class_depth, *consts)


def solution(mesh):
    sizes = dict(mesh.shape)
    in_specs = (P(None, "xs", "al"), P("xs", "al"), P("xs", "al"), P("xs", "al"), P())
    return jax.shard_map(
        functools.partial(per_device, sizes["xs"], sizes["al"]),
        mesh=mesh, in_specs=in_specs, out_specs=P(None, "xs", "al"), check_vma=False,
    )
```

```python
import functools

import jax
import jax.numpy as jnp
import numpy as np
from jax import lax
from jax.experimental import pallas as pl
from jax.experimental.pallas import tpu as pltpu
from jax.sharding import PartitionSpec as P

MESH = pl.DeviceIdType.MESH
CLASSES = 8
ITERS = 8
ROWS, COLS = 128, 512
HALO = 8
EROWS, ECOLS = ROWS + 2 * HALO, COLS + 128
FPAD = 16
Q = 1.0 / 3.0
A2 = 0.5 * 14.0 / 9.0
B4 = 0.25 / 9.0
BREAKING = 0.05
VMEM_BYTES = 63 * 2**20
F32, BF16 = jnp.float32, jnp.bfloat16


def tridiagonal_inverse(length):
    band = np.eye(length) + Q * (np.eye(length, k=1) + np.eye(length, k=-1))
    return np.linalg.inv(band)


CORNER = float(tridiagonal_inverse(ROWS)[0, 0])
NEXT = (1.0 - CORNER) / Q
LINK = Q * CORNER
COUPLE = 1.0 / (1.0 - LINK * LINK)


def halves(matrix):
    matrix = matrix.astype(np.float32)
    high = matrix.astype(jnp.bfloat16)
    low = (matrix - high.astype(np.float32)).astype(jnp.bfloat16)
    return high, low


def split_bf16(value):
    high = value.astype(BF16)
    return high, (value - high.astype(F32)).astype(BF16)


def two_sum(a, b):
    s = a + b
    t = s - a
    return s, (a - (s - t)) + (b - t)


def quick_sum(a, b):
    s = a + b
    return s, b - (s - a)


def cut(a):
    t = 4097.0 * a
    high = t - (t - a)
    return high, a - high


def two_prod(a, b):
    p = a * b
    ah, al = cut(a)
    bh, bl = cut(b)
    return p, ((ah * bh - p) + ah * bl + al * bh) + al * bl


def dd_add(a, b):
    s, e = two_sum(a[0], b[0])
    t, f = two_sum(a[1], b[1])
    s, e = quick_sum(s, e + t)
    return quick_sum(s, e + f)


def dd_neg(a):
    return -a[0], -a[1]


def dd_mul(a, b):
    p, e = two_prod(a[0], b[0])
    return quick_sum(p, e + (a[0] * b[1] + a[1] * b[0]))


def dd_scale(a, b):
    p, e = two_prod(a[0], b)
    return quick_sum(p, e + a[1] * b)


def dd_half(a):
    return 0.5 * a[0], 0.5 * a[1]


def dd_div(a, b):
    first = a[0] / b[0]
    rest = dd_add(a, dd_neg(dd_scale(b, first)))
    return quick_sum(first, rest[0] / b[0])


def rolled(value, shift, axis):
    size = value.shape[axis]
    return pltpu.roll(value, shift % size, axis)


def iota(shape, axis):
    return lax.broadcasted_iota(jnp.int32, shape, axis)


def lane_source(field):
    d = rolled(field, -1, 1) - rolled(field, 1, 1)
    s = A2 * d + B4 * (rolled(d, -1, 1) + rolled(d, 1, 1))
    lane = iota(field.shape, 1)
    return jnp.where((lane >= 2) & (lane < COLS - 2), s, 0.0)


def row_source(around, start):
    d = rolled(around, -1, 0) - rolled(around, 1, 0)
    s = (A2 * d + B4 * (rolled(d, -1, 0) + rolled(d, 1, 0)))[8:24]
    row = iota(s.shape, 0) + start
    return jnp.where((row >= 2) & (row < ROWS - 2), s, 0.0)


def edge_items(f):
    return A2 * f[1] + B4 * f[2], A2 * (f[2] - f[0]) + B4 * f[3]


def kernel(nz, na, ws, dc, on, ce, cd, xh, xl, yh, yl, exl, exr, ey, out,
           wv, dv, ov, cv, xhv, xlv, yhv, ylv, exlv, exrv, eyv,
           fld, dep, sxh, sxl, syh, syl, hx, hy, er, ec, stress, part, ratev, solv,
           rowmsg, rowgot, colmsg, colgot, bx, by, cext, cs, cright, cleft, fright, fleft, fmsg, tau, crec, acc,
           stmsg, stz, sta, dtmsg, dtz, dta, nsc,
           insem, outsem, ssem, rowsem, colsem, crowsem, ccolsem, ccorsem, frowsem, fcolsem, fcorsem,
           stzs, stas, dtzs, dtas, stzr, star, dtzr, dtar):
    z, a = lax.axis_index("xs"), lax.axis_index("al")
    up, down = lax.rem(z + nz - 1, nz), lax.rem(z + 1, nz)
    left, right = lax.rem(a + na - 1, na), lax.rem(a + 1, na)
    has_up = (z > 0).astype(F32)
    has_down = (z < nz - 1).astype(F32)

    barrier = pltpu.get_barrier_semaphore()
    zpeers = [lax.rem(z + k, nz) for k in range(1, nz)]
    apeers = [lax.rem(a + k, na) for k in range(1, na)]
    corners = [(up, left), (up, right), (down, left), (down, right)]
    greet = [(p, a) for p in zpeers] + [(z, p) for p in apeers] + corners
    for who in greet:
        pl.semaphore_signal(barrier, inc=1, device_id=who, device_id_type=MESH)

    loads = [pltpu.make_async_copy(s, d, insem.at[k]) for k, (s, d) in enumerate(
        [(ws, wv), (dc, dv), (on, ov), (ce, cv), (xh, xhv), (xl, xlv), (yh, yhv), (yl, ylv), (exl, exlv), (exr, exrv), (ey, eyv)])]
    for load in loads:
        load.start()

    sends = []

    def send(src, dst, sem_index, recv, who):
        copy = pltpu.make_async_remote_copy(src_ref=src, dst_ref=dst, send_sem=ssem.at[sem_index], recv_sem=recv,
                                            device_id=who, device_id_type=MESH)
        copy.start()
        sends.append(copy)
        return copy

    for load in loads[:2]:
        load.wait()
    SUR, FX, FY, U, V, FXU, FXV, FYV = range(8)
    ACROSS = (SUR, FX, U, V, FXU, FXV)
    ALONG = (SUR, FY, U, V, FXV, FYV)

    def first(i, sums):
        rows = pl.ds(pl.multiple_of(i * 16, 16), 16)
        inner = pl.ds(pl.multiple_of(i * 16 + FPAD, 16), 16)
        kind = dv[rows, :]
        still = jnp.full((16, COLS), cd[0], F32)
        for k in range(1, CLASSES):
            still = jnp.where(kind == k, cd[k], still)
        surface, px, py = wv[0, rows, :], wv[1, rows, :], wv[2, rows, :]
        depth = still + surface
        u, v = px / depth, py / depth
        fields = [surface, px, py, u, v, px * u, px * v, py * v]
        for k, f in enumerate(fields):
            fld[k, inner, :] = f
        dep[rows, :] = depth
        c = depth * depth * (1.0 / 3.0)
        cext[pl.ds(pl.multiple_of(i * 16 + HALO, 8), 16), 0:COLS] = c
        for k, f in enumerate(ALONG):
            high, low = split_bf16(lane_source(fields[f]))
            syh[k, rows, :] = high
            syl[k, rows, :] = low
        energy = surface * surface + px * px + py * py
        return sums[0] + c * energy, sums[1] + energy

    nil = jnp.zeros((16, COLS), F32)
    stat = lax.fori_loop(0, ROWS // 16, first, (nil, nil))

    def across_sources(ref, which):
        def body(i, _):
            rows = pl.ds(pl.multiple_of(i * 16, 16), 16)
            for k, f in enumerate(which):
                around = ref[f, pl.ds(pl.multiple_of(i * 16 + FPAD - 8, 8), 32), :]
                high, low = split_bf16(row_source(around, i * 16))
                sxh[k, rows, :] = high
                sxl[k, rows, :] = low
            return 0
        lax.fori_loop(0, ROWS // 16, body, 0)

    def solves(count):
        def body(k, _):
            dot = functools.partial(jnp.dot, preferred_element_type=F32)
            hx[k] = dot(xhv[...], sxh[k]) + (dot(xhv[...], sxl[k]) + dot(xlv[...], sxh[k]))
            hy[k] = dot(syh[k], yhv[...]) + (dot(syl[k], yhv[...]) + dot(syh[k], ylv[...]))
            return 0
        lax.fori_loop(0, count, body, 0)

    lane128 = iota((ROWS, 128), 1)

    def edges_out(ref, across, along, stage):
        for k, f in enumerate(across):
            for j in range(4):
                er[j, k:k + 1, :] = ref[f, FPAD + j:FPAD + j + 1, :]
                er[4 + j, k:k + 1, :] = ref[f, FPAD + ROWS - 1 - j:FPAD + ROWS - j, :]
            er[8, k:k + 1, :] = hx[k, 0:1, :]
            er[9, k:k + 1, :] = hx[k, ROWS - 1:ROWS, :]
        for k, f in enumerate(along):
            fl = ref[f, FPAD:FPAD + ROWS, 0:128]
            fr = ref[f, FPAD:FPAD + ROWS, COLS - 128:COLS]
            tile = jnp.where(lane128 < 32, fl, jnp.where(lane128 < 64, rolled(hy[k, :, 0:128], 32, 1), jnp.where(
                lane128 < 96, rolled(hy[k, :, COLS - 128:COLS], -32, 1), fr)))
            turned = tile.T
            for j in range(4):
                ec[j, k:k + 1, :] = turned[j:j + 1, :]
                ec[4 + j, k:k + 1, :] = turned[127 - j:128 - j, :]
            ec[8, k:k + 1, :] = turned[32:33, :]
            ec[9, k:k + 1, :] = turned[95:96, :]
        for e, msg in ((er, rowmsg), (ec, colmsg)):
            s0, s1 = edge_items([e[j] for j in range(4)])
            msg[stage, 0, 0] = e[0]
            msg[stage, 0, 1] = e[1]
            msg[stage, 0, 2] = e[8] + CORNER * s0 + NEXT * s1
            t0, t1 = edge_items([e[4 + j] for j in range(4)])
            msg[stage, 1, 0] = e[4]
            msg[stage, 1, 1] = e[5]
            msg[stage, 1, 2] = e[9] - CORNER * t0 - NEXT * t1

    def edges_send(stage):
        base = 4 * stage
        return [
            send(rowmsg.at[stage, 0], rowgot.at[stage, 1], base, rowsem.at[stage, 1], (up, a)),
            send(rowmsg.at[stage, 1], rowgot.at[stage, 0], base + 1, rowsem.at[stage, 0], (down, a)),
            send(colmsg.at[stage, 0], colgot.at[stage, 1], base + 2, colsem.at[stage, 1], (z, left)),
            send(colmsg.at[stage, 1], colgot.at[stage, 0], base + 3, colsem.at[stage, 0], (z, right)),
        ]

    def closing(e, got, keep_low, keep_high):
        f0, f1 = e[0], e[1]
        p1, p2, ph = got[0, 0] * keep_low, got[0, 1] * keep_low, got[0, 2]
        s0, s1 = edge_items([e[j] for j in range(4)])
        s0 = s0 - A2 * p1 - B4 * p2
        s1 = s1 - B4 * p1
        own = e[8] + CORNER * s0 + NEXT * s1
        theirs = ph + CORNER * (A2 * f0 + B4 * f1) + NEXT * (B4 * f0)
        gp = (theirs - LINK * own) * COUPLE * keep_low
        low, low_end = s0 - s1 * (1.0 / Q) - Q * gp, s1 * (1.0 / Q)
        l0, l1 = e[4], e[5]
        n1, n2, nh = got[1, 0] * keep_high, got[1, 1] * keep_high, got[1, 2]
        t0, t1 = edge_items([e[4 + j] for j in range(4)])
        t0 = A2 * n1 + B4 * n2 - t0
        t1 = B4 * n1 - t1
        own = e[9] + CORNER * t0 + NEXT * t1
        theirs = nh - CORNER * (A2 * l0 + B4 * l1) - NEXT * (B4 * l0)
        gn = (theirs - LINK * own) * COUPLE * keep_high
        return low, t0 - t1 * (1.0 / Q) - Q * gn, low_end, t1 * (1.0 / Q)

    def close_across(count, stage):
        low, high, low_end, high_end = closing(er, rowgot.at[stage], has_up, has_down)
        for k in range(count):
            hx[k, 0:1, :] = hx[k, 0:1, :] + low_end[k:k + 1, :]
            hx[k, ROWS - 1:ROWS, :] = hx[k, ROWS - 1:ROWS, :] + high_end[k:k + 1, :]
        return low, high

    def close_along(count, stage):
        terms = closing(ec, colgot.at[stage], 1.0, 1.0)
        block = jnp.concatenate(list(terms) + [jnp.zeros((96, 128), F32)], axis=0)
        turned = block.T
        for k in range(count):
            col = [jnp.broadcast_to(turned[:, 8 * j + k:8 * j + k + 1], (ROWS, 128)) for j in range(4)]
            hy[k, :, 0:128] = hy[k, :, 0:128] + col[0] * eyv[0:1, :] + jnp.where(lane128 == 0, col[2], 0.0)
            hy[k, :, COLS - 128:COLS] = (hy[k, :, COLS - 128:COLS] + col[1] * eyv[1:2, :]
                                         + jnp.where(lane128 == 127, col[3], 0.0))

    across_sources(fld, ACROSS)
    for load in loads[4:]:
        load.wait()
    solves(6)
    edges_out(fld, ACROSS, ALONG, 0)

    stat_c, stat_e = [t[0:8] + t[8:16] for t in stat]
    stat_c, stat_e = [sum(t[:, 128 * j:128 * (j + 1)] for j in range(4)) for t in (stat_c, stat_e)]
    sub8, lane8 = iota((8, 128), 0), iota((8, 128), 1)
    mixed = jnp.where(sub8 < 4, stat_c + rolled(stat_c, 4, 0), stat_e + rolled(stat_e, 4, 0))
    for s in (64, 32, 16, 8, 4, 2, 1):
        mixed = mixed + rolled(mixed, s, 1)
    mixed = mixed + jnp.where(sub8 % 4 < 2, rolled(mixed, -2, 0), rolled(mixed, 2, 0))
    mixed = mixed + jnp.where(sub8 % 2 < 1, rolled(mixed, -1, 0), rolled(mixed, 1, 0))
    stmsg[0] = mixed

    pl.semaphore_wait(barrier, len(greet))

    first_edges = edges_send(0)

    def spread_z(msg, slots, ss, rs):
        copies = []
        for k, p in enumerate(zpeers):
            copy = pltpu.make_async_remote_copy(src_ref=msg, dst_ref=slots.at[z], send_sem=ss.at[k], recv_sem=rs.at[z],
                                                device_id=(p, a), device_id_type=MESH)
            copy.start()
            copies.append(copy)
        slots[z] = msg[...]
        return copies

    def spread_a(msg, slots, ss, rs):
        copies = []
        for k, p in enumerate(apeers):
            copy = pltpu.make_async_remote_copy(src_ref=msg, dst_ref=slots.at[a], send_sem=ss.at[k], recv_sem=rs.at[a],
                                                device_id=(z, p), device_id_type=MESH)
            copy.start()
            copies.append(copy)
        slots[a] = msg[...]
        return copies

    def arrived(msg, slots, ss, rs, peers):
        for k, p in enumerate(peers):
            pltpu.make_async_remote_copy(src_ref=msg, dst_ref=slots.at[p], send_sem=ss.at[k], recv_sem=rs.at[p],
                                         device_id=(z, right), device_id_type=MESH).wait_recv()

    stz_copies = spread_z(stmsg.at[0], stz, stzs, stzr)

    top, bottom = pl.ds(0, HALO), pl.ds(EROWS - HALO, HALO)
    inner = pl.ds(HALO, ROWS)
    first_rows, last_rows = pl.ds(HALO, HALO), pl.ds(ROWS, HALO)
    low_cols, high_cols = pl.ds(0, 128), pl.ds(COLS - 128, 128)
    whole_cols = pl.ds(0, COLS)
    c_copies = [
        send(cext.at[first_rows, whole_cols], cext.at[bottom, whole_cols], 8, crowsem.at[1], (up, a)),
        send(cext.at[last_rows, whole_cols], cext.at[top, whole_cols], 9, crowsem.at[0], (down, a)),
        send(cext.at[inner, low_cols], cright.at[inner, :], 10, ccolsem.at[1], (z, left)),
        send(cext.at[inner, high_cols], cleft.at[inner, :], 11, ccolsem.at[0], (z, right)),
        send(cext.at[first_rows, low_cols], cright.at[bottom, :], 12, ccorsem.at[0], (up, left)),
        send(cext.at[first_rows, high_cols], cleft.at[bottom, :], 13, ccorsem.at[1], (up, right)),
        send(cext.at[last_rows, low_cols], cright.at[top, :], 14, ccorsem.at[2], (down, left)),
        send(cext.at[last_rows, high_cols], cleft.at[top, :], 15, ccorsem.at[3], (down, right)),
    ]

    for copy in first_edges:
        copy.wait_recv()
    xlow, xhigh = close_across(6, 0)
    close_along(6, 0)
    for load in loads[2:4]:
        load.wait()

    def wide(tile):
        return jnp.concatenate([tile] * 4, axis=1)

    er[0] = xlow
    er[1] = xhigh

    def second(i, _):
        rows = pl.ds(pl.multiple_of(i * 16, 16), 16)
        inner16 = pl.ds(pl.multiple_of(i * 16 + FPAD, 16), 16)
        wl, wr = wide(exlv[rows, :]), wide(exrv[rows, :])
        gx = [hx[k, rows, :] + (wl * er[0, k:k + 1, :] + wr * er[1, k:k + 1, :]) for k in range(6)]
        gy = [hy[k, rows, :] for k in range(6)]
        depth = dep[rows, :]
        rate = -(gx[1] + gy[1])
        active = (ov[rows, :] * (1 - cv[rows, :])).astype(F32)
        weight = BREAKING * active * depth * jnp.abs(rate) * depth
        sxx = 2.0 * weight * gx[2]
        sxy = weight * (gy[2] + gx[3])
        syy = 2.0 * weight * gy[3]
        ratev[rows, :] = rate
        stress[0, inner16, :] = sxx
        stress[1, inner16, :] = sxy
        stress[2, inner16, :] = syy
        part[0, rows, :] = -gx[4] - gy[4] - depth * gx[0]
        part[1, rows, :] = -gx[5] - gy[5] - depth * gy[0]
        for k, f in enumerate((sxy, syy)):
            high, low = split_bf16(lane_source(f))
            syh[k, rows, :] = high
            syl[k, rows, :] = low
        return 0

    lax.fori_loop(0, ROWS // 16, second, 0)
    rate_out = pltpu.make_async_copy(ratev, out.at[0], outsem.at[0])
    rate_out.start()
    across_sources(stress, (0, 1))
    solves(2)
    edges_out(stress, (0, 1), (1, 2), 1)
    second_edges = edges_send(1)

    arrived(stmsg.at[0], stz, stzs, stzr, zpeers)
    stmsg[1] = functools.reduce(lambda s, k: s + stz[k], range(1, nz), stz[0])
    sta_copies = spread_a(stmsg.at[1], sta, stas, star)

    for copy in second_edges:
        copy.wait_recv()
    xlow, xhigh = close_across(2, 1)
    close_along(2, 1)
    er[0] = xlow
    er[1] = xhigh

    def third(i, _):
        rows = pl.ds(pl.multiple_of(i * 16, 16), 16)
        ext = pl.ds(pl.multiple_of(i * 16 + HALO, 8), 16)
        wl, wr = wide(exlv[rows, :]), wide(exrv[rows, :])
        gx = [hx[k, rows, :] + (wl * er[0, k:k + 1, :] + wr * er[1, k:k + 1, :]) for k in range(2)]
        fx = part[0, rows, :] + gx[0] + hy[0, rows, :]
        fy = part[1, rows, :] + gx[1] + hy[1, rows, :]
        bx[ext, 0:COLS] = fx
        by[ext, 0:COLS] = fy
        lane = iota((16, 128), 1)
        fmsg[0, rows, :] = jnp.where(lane < 64, fx[:, 0:128], rolled(fy[:, 0:128], 64, 1))
        fmsg[1, rows, :] = jnp.where(lane < 64, rolled(fy[:, COLS - 128:], 64, 1), fx[:, COLS - 128:])
        return 0

    lax.fori_loop(0, ROWS // 16, third, 0)
    lo8, hi8 = pl.ds(0, HALO), pl.ds(ROWS - HALO, HALO)
    f_copies = [
        send(bx.at[first_rows, whole_cols], bx.at[bottom, whole_cols], 16, frowsem.at[0], (up, a)),
        send(bx.at[last_rows, whole_cols], bx.at[top, whole_cols], 17, frowsem.at[1], (down, a)),
        send(by.at[first_rows, whole_cols], by.at[bottom, whole_cols], 18, frowsem.at[2], (up, a)),
        send(by.at[last_rows, whole_cols], by.at[top, whole_cols], 19, frowsem.at[3], (down, a)),
        send(fmsg.at[0], fright.at[inner, :], 20, fcolsem.at[1], (z, left)),
        send(fmsg.at[1], fleft.at[inner, :], 21, fcolsem.at[0], (z, right)),
        send(fmsg.at[0, lo8, :], fright.at[bottom, :], 22, fcorsem.at[0], (up, left)),
        send(fmsg.at[1, lo8, :], fleft.at[bottom, :], 23, fcorsem.at[1], (up, right)),
        send(fmsg.at[0, hi8, :], fright.at[top, :], 24, fcorsem.at[2], (down, left)),
        send(fmsg.at[1, hi8, :], fleft.at[top, :], 25, fcorsem.at[3], (down, right)),
    ]

    arrived(stmsg.at[1], sta, stas, star, apeers)
    total = functools.reduce(lambda s, k: s + sta[k], range(1, na), sta[0])
    weight_c = jnp.broadcast_to(total[0:1, 0:1], (8, 128))
    weight_e = jnp.broadcast_to(total[4:5, 0:1], (8, 128))
    top_value = jnp.where(weight_e > 0.0, 10.0 * weight_c / weight_e, 100.0)
    half_top = 0.5 * top_value
    shrink = 1.0 / half_top
    for copy in c_copies:
        copy.wait_recv()

    def wide5(tile):
        return jnp.concatenate([tile] * 5, axis=1)

    sub = iota((8, ECOLS), 0)
    lanes = iota((8, 128), 1)
    shrink5 = wide5(shrink)

    def scaled_c(i, _):
        rows = pl.ds(pl.multiple_of(i * 8, 8), 8)
        side = jnp.where(lanes < 64, cright[rows, :], cleft[rows, :])
        c = jnp.concatenate([cext[rows, 0:COLS], side], axis=1) * shrink5
        c = c * jnp.where(i == 0, has_up, jnp.where(i == EROWS // 8 - 1, has_down, 1.0))
        cs[rows, :] = c
        crec[rows, :] = 1.0 / c
        return 0

    lax.fori_loop(0, EROWS // 8, scaled_c, 0)
    for copy in f_copies:
        copy.wait_recv()

    def sides(i, _):
        rows = pl.ds(pl.multiple_of(i * 8, 8), 8)
        from_right, from_left = fright[rows, :], fleft[rows, :]
        bx[rows, COLS:ECOLS] = jnp.where(lanes < 64, from_right, from_left)
        by[rows, COLS:ECOLS] = jnp.where(lanes < 64, rolled(from_right, 64, 1), rolled(from_left, 64, 1))
        return 0

    lax.fori_loop(0, EROWS // 8, sides, 0)
    bx[bottom, :] = bx[bottom, :] * has_down

    def tile_at(ref, i):
        return ref[8 * i:8 * i + 8, :]

    def below_of(x, nxt):
        return jnp.where(sub == 7, rolled(nxt, -1, 0), rolled(x, -1, 0))

    def above_of(x, prv):
        return jnp.where(sub == 0, rolled(prv, 1, 0), rolled(x, 1, 0))

    TILES = EROWS // 8

    def inside(t):
        return t[:, 0:COLS]

    nil8 = jnp.zeros((8, COLS), F32)
    norm, sums = nil8, nil8
    wx = tile_at(bx, 0)
    for i in range(TILES):
        nxt = tile_at(bx, min(i + 1, TILES - 1))
        wy = tile_at(by, i)
        t = tile_at(cs, i) * ((below_of(wx, nxt) - wx) + (rolled(wy, -1, 1) - wy))
        tau[0, 8 * i:8 * i + 8, :] = t
        if 0 < i < TILES - 1:
            norm = norm + (inside(wx) * inside(wx) + inside(wy) * inside(wy))
            sums = sums + inside(t) * (inside(t) * inside(tile_at(crec, i)))
        wx = nxt
    acc[0] = sums
    acc[15] = norm
    last_diag = jnp.where((sub == 7) & (z == nz - 1), 3.0, 4.0)

    def sweep(k, start):
        cross_sum, square_sum = nil8, nil8
        first_tile, stop = (1, TILES - 1) if start == 2 else (0, TILES)
        prv = tau[k, 8 * max(first_tile - 1, 0):8 * max(first_tile - 1, 0) + 8, :]
        x = tau[k, 8 * first_tile:8 * first_tile + 8, :]
        for i in range(first_tile, stop):
            j = min(i + 1, TILES - 1)
            nxt = tau[k, 8 * j:8 * j + 8, :]
            around = (above_of(x, prv) + below_of(x, nxt)) + (rolled(x, -1, 1) + rolled(x, 1, 1))
            diag = last_diag if i == TILES - 2 else 4.0
            t = tile_at(cs, i) * (diag * x - around) - x
            if start > 0:
                t = 2.0 * t - tau[k - 1, 8 * i:8 * i + 8, :]
            tau[k + 1, 8 * i:8 * i + 8, :] = t
            if 0 < i < TILES - 1:
                q = inside(t) * inside(tile_at(crec, i))
                cross_sum = cross_sum + inside(x) * q
                square_sum = square_sum + inside(t) * q
            prv, x = x, nxt
        acc[2 * k + 1] = cross_sum
        acc[2 * k + 2] = square_sum

    sweep(0, 0)

    def sweeps(k, _):
        sweep(k, 1)
        return 0

    lax.fori_loop(1, ITERS - 2, sweeps, 0)
    sweep(ITERS - 2, 2)
    dots = [acc[k] for k in range(16)]

    def fold(t):
        s0 = dd_add(two_sum(t[:, 0:128], t[:, 128:256]), two_sum(t[:, 256:384], t[:, 384:512]))
        return s0

    level = [fold(t) for t in dots]
    for width, span in ((8, 4), (4, 2), (2, 1)):
        mask = sub8 % (2 * span) < span

        def merge(p, q, mask=mask, span=span):
            def parts(g, h):
                w = jnp.where(mask, h, g)
                return jnp.where(mask, g, h), jnp.where(mask, rolled(w, -span, 0), rolled(w, span, 0))
            xh_, yh_ = parts(p[0], q[0])
            xl_, yl_ = parts(p[1], q[1])
            return dd_add((xh_, xl_), (yh_, yl_))

        level = [merge(level[i], level[i + width]) for i in range(width)]
    for s in (64, 32, 16, 8, 4, 2, 1):
        level = [dd_add(p, (rolled(p[0], s, 1), rolled(p[1], s, 1))) for p in level]
    even, odd = level

    dtmsg[0] = jnp.where(lane8 < 32, even[0], jnp.where(lane8 < 64, odd[0], jnp.where(lane8 < 96, even[1], odd[1])))
    dtz_copies = spread_z(dtmsg.at[0], dtz, dtzs, dtzr)
    arrived(dtmsg.at[0], dtz, dtzs, dtzr, zpeers)

    def gathered(slots, count):
        level = [(slots[k], rolled(slots[k], 64, 1)) for k in range(count)]
        while len(level) > 1:
            level = [dd_add(level[2 * i], level[2 * i + 1]) for i in range(len(level) // 2)]
        return level[0]

    sums = gathered(dtz, nz)
    dtmsg[1] = jnp.where(lane8 < 64, sums[0], rolled(sums[1], 64, 1))
    dta_copies = spread_a(dtmsg.at[1], dta, dtas, dtar)
    arrived(dtmsg.at[1], dta, dtas, dtar, apeers)
    sums = gathered(dta, na)

    def pick(value, lane):
        return jnp.broadcast_to(value[:, lane:lane + 1], (8, 128))

    def row_of(value, r):
        return tuple(jnp.broadcast_to(part_[r:r + 1, :], (8, 128)) for part_ in value)

    even = pick(sums[0], 0), pick(sums[1], 0)
    odd = pick(sums[0], 32), pick(sums[1], 32)
    square = row_of(odd, 7)
    even = dd_add((2.0 * even[0], 2.0 * even[1]), dd_neg(row_of(even, 0)))
    odd = dd_add((2.0 * odd[0], 2.0 * odd[1]), dd_neg(row_of(odd, 0)))

    MOM, SEC, GRAM, MIX = range(4)
    nsc[...] = jnp.zeros(nsc.shape, F32)
    for part_ in range(2):
        for j in range(15):
            value = (even, odd)[j % 2][part_][j // 2:j // 2 + 1, :]
            nsc[MOM, part_, 8 + j:9 + j, :] = value
            if j == 1:
                nsc[MOM, part_, 7:8, :] = value

    def entries(which, start, count=8):
        return nsc[which, 0, start:start + count, :], nsc[which, 1, start:start + count, :]

    def widened(which, start):
        return dd_add(entries(which, start), dd_half(dd_add(entries(which, start + 1), entries(which, start - 1))))

    for start in (8, 16):
        value = widened(MOM, start)
        nsc[SEC, 0, start:start + 8, :], nsc[SEC, 1, start:start + 8, :] = value
        mix = dd_add(entries(MOM, start), dd_scale(value, half_top))
        nsc[MIX, 0, start:start + 8, :], nsc[MIX, 1, start:start + 8, :] = mix
    for part_ in range(2):
        nsc[SEC, part_, 7:8, :] = nsc[SEC, part_, 9:10, :]
    for start in (8, 16):
        value = dd_add(entries(SEC, start), dd_scale(widened(SEC, start), half_top))
        nsc[GRAM, 0, start:start + 8, :], nsc[GRAM, 1, start:start + 8, :] = value
    for part_ in range(2):
        for j in range(1, 8):
            nsc[GRAM, part_, 8 - j:9 - j, :] = nsc[GRAM, part_, 8 + j:9 + j, :]

    def with_first(value, head):
        return tuple(jnp.where(sub8 == 0, h, v) for v, h in zip(value, head))

    moment0 = row_of(entries(MOM, 8), 0)
    matrix = [with_first(entries(MIX, 7), dd_add(square, dd_scale(moment0, half_top)))]
    for l in range(ITERS - 1):
        column = dd_half(dd_add(entries(GRAM, 7 + l), entries(GRAM, 7 - l)))
        matrix.append(with_first(column, row_of(entries(MIX, 8 + l), 0)))
    right_side = with_first(entries(MOM, 7), square)
    diagonal = jnp.zeros((8, 128), F32)
    first_diagonal = [row_of(matrix[k], k)[0] for k in range(ITERS)]
    for k in range(ITERS):
        pivot = row_of(matrix[k], k)
        usable = pivot[0] > 1e-11 * first_diagonal[k]
        safe = jnp.where(usable, pivot[0], 1.0), jnp.where(usable, pivot[1], 0.0)
        factor = dd_div(matrix[k], safe)
        skip = (sub8 == k) | jnp.logical_not(usable)
        factor = tuple(jnp.where(skip, 0.0, f) for f in factor)
        diagonal = jnp.where((sub8 == k) & usable, pivot[0], diagonal)
        for l in range(k + 1, ITERS):
            matrix[l] = dd_add(matrix[l], dd_neg(dd_mul(factor, row_of(matrix[l], k))))
        right_side = dd_add(right_side, dd_neg(dd_mul(factor, row_of(right_side, k))))
    answer = jnp.where(diagonal > 0.0, right_side[0] / jnp.where(diagonal > 0.0, diagonal, 1.0), 0.0)
    nsc[MOM, 0, 0:8, :] = answer

    weights = [jnp.broadcast_to(nsc[MOM, 0, k:k + 1, :], (8, 128)) for k in range(ITERS)]

    def combined(j, w):
        return functools.reduce(lambda s, t: s + t, [w[l + 1] * tau[l, 8 * j:8 * j + 8, :] for l in range(ITERS - 1)])

    w5 = [wide5(w) for w in weights]
    gain = wide(weights[0])
    prv = combined(0, w5)
    for i in range(ROWS // 8):
        here = combined(i + 1, w5)
        solv[0, 8 * i:8 * i + 8, :] = gain * inside(tile_at(bx, i + 1)) - inside(here - above_of(here, prv))
        solv[1, 8 * i:8 * i + 8, :] = gain * inside(tile_at(by, i + 1)) - inside(here - rolled(here, 1, 1))
        prv = here
    solved_out = pltpu.make_async_copy(solv, out.at[pl.ds(1, 2)], outsem.at[1])
    solved_out.start()
    for copy in sends + stz_copies + sta_copies + dtz_copies + dta_copies:
        copy.wait_send()
    rate_out.wait()
    solved_out.wait()


def per_device(nz, na, wave_state, depth_class, onset_flag, cessation, class_depth):
    across, along = tridiagonal_inverse(ROWS), tridiagonal_inverse(COLS)
    xh, xl = halves(across)
    yh, yl = halves(along)
    exl = np.repeat(across[:, :1], 128, axis=1).astype(np.float32)
    exr = np.repeat(across[:, -1:], 128, axis=1).astype(np.float32)
    ey = np.zeros((8, 128), np.float32)
    ey[0] = along[0, :128]
    ey[1] = along[-1, -128:]
    consts = [jnp.asarray(t) for t in (xh, xl, yh, yl, exl, exr, ey)]
    dma = pltpu.SemaphoreType.DMA

    def vm(*shape, dtype=F32):
        return pltpu.VMEM(shape, dtype)

    scratch = [
        vm(3, ROWS, COLS), vm(ROWS, COLS, dtype=jnp.int32), vm(ROWS, COLS, dtype=jnp.int32), vm(ROWS, COLS, dtype=jnp.int32),
        vm(ROWS, ROWS, dtype=BF16), vm(ROWS, ROWS, dtype=BF16), vm(COLS, COLS, dtype=BF16), vm(COLS, COLS, dtype=BF16),
        vm(ROWS, 128), vm(ROWS, 128), vm(8, 128),
        vm(8, ROWS + 2 * FPAD, COLS), vm(ROWS, COLS),
        vm(6, ROWS, COLS, dtype=BF16), vm(6, ROWS, COLS, dtype=BF16), vm(6, ROWS, COLS, dtype=BF16), vm(6, ROWS, COLS, dtype=BF16),
        vm(6, ROWS, COLS), vm(6, ROWS, COLS), vm(10, 8, COLS), vm(10, 8, 128),
        vm(3, ROWS + 2 * FPAD, COLS), vm(2, ROWS, COLS), vm(ROWS, COLS), vm(2, ROWS, COLS),
        vm(2, 2, 3, 8, COLS), vm(2, 2, 3, 8, COLS), vm(2, 2, 3, 8, 128), vm(2, 2, 3, 8, 128),
        vm(EROWS, ECOLS), vm(EROWS, ECOLS), vm(EROWS, ECOLS), vm(EROWS, ECOLS),
        vm(EROWS, 128), vm(EROWS, 128), vm(EROWS, 128), vm(EROWS, 128), vm(2, ROWS, 128),
        vm(ITERS, EROWS, ECOLS), vm(EROWS, ECOLS), vm(16, 8, COLS),
        vm(2, 8, 128), vm(nz, 8, 128), vm(na, 8, 128), vm(2, 8, 128), vm(nz, 8, 128), vm(na, 8, 128), vm(4, 2, 32, 128),
        dma((11,)), dma((2,)), dma((26,)), dma((2, 2)), dma((2, 2)), dma((2,)), dma((2,)), dma((4,)), dma((4,)), dma((2,)), dma((4,)),
        dma((nz - 1,)), dma((na - 1,)), dma((nz - 1,)), dma((na - 1,)), dma((nz,)), dma((na,)), dma((nz,)), dma((na,)),
    ]
    anywhere = pl.BlockSpec(memory_space=pl.ANY)
    return pl.pallas_call(
        functools.partial(kernel, nz, na),
        out_shape=jax.ShapeDtypeStruct((3, ROWS, COLS), F32),
        in_specs=[anywhere] * 4 + [pl.BlockSpec(memory_space=pltpu.SMEM)] + [anywhere] * 7,
        out_specs=anywhere,
        scratch_shapes=scratch,
        compiler_params=pltpu.CompilerParams(collective_id=0, has_side_effects=True, vmem_limit_bytes=VMEM_BYTES),
    )(wave_state, depth_class, onset_flag, cessation, class_depth, *consts)


def solution(mesh):
    sizes = dict(mesh.shape)
    in_specs = (P(None, "xs", "al"), P("xs", "al"), P("xs", "al"), P("xs", "al"), P())
    return jax.shard_map(
        functools.partial(per_device, sizes["xs"], sizes["al"]),
        mesh=mesh, in_specs=in_specs, out_specs=P(None, "xs", "al"), check_vma=False,
    )
```

```python
import functools

import jax
import jax.numpy as jnp
import numpy as np
from jax import lax
from jax.experimental import pallas as pl
from jax.experimental.pallas import tpu as pltpu
from jax.sharding import PartitionSpec as P

MESH = pl.DeviceIdType.MESH
CLASSES = 8
ITERS = 8
ROWS, COLS = 128, 512
HALO = 8
EROWS, ECOLS = ROWS + 2 * HALO, COLS + 128
FPAD = 16
Q = 1.0 / 3.0
A2 = 0.5 * 14.0 / 9.0
B4 = 0.25 / 9.0
BREAKING = 0.05
VMEM_BYTES = 63 * 2**20
F32, BF16 = jnp.float32, jnp.bfloat16


def tridiagonal_inverse(length):
    band = np.eye(length) + Q * (np.eye(length, k=1) + np.eye(length, k=-1))
    return np.linalg.inv(band)


CORNER = float(tridiagonal_inverse(ROWS)[0, 0])
NEXT = (1.0 - CORNER) / Q
LINK = Q * CORNER
COUPLE = 1.0 / (1.0 - LINK * LINK)


def halves(matrix):
    matrix = matrix.astype(np.float32)
    high = matrix.astype(jnp.bfloat16)
    low = (matrix - high.astype(np.float32)).astype(jnp.bfloat16)
    return high, low


def split_bf16(value):
    high = value.astype(BF16)
    return high, (value - high.astype(F32)).astype(BF16)


def two_sum(a, b):
    s = a + b
    t = s - a
    return s, (a - (s - t)) + (b - t)


def quick_sum(a, b):
    s = a + b
    return s, b - (s - a)


def cut(a):
    t = 4097.0 * a
    high = t - (t - a)
    return high, a - high


def two_prod(a, b):
    p = a * b
    ah, al = cut(a)
    bh, bl = cut(b)
    return p, ((ah * bh - p) + ah * bl + al * bh) + al * bl


def dd_add(a, b):
    s, e = two_sum(a[0], b[0])
    t, f = two_sum(a[1], b[1])
    s, e = quick_sum(s, e + t)
    return quick_sum(s, e + f)


def dd_neg(a):
    return -a[0], -a[1]


def dd_mul(a, b):
    p, e = two_prod(a[0], b[0])
    return quick_sum(p, e + (a[0] * b[1] + a[1] * b[0]))


def dd_scale(a, b):
    p, e = two_prod(a[0], b)
    return quick_sum(p, e + a[1] * b)


def dd_half(a):
    return 0.5 * a[0], 0.5 * a[1]


def dd_div(a, b):
    first = a[0] / b[0]
    rest = dd_add(a, dd_neg(dd_scale(b, first)))
    return quick_sum(first, rest[0] / b[0])


def rolled(value, shift, axis):
    size = value.shape[axis]
    return pltpu.roll(value, shift % size, axis)


def iota(shape, axis):
    return lax.broadcasted_iota(jnp.int32, shape, axis)


def lane_source(field):
    d = rolled(field, -1, 1) - rolled(field, 1, 1)
    s = A2 * d + B4 * (rolled(d, -1, 1) + rolled(d, 1, 1))
    lane = iota(field.shape, 1)
    return jnp.where((lane >= 2) & (lane < COLS - 2), s, 0.0)


def row_source(around, start):
    d = rolled(around, -1, 0) - rolled(around, 1, 0)
    s = (A2 * d + B4 * (rolled(d, -1, 0) + rolled(d, 1, 0)))[8:24]
    if start == 0:
        s = jnp.where(iota(s.shape, 0) >= 2, s, 0.0)
    if start == ROWS - 16:
        s = jnp.where(iota(s.shape, 0) < 14, s, 0.0)
    return s


def edge_items(f):
    return A2 * f[1] + B4 * f[2], A2 * (f[2] - f[0]) + B4 * f[3]


def kernel(nz, na, ws, dc, on, ce, cd, xhl, yh, yl, exl, exr, ey, out,
           wv, dv, ov, cv, xhv, yhv, ylv, exlv, exrv, eyv,
           fld, dep, sxh, sxl, syh, syl, hx, hy, er, ec, stress, part, ratev, solv,
           rowmsg, rowgot, colmsg, colgot, bx, by, cext, cs, cright, cleft, fright, fleft, fmsg, tau, crec, acc,
           stmsg, stz, sta, dtmsg, dtz, dta, nsc,
           insem, outsem, ssem, rowsem, colsem, crowsem, ccolsem, ccorsem, frowsem, fcolsem, fcorsem,
           stzs, stas, dtzs, dtas, stzr, star, dtzr, dtar):
    z, a = lax.axis_index("xs"), lax.axis_index("al")
    up, down = lax.rem(z + nz - 1, nz), lax.rem(z + 1, nz)
    left, right = lax.rem(a + na - 1, na), lax.rem(a + 1, na)
    has_up = (z > 0).astype(F32)
    has_down = (z < nz - 1).astype(F32)

    barrier = pltpu.get_barrier_semaphore()
    zpeers = [lax.rem(z + k, nz) for k in sorted(range(1, nz), key=lambda k: -min(k, nz - k))]
    apeers = [lax.rem(a + k, na) for k in range(1, na)]
    corners = [(up, left), (up, right), (down, left), (down, right)]
    greet = [(p, a) for p in zpeers] + [(z, p) for p in apeers] + corners
    loads = [pltpu.make_async_copy(s, d, insem.at[k]) for k, (s, d) in enumerate(
        [(ws, wv), (dc, dv), (on, ov), (ce, cv), (xhl, xhv), (yh, yhv), (yl, ylv), (exl, exlv), (exr, exrv), (ey, eyv)])]
    for load in loads:
        load.start()
    for who in greet:
        pl.semaphore_signal(barrier, inc=1, device_id=who, device_id_type=MESH)

    sends = []

    def send(src, dst, sem_index, recv, who):
        copy = pltpu.make_async_remote_copy(src_ref=src, dst_ref=dst, send_sem=ssem.at[sem_index], recv_sem=recv,
                                            device_id=who, device_id_type=MESH)
        copy.start()
        sends.append(copy)
        return copy

    for load in loads[:2]:
        load.wait()
    SUR, FX, FY, U, V, FXU, FXV, FYV = range(8)
    ACROSS = (SUR, FX, U, V, FXU, FXV)
    ALONG = (SUR, FY, U, V, FXV, FYV)

    def first(i, sums):
        rows = pl.ds(i * 16, 16)
        inner = pl.ds(i * 16 + FPAD, 16)
        kind = dv[rows, :]
        still = jnp.full((16, COLS), cd[0], F32)
        for k in range(1, CLASSES):
            still = jnp.where(kind == k, cd[k], still)
        surface, px, py = wv[0, rows, :], wv[1, rows, :], wv[2, rows, :]
        depth = still + surface
        u, v = px / depth, py / depth
        fields = [surface, px, py, u, v, px * u, px * v, py * v]
        for k, f in enumerate(fields):
            fld[k, inner, :] = f
        dep[rows, :] = depth
        c = depth * depth * (1.0 / 3.0)
        cext[pl.ds(i * 16 + HALO, 16), 0:COLS] = c
        for k, f in enumerate(ALONG):
            high, low = split_bf16(lane_source(fields[f]))
            syh[k, rows, :] = high
            syl[k, rows, :] = low
        energy = surface * surface + px * px + py * py
        return sums[0] + c * energy, sums[1] + energy

    nil = jnp.zeros((16, COLS), F32)
    stat = nil, nil
    for i in range(ROWS // 16):
        stat = first(i, stat)

    def across_sources(ref, which):
        for k, f in enumerate(which):
            for i in range(ROWS // 16):
                around = ref[f, i * 16 + FPAD - 8:i * 16 + FPAD + 24, :]
                high, low = split_bf16(row_source(around, i * 16))
                sxh[k, i * 16:i * 16 + 16, :] = high
                sxl[k, i * 16:i * 16 + 16, :] = low

    def solves(count):
        dot = functools.partial(jnp.dot, preferred_element_type=F32)
        high = syh[0:count].reshape(count * ROWS, COLS)
        low = syl[0:count].reshape(count * ROWS, COLS)
        solved = dot(high, yhv[...]) + (dot(low, yhv[...]) + dot(high, ylv[...]))
        hy[0:count] = solved.reshape(count, ROWS, COLS)
        for k in range(count):
            both = dot(xhv[...], sxh[k])
            hx[k] = both[0:ROWS] + (both[ROWS:] + dot(xhv[0:ROWS, :], sxl[k]))

    lane128 = iota((ROWS, 128), 1)

    def edges_out(ref, across, along, stage):
        for k, f in enumerate(across):
            for j in range(4):
                er[j, k:k + 1, :] = ref[f, FPAD + j:FPAD + j + 1, :]
                er[4 + j, k:k + 1, :] = ref[f, FPAD + ROWS - 1 - j:FPAD + ROWS - j, :]
            er[8, k:k + 1, :] = hx[k, 0:1, :]
            er[9, k:k + 1, :] = hx[k, ROWS - 1:ROWS, :]
        for k, f in enumerate(along):
            fl = ref[f, FPAD:FPAD + ROWS, 0:128]
            fr = ref[f, FPAD:FPAD + ROWS, COLS - 128:COLS]
            tile = jnp.where(lane128 < 32, fl, jnp.where(lane128 < 64, rolled(hy[k, :, 0:128], 32, 1), jnp.where(
                lane128 < 96, rolled(hy[k, :, COLS - 128:COLS], -32, 1), fr)))
            turned = tile.T
            for j in range(4):
                ec[j, k:k + 1, :] = turned[j:j + 1, :]
                ec[4 + j, k:k + 1, :] = turned[127 - j:128 - j, :]
            ec[8, k:k + 1, :] = turned[32:33, :]
            ec[9, k:k + 1, :] = turned[95:96, :]
        for e, msg in ((er, rowmsg), (ec, colmsg)):
            s0, s1 = edge_items([e[j] for j in range(4)])
            msg[stage, 0, 0] = e[0]
            msg[stage, 0, 1] = e[1]
            msg[stage, 0, 2] = e[8] + CORNER * s0 + NEXT * s1
            t0, t1 = edge_items([e[4 + j] for j in range(4)])
            msg[stage, 1, 0] = e[4]
            msg[stage, 1, 1] = e[5]
            msg[stage, 1, 2] = e[9] - CORNER * t0 - NEXT * t1

    def edges_send(stage):
        base = 4 * stage
        return [
            send(rowmsg.at[stage, 0], rowgot.at[stage, 1], base, rowsem.at[stage, 1], (up, a)),
            send(rowmsg.at[stage, 1], rowgot.at[stage, 0], base + 1, rowsem.at[stage, 0], (down, a)),
            send(colmsg.at[stage, 0], colgot.at[stage, 1], base + 2, colsem.at[stage, 1], (z, left)),
            send(colmsg.at[stage, 1], colgot.at[stage, 0], base + 3, colsem.at[stage, 0], (z, right)),
        ]

    def closing(e, got, keep_low, keep_high):
        f0, f1 = e[0], e[1]
        p1, p2, ph = got[0, 0] * keep_low, got[0, 1] * keep_low, got[0, 2]
        s0, s1 = edge_items([e[j] for j in range(4)])
        s0 = s0 - A2 * p1 - B4 * p2
        s1 = s1 - B4 * p1
        own = e[8] + CORNER * s0 + NEXT * s1
        theirs = ph + CORNER * (A2 * f0 + B4 * f1) + NEXT * (B4 * f0)
        gp = (theirs - LINK * own) * COUPLE * keep_low
        low, low_end = s0 - s1 * (1.0 / Q) - Q * gp, s1 * (1.0 / Q)
        l0, l1 = e[4], e[5]
        n1, n2, nh = got[1, 0] * keep_high, got[1, 1] * keep_high, got[1, 2]
        t0, t1 = edge_items([e[4 + j] for j in range(4)])
        t0 = A2 * n1 + B4 * n2 - t0
        t1 = B4 * n1 - t1
        own = e[9] + CORNER * t0 + NEXT * t1
        theirs = nh - CORNER * (A2 * l0 + B4 * l1) - NEXT * (B4 * l0)
        gn = (theirs - LINK * own) * COUPLE * keep_high
        return low, t0 - t1 * (1.0 / Q) - Q * gn, low_end, t1 * (1.0 / Q)

    def close_across(count, stage):
        low, high, low_end, high_end = closing(er, rowgot.at[stage], has_up, has_down)
        for k in range(count):
            hx[k, 0:1, :] = hx[k, 0:1, :] + low_end[k:k + 1, :]
            hx[k, ROWS - 1:ROWS, :] = hx[k, ROWS - 1:ROWS, :] + high_end[k:k + 1, :]
        return low, high

    def close_along(count, stage):
        terms = closing(ec, colgot.at[stage], 1.0, 1.0)
        block = jnp.concatenate(list(terms) + [jnp.zeros((96, 128), F32)], axis=0)
        turned = block.T
        for k in range(count):
            col = [jnp.broadcast_to(turned[:, 8 * j + k:8 * j + k + 1], (ROWS, 128)) for j in range(4)]
            hy[k, :, 0:128] = hy[k, :, 0:128] + col[0] * eyv[0:1, :] + jnp.where(lane128 == 0, col[2], 0.0)
            hy[k, :, COLS - 128:COLS] = (hy[k, :, COLS - 128:COLS] + col[1] * eyv[1:2, :]
                                         + jnp.where(lane128 == 127, col[3], 0.0))

    across_sources(fld, ACROSS)
    for load in loads[4:]:
        load.wait()
    solves(6)
    edges_out(fld, ACROSS, ALONG, 0)

    stat_c, stat_e = [t[0:8] + t[8:16] for t in stat]
    stat_c, stat_e = [sum(t[:, 128 * j:128 * (j + 1)] for j in range(4)) for t in (stat_c, stat_e)]
    sub8, lane8 = iota((8, 128), 0), iota((8, 128), 1)
    mixed = jnp.where(sub8 < 4, stat_c + rolled(stat_c, 4, 0), stat_e + rolled(stat_e, 4, 0))
    for s in (64, 32, 16, 8, 4, 2, 1):
        mixed = mixed + rolled(mixed, s, 1)
    mixed = mixed + jnp.where(sub8 % 4 < 2, rolled(mixed, -2, 0), rolled(mixed, 2, 0))
    mixed = mixed + jnp.where(sub8 % 2 < 1, rolled(mixed, -1, 0), rolled(mixed, 1, 0))
    stmsg[0] = mixed

    pl.semaphore_wait(barrier, len(greet))

    first_edges = edges_send(0)

    def spread_z(msg, slots, ss, rs):
        copies = []
        for k, p in enumerate(zpeers):
            copy = pltpu.make_async_remote_copy(src_ref=msg, dst_ref=slots.at[z], send_sem=ss.at[k], recv_sem=rs.at[z],
                                                device_id=(p, a), device_id_type=MESH)
            copy.start()
            copies.append(copy)
        slots[z] = msg[...]
        return copies

    def spread_a(msg, slots, ss, rs):
        copies = []
        for k, p in enumerate(apeers):
            copy = pltpu.make_async_remote_copy(src_ref=msg, dst_ref=slots.at[a], send_sem=ss.at[k], recv_sem=rs.at[a],
                                                device_id=(z, p), device_id_type=MESH)
            copy.start()
            copies.append(copy)
        slots[a] = msg[...]
        return copies

    def arrived(msg, slots, ss, rs, peers):
        for k, p in enumerate(peers):
            pltpu.make_async_remote_copy(src_ref=msg, dst_ref=slots.at[p], send_sem=ss.at[k], recv_sem=rs.at[p],
                                         device_id=(z, right), device_id_type=MESH).wait_recv()

    stz_copies = spread_z(stmsg.at[0], stz, stzs, stzr)

    top, bottom = pl.ds(0, HALO), pl.ds(EROWS - HALO, HALO)
    inner = pl.ds(HALO, ROWS)
    first_rows, last_rows = pl.ds(HALO, HALO), pl.ds(ROWS, HALO)
    low_cols, high_cols = pl.ds(0, 128), pl.ds(COLS - 128, 128)
    whole_cols = pl.ds(0, COLS)
    c_copies = [
        send(cext.at[first_rows, whole_cols], cext.at[bottom, whole_cols], 8, crowsem.at[1], (up, a)),
        send(cext.at[last_rows, whole_cols], cext.at[top, whole_cols], 9, crowsem.at[0], (down, a)),
        send(cext.at[inner, low_cols], cright.at[inner, :], 10, ccolsem.at[1], (z, left)),
        send(cext.at[inner, high_cols], cleft.at[inner, :], 11, ccolsem.at[0], (z, right)),
        send(cext.at[first_rows, low_cols], cright.at[bottom, :], 12, ccorsem.at[0], (up, left)),
        send(cext.at[first_rows, high_cols], cleft.at[bottom, :], 13, ccorsem.at[1], (up, right)),
        send(cext.at[last_rows, low_cols], cright.at[top, :], 14, ccorsem.at[2], (down, left)),
        send(cext.at[last_rows, high_cols], cleft.at[top, :], 15, ccorsem.at[3], (down, right)),
    ]

    for copy in first_edges:
        copy.wait_recv()
    xlow, xhigh = close_across(6, 0)
    close_along(6, 0)
    for load in loads[2:4]:
        load.wait()

    def wide(tile):
        return jnp.concatenate([tile] * 4, axis=1)

    er[0] = xlow
    er[1] = xhigh

    def second(i):
        rows = pl.ds(i * 16, 16)
        inner16 = pl.ds(i * 16 + FPAD, 16)
        wl, wr = wide(exlv[rows, :]), wide(exrv[rows, :])
        gx = [hx[k, rows, :] + (wl * er[0, k:k + 1, :] + wr * er[1, k:k + 1, :]) for k in range(6)]
        gy = [hy[k, rows, :] for k in range(6)]
        depth = dep[rows, :]
        rate = -(gx[1] + gy[1])
        active = (ov[rows, :] * (1 - cv[rows, :])).astype(F32)
        weight = BREAKING * active * depth * jnp.abs(rate) * depth
        sxx = 2.0 * weight * gx[2]
        sxy = weight * (gy[2] + gx[3])
        syy = 2.0 * weight * gy[3]
        ratev[rows, :] = -rate
        stress[0, inner16, :] = sxx
        stress[1, inner16, :] = sxy
        stress[2, inner16, :] = syy
        part[0, rows, :] = -gx[4] - gy[4] - depth * gx[0]
        part[1, rows, :] = -gx[5] - gy[5] - depth * gy[0]
        for k, f in enumerate((sxy, syy)):
            high, low = split_bf16(lane_source(f))
            syh[k, rows, :] = high
            syl[k, rows, :] = low

    for i in range(ROWS // 16):
        second(i)
    rate_out = pltpu.make_async_copy(ratev, out.at[0], outsem.at[0])
    rate_out.start()
    across_sources(stress, (0, 1))
    solves(2)
    edges_out(stress, (0, 1), (1, 2), 1)
    second_edges = edges_send(1)

    arrived(stmsg.at[0], stz, stzs, stzr, zpeers)
    stmsg[1] = functools.reduce(lambda s, k: s + stz[k], range(1, nz), stz[0])
    sta_copies = spread_a(stmsg.at[1], sta, stas, star)

    for copy in second_edges:
        copy.wait_recv()
    xlow, xhigh = close_across(2, 1)
    close_along(2, 1)
    er[0] = xlow
    er[1] = xhigh

    def third(i):
        rows = pl.ds(i * 16, 16)
        ext = pl.ds(i * 16 + HALO, 16)
        wl, wr = wide(exlv[rows, :]), wide(exrv[rows, :])
        gx = [hx[k, rows, :] + (wl * er[0, k:k + 1, :] + wr * er[1, k:k + 1, :]) for k in range(2)]
        fx = part[0, rows, :] + gx[0] + hy[0, rows, :]
        fy = part[1, rows, :] + gx[1] + hy[1, rows, :]
        bx[ext, 0:COLS] = fx
        by[ext, 0:COLS] = fy
        lane = iota((16, 128), 1)
        fmsg[0, rows, :] = jnp.where(lane < 64, fx[:, 0:128], rolled(fy[:, 0:128], 64, 1))
        fmsg[1, rows, :] = jnp.where(lane < 64, rolled(fy[:, COLS - 128:], 64, 1), fx[:, COLS - 128:])

    for i in range(ROWS // 16):
        third(i)
    lo8, hi8 = pl.ds(0, HALO), pl.ds(ROWS - HALO, HALO)
    f_copies = [
        send(bx.at[first_rows, whole_cols], bx.at[bottom, whole_cols], 16, frowsem.at[0], (up, a)),
        send(bx.at[last_rows, whole_cols], bx.at[top, whole_cols], 17, frowsem.at[1], (down, a)),
        send(by.at[first_rows, whole_cols], by.at[bottom, whole_cols], 18, frowsem.at[2], (up, a)),
        send(by.at[last_rows, whole_cols], by.at[top, whole_cols], 19, frowsem.at[3], (down, a)),
        send(fmsg.at[0], fright.at[inner, :], 20, fcolsem.at[1], (z, left)),
        send(fmsg.at[1], fleft.at[inner, :], 21, fcolsem.at[0], (z, right)),
        send(fmsg.at[0, lo8, :], fright.at[bottom, :], 22, fcorsem.at[0], (up, left)),
        send(fmsg.at[1, lo8, :], fleft.at[bottom, :], 23, fcorsem.at[1], (up, right)),
        send(fmsg.at[0, hi8, :], fright.at[top, :], 24, fcorsem.at[2], (down, left)),
        send(fmsg.at[1, hi8, :], fleft.at[top, :], 25, fcorsem.at[3], (down, right)),
    ]

    arrived(stmsg.at[1], sta, stas, star, apeers)
    total = functools.reduce(lambda s, k: s + sta[k], range(1, na), sta[0])
    weight_c = jnp.broadcast_to(total[0:1, 0:1], (8, 128))
    weight_e = jnp.broadcast_to(total[4:5, 0:1], (8, 128))
    top_value = jnp.where(weight_e > 0.0, 10.0 * weight_c / weight_e, 100.0)
    half_top = 0.5 * top_value
    shrink = 1.0 / half_top
    for copy in c_copies:
        copy.wait_recv()

    def wide5(tile):
        return jnp.concatenate([tile] * 5, axis=1)

    sub = iota((8, ECOLS), 0)
    lanes = iota((8, 128), 1)
    shrink5 = wide5(shrink)

    def scaled_c(i, _):
        rows = pl.ds(pl.multiple_of(i * 8, 8), 8)
        side = jnp.where(lanes < 64, cright[rows, :], cleft[rows, :])
        c = jnp.concatenate([cext[rows, 0:COLS], side], axis=1) * shrink5
        c = c * jnp.where(i == 0, has_up, jnp.where(i == EROWS // 8 - 1, has_down, 1.0))
        cs[rows, :] = c
        crec[rows, :] = 1.0 / c
        return 0

    lax.fori_loop(0, EROWS // 8, scaled_c, 0)
    for copy in f_copies:
        copy.wait_recv()

    def sides(i, _):
        rows = pl.ds(pl.multiple_of(i * 8, 8), 8)
        from_right, from_left = fright[rows, :], fleft[rows, :]
        bx[rows, COLS:ECOLS] = jnp.where(lanes < 64, from_right, from_left)
        by[rows, COLS:ECOLS] = jnp.where(lanes < 64, rolled(from_right, 64, 1), rolled(from_left, 64, 1))
        return 0

    lax.fori_loop(0, EROWS // 8, sides, 0)
    bx[bottom, :] = bx[bottom, :] * has_down

    def tile_at(ref, i):
        return ref[8 * i:8 * i + 8, :]

    def below_of(x, nxt):
        return jnp.where(sub == 7, rolled(nxt, -1, 0), rolled(x, -1, 0))

    def above_of(x, prv):
        return jnp.where(sub == 0, rolled(prv, 1, 0), rolled(x, 1, 0))

    TILES = EROWS // 8

    def inside(t):
        return t[:, 0:COLS]

    nil8 = jnp.zeros((8, COLS), F32)
    norm, sums = nil8, nil8
    wx = tile_at(bx, 0)
    for i in range(TILES):
        nxt = tile_at(bx, min(i + 1, TILES - 1))
        wy = tile_at(by, i)
        t = tile_at(cs, i) * ((below_of(wx, nxt) - wx) + (rolled(wy, -1, 1) - wy))
        tau[0, 8 * i:8 * i + 8, :] = t
        if 0 < i < TILES - 1:
            norm = norm + (inside(wx) * inside(wx) + inside(wy) * inside(wy))
            sums = sums + inside(t) * (inside(t) * inside(tile_at(crec, i)))
        wx = nxt
    acc[0] = sums
    acc[15] = norm
    last_diag = jnp.where((sub == 7) & (z == nz - 1), 3.0, 4.0)

    def sweep(k, start):
        cross_sum, square_sum = nil8, nil8
        first_tile, stop = (1, TILES - 1) if start == 2 else (0, TILES)
        prv = tau[k, 8 * max(first_tile - 1, 0):8 * max(first_tile - 1, 0) + 8, :]
        x = tau[k, 8 * first_tile:8 * first_tile + 8, :]
        for i in range(first_tile, stop):
            j = min(i + 1, TILES - 1)
            nxt = tau[k, 8 * j:8 * j + 8, :]
            around = (above_of(x, prv) + below_of(x, nxt)) + (rolled(x, -1, 1) + rolled(x, 1, 1))
            diag = last_diag if i == TILES - 2 else 4.0
            t = tile_at(cs, i) * (diag * x - around) - x
            if start > 0:
                t = 2.0 * t - tau[k - 1, 8 * i:8 * i + 8, :]
            tau[k + 1, 8 * i:8 * i + 8, :] = t
            if 0 < i < TILES - 1:
                q = inside(t) * inside(tile_at(crec, i))
                cross_sum = cross_sum + inside(x) * q
                square_sum = square_sum + inside(t) * q
            prv, x = x, nxt
        acc[2 * k + 1] = cross_sum
        acc[2 * k + 2] = square_sum

    sweep(0, 0)

    def sweeps(k, _):
        sweep(k, 1)
        return 0

    lax.fori_loop(1, ITERS - 2, sweeps, 0)
    sweep(ITERS - 2, 2)
    dots = [acc[k] for k in range(16)]

    def fold(t):
        s0 = dd_add(two_sum(t[:, 0:128], t[:, 128:256]), two_sum(t[:, 256:384], t[:, 384:512]))
        return s0

    level = [fold(t) for t in dots]
    for width, span in ((8, 4), (4, 2), (2, 1)):
        mask = sub8 % (2 * span) < span

        def merge(p, q, mask=mask, span=span):
            def parts(g, h):
                w = jnp.where(mask, h, g)
                return jnp.where(mask, g, h), jnp.where(mask, rolled(w, -span, 0), rolled(w, span, 0))
            xh_, yh_ = parts(p[0], q[0])
            xl_, yl_ = parts(p[1], q[1])
            return dd_add((xh_, xl_), (yh_, yl_))

        level = [merge(level[i], level[i + width]) for i in range(width)]
    for s in (64, 32, 16, 8, 4, 2, 1):
        level = [dd_add(p, (rolled(p[0], s, 1), rolled(p[1], s, 1))) for p in level]
    even, odd = level

    dtmsg[0] = jnp.where(lane8 < 32, even[0], jnp.where(lane8 < 64, odd[0], jnp.where(lane8 < 96, even[1], odd[1])))
    dtz_copies = spread_z(dtmsg.at[0], dtz, dtzs, dtzr)
    arrived(dtmsg.at[0], dtz, dtzs, dtzr, zpeers)

    def gathered(slots, count):
        level = [(slots[k], rolled(slots[k], 64, 1)) for k in range(count)]
        while len(level) > 1:
            level = [dd_add(level[2 * i], level[2 * i + 1]) for i in range(len(level) // 2)]
        return level[0]

    sums = gathered(dtz, nz)
    dtmsg[1] = jnp.where(lane8 < 64, sums[0], rolled(sums[1], 64, 1))
    dta_copies = spread_a(dtmsg.at[1], dta, dtas, dtar)
    arrived(dtmsg.at[1], dta, dtas, dtar, apeers)
    sums = gathered(dta, na)

    def pick(value, lane):
        return jnp.broadcast_to(value[:, lane:lane + 1], (8, 128))

    def row_of(value, r):
        return tuple(jnp.broadcast_to(part_[r:r + 1, :], (8, 128)) for part_ in value)

    even = pick(sums[0], 0), pick(sums[1], 0)
    odd = pick(sums[0], 32), pick(sums[1], 32)
    square = row_of(odd, 7)
    even = dd_add((2.0 * even[0], 2.0 * even[1]), dd_neg(row_of(even, 0)))
    odd = dd_add((2.0 * odd[0], 2.0 * odd[1]), dd_neg(row_of(odd, 0)))

    MOM, SEC, GRAM, MIX = range(4)
    nsc[...] = jnp.zeros(nsc.shape, F32)
    for part_ in range(2):
        for j in range(15):
            value = (even, odd)[j % 2][part_][j // 2:j // 2 + 1, :]
            nsc[MOM, part_, 8 + j:9 + j, :] = value
            if j == 1:
                nsc[MOM, part_, 7:8, :] = value

    def entries(which, start, count=8):
        return nsc[which, 0, start:start + count, :], nsc[which, 1, start:start + count, :]

    def widened(which, start):
        return dd_add(entries(which, start), dd_half(dd_add(entries(which, start + 1), entries(which, start - 1))))

    for start in (8, 16):
        value = widened(MOM, start)
        nsc[SEC, 0, start:start + 8, :], nsc[SEC, 1, start:start + 8, :] = value
        mix = dd_add(entries(MOM, start), dd_scale(value, half_top))
        nsc[MIX, 0, start:start + 8, :], nsc[MIX, 1, start:start + 8, :] = mix
    for part_ in range(2):
        nsc[SEC, part_, 7:8, :] = nsc[SEC, part_, 9:10, :]
    for start in (8, 16):
        value = dd_add(entries(SEC, start), dd_scale(widened(SEC, start), half_top))
        nsc[GRAM, 0, start:start + 8, :], nsc[GRAM, 1, start:start + 8, :] = value
    for part_ in range(2):
        for j in range(1, 8):
            nsc[GRAM, part_, 8 - j:9 - j, :] = nsc[GRAM, part_, 8 + j:9 + j, :]

    def with_first(value, head):
        return tuple(jnp.where(sub8 == 0, h, v) for v, h in zip(value, head))

    moment0 = row_of(entries(MOM, 8), 0)
    matrix = [with_first(entries(MIX, 7), dd_add(square, dd_scale(moment0, half_top)))]
    for l in range(ITERS - 1):
        column = dd_half(dd_add(entries(GRAM, 7 + l), entries(GRAM, 7 - l)))
        matrix.append(with_first(column, row_of(entries(MIX, 8 + l), 0)))
    right_side = with_first(entries(MOM, 7), square)
    diagonal = jnp.zeros((8, 128), F32)
    first_diagonal = [row_of(matrix[k], k)[0] for k in range(ITERS)]
    for k in range(ITERS):
        pivot = row_of(matrix[k], k)
        usable = pivot[0] > 1e-11 * first_diagonal[k]
        safe = jnp.where(usable, pivot[0], 1.0), jnp.where(usable, pivot[1], 0.0)
        factor = dd_div(matrix[k], safe)
        skip = (sub8 == k) | jnp.logical_not(usable)
        factor = tuple(jnp.where(skip, 0.0, f) for f in factor)
        diagonal = jnp.where((sub8 == k) & usable, pivot[0], diagonal)
        for l in range(k + 1, ITERS):
            matrix[l] = dd_add(matrix[l], dd_neg(dd_mul(factor, row_of(matrix[l], k))))
        right_side = dd_add(right_side, dd_neg(dd_mul(factor, row_of(right_side, k))))
    answer = jnp.where(diagonal > 0.0, right_side[0] / jnp.where(diagonal > 0.0, diagonal, 1.0), 0.0)
    nsc[MOM, 0, 0:8, :] = answer

    weights = [jnp.broadcast_to(nsc[MOM, 0, k:k + 1, :], (8, 128)) for k in range(ITERS)]

    def combined(j, w):
        return functools.reduce(lambda s, t: s + t, [w[l + 1] * tau[l, 8 * j:8 * j + 8, :] for l in range(ITERS - 1)])

    w5 = [wide5(w) for w in weights]
    gain = wide(weights[0])
    prv = combined(0, w5)
    for i in range(ROWS // 8):
        here = combined(i + 1, w5)
        solv[0, 8 * i:8 * i + 8, :] = inside(here - above_of(here, prv)) - gain * inside(tile_at(bx, i + 1))
        solv[1, 8 * i:8 * i + 8, :] = inside(here - rolled(here, 1, 1)) - gain * inside(tile_at(by, i + 1))
        prv = here
    solved_out = pltpu.make_async_copy(solv, out.at[pl.ds(1, 2)], outsem.at[1])
    solved_out.start()
    for copy in sends + stz_copies + sta_copies + dtz_copies + dta_copies:
        copy.wait_send()
    rate_out.wait()
    solved_out.wait()


def per_device(nz, na, wave_state, depth_class, onset_flag, cessation, class_depth):
    across, along = tridiagonal_inverse(ROWS), tridiagonal_inverse(COLS)
    xhl = np.concatenate(halves(across), axis=0)
    yh, yl = halves(along)
    exl = np.repeat(across[:, :1], 128, axis=1).astype(np.float32)
    exr = np.repeat(across[:, -1:], 128, axis=1).astype(np.float32)
    ey = np.zeros((8, 128), np.float32)
    ey[0] = along[0, :128]
    ey[1] = along[-1, -128:]
    consts = [jnp.asarray(t) for t in (xhl, yh, yl, exl, exr, ey)]
    dma = pltpu.SemaphoreType.DMA

    def vm(*shape, dtype=F32):
        return pltpu.VMEM(shape, dtype)

    scratch = [
        vm(3, ROWS, COLS), vm(ROWS, COLS, dtype=jnp.int32), vm(ROWS, COLS, dtype=jnp.int32), vm(ROWS, COLS, dtype=jnp.int32),
        vm(2 * ROWS, ROWS, dtype=BF16), vm(COLS, COLS, dtype=BF16), vm(COLS, COLS, dtype=BF16),
        vm(ROWS, 128), vm(ROWS, 128), vm(8, 128),
        vm(8, ROWS + 2 * FPAD, COLS), vm(ROWS, COLS),
        vm(6, ROWS, COLS, dtype=BF16), vm(6, ROWS, COLS, dtype=BF16), vm(6, ROWS, COLS, dtype=BF16), vm(6, ROWS, COLS, dtype=BF16),
        vm(6, ROWS, COLS), vm(6, ROWS, COLS), vm(10, 8, COLS), vm(10, 8, 128),
        vm(3, ROWS + 2 * FPAD, COLS), vm(2, ROWS, COLS), vm(ROWS, COLS), vm(2, ROWS, COLS),
        vm(2, 2, 3, 8, COLS), vm(2, 2, 3, 8, COLS), vm(2, 2, 3, 8, 128), vm(2, 2, 3, 8, 128),
        vm(EROWS, ECOLS), vm(EROWS, ECOLS), vm(EROWS, ECOLS), vm(EROWS, ECOLS),
        vm(EROWS, 128), vm(EROWS, 128), vm(EROWS, 128), vm(EROWS, 128), vm(2, ROWS, 128),
        vm(ITERS, EROWS, ECOLS), vm(EROWS, ECOLS), vm(16, 8, COLS),
        vm(2, 8, 128), vm(nz, 8, 128), vm(na, 8, 128), vm(2, 8, 128), vm(nz, 8, 128), vm(na, 8, 128), vm(4, 2, 32, 128),
        dma((11,)), dma((2,)), dma((26,)), dma((2, 2)), dma((2, 2)), dma((2,)), dma((2,)), dma((4,)), dma((4,)), dma((2,)), dma((4,)),
        dma((nz - 1,)), dma((na - 1,)), dma((nz - 1,)), dma((na - 1,)), dma((nz,)), dma((na,)), dma((nz,)), dma((na,)),
    ]
    anywhere = pl.BlockSpec(memory_space=pl.ANY)
    negated = pl.pallas_call(
        functools.partial(kernel, nz, na),
        out_shape=jax.ShapeDtypeStruct((3, ROWS, COLS), F32),
        in_specs=[anywhere] * 4 + [pl.BlockSpec(memory_space=pltpu.SMEM)] + [anywhere] * 6,
        out_specs=anywhere,
        scratch_shapes=scratch,
        compiler_params=pltpu.CompilerParams(collective_id=0, has_side_effects=True, vmem_limit_bytes=VMEM_BYTES),
    )(wave_state, depth_class, onset_flag, cessation, class_depth, *consts)
    return -negated


def solution(mesh):
    sizes = dict(mesh.shape)
    in_specs = (P(None, "xs", "al"), P("xs", "al"), P("xs", "al"), P("xs", "al"), P())
    return jax.shard_map(
        functools.partial(per_device, sizes["xs"], sizes["al"]),
        mesh=mesh, in_specs=in_specs, out_specs=P(None, "xs", "al"), check_vma=False,
    )
```

```python
import functools

import jax
import jax.numpy as jnp
import numpy as np
from jax import lax
from jax.experimental import pallas as pl
from jax.experimental.pallas import tpu as pltpu
from jax.sharding import PartitionSpec as P

MESH = pl.DeviceIdType.MESH
CLASSES = 8
ITERS = 8
ROWS, COLS = 128, 512
HALO = 8
EROWS, ECOLS = ROWS + 2 * HALO, COLS + 128
FPAD = 16
Q = 1.0 / 3.0
A2 = 0.5 * 14.0 / 9.0
B4 = 0.25 / 9.0
BREAKING = 0.05
VMEM_BYTES = 63 * 2**20
F32, BF16 = jnp.float32, jnp.bfloat16


def tridiagonal_inverse(length):
    band = np.eye(length) + Q * (np.eye(length, k=1) + np.eye(length, k=-1))
    return np.linalg.inv(band)


CORNER = float(tridiagonal_inverse(ROWS)[0, 0])
NEXT = (1.0 - CORNER) / Q
LINK = Q * CORNER
COUPLE = 1.0 / (1.0 - LINK * LINK)


def halves(matrix):
    matrix = matrix.astype(np.float32)
    high = matrix.astype(jnp.bfloat16)
    low = (matrix - high.astype(np.float32)).astype(jnp.bfloat16)
    return high, low


def split_bf16(value):
    high = value.astype(BF16)
    return high, (value - high.astype(F32)).astype(BF16)


def two_sum(a, b):
    s = a + b
    t = s - a
    return s, (a - (s - t)) + (b - t)


def quick_sum(a, b):
    s = a + b
    return s, b - (s - a)


def cut(a):
    t = 4097.0 * a
    high = t - (t - a)
    return high, a - high


def two_prod(a, b):
    p = a * b
    ah, al = cut(a)
    bh, bl = cut(b)
    return p, ((ah * bh - p) + ah * bl + al * bh) + al * bl


def dd_add(a, b):
    s, e = two_sum(a[0], b[0])
    t, f = two_sum(a[1], b[1])
    s, e = quick_sum(s, e + t)
    return quick_sum(s, e + f)


def dd_neg(a):
    return -a[0], -a[1]


def dd_mul(a, b):
    p, e = two_prod(a[0], b[0])
    return quick_sum(p, e + (a[0] * b[1] + a[1] * b[0]))


def dd_scale(a, b):
    p, e = two_prod(a[0], b)
    return quick_sum(p, e + a[1] * b)


def dd_half(a):
    return 0.5 * a[0], 0.5 * a[1]


def dd_div(a, b):
    first = a[0] / b[0]
    rest = dd_add(a, dd_neg(dd_scale(b, first)))
    return quick_sum(first, rest[0] / b[0])


def rolled(value, shift, axis):
    size = value.shape[axis]
    return pltpu.roll(value, shift % size, axis)


def iota(shape, axis):
    return lax.broadcasted_iota(jnp.int32, shape, axis)


def lane_source(field):
    return rolled(field, -1, 1) - field


def row_source(around):
    return (rolled(around, -1, 0) - around)[0:16]


def derivative_matrix(length):
    eye, shift = np.eye(length), functools.partial(np.eye, length)
    near = A2 * (eye + shift(k=-1))
    far = B4 * (shift(k=1) + eye + shift(k=-1) + shift(k=-2))
    inside = np.zeros((length, 1))
    inside[2:length - 2] = 1.0
    return tridiagonal_inverse(length) @ (inside * (near + far))


def edge_items(f):
    return A2 * f[1] + B4 * f[2], A2 * (f[2] - f[0]) + B4 * f[3]


def kernel(nz, na, ws, dc, on, ce, cd, xhl, yh, yl, exl, exr, ey, out,
           wv, dv, ov, cv, xhv, yhv, ylv, exlv, exrv, eyv,
           fld, dep, sxh, sxl, syh, syl, hx, hy, er, ec, stress, part, ratev, solv,
           rowmsg, rowgot, colmsg, colgot, bx, by, cext, cs, cright, cleft, fright, fleft, fmsg, tau, crec, acc,
           stmsg, stz, sta, dtmsg, dtz, dta, nsc,
           insem, outsem, ssem, rowsem, colsem, crowsem, ccolsem, ccorsem, frowsem, fcolsem, fcorsem,
           stzsem, stasem, dtzsem, dtasem):
    z, a = lax.axis_index("xs"), lax.axis_index("al")
    up, down = lax.rem(z + nz - 1, nz), lax.rem(z + 1, nz)
    left, right = lax.rem(a + na - 1, na), lax.rem(a + 1, na)
    has_up = (z > 0).astype(F32)
    has_down = (z < nz - 1).astype(F32)

    barrier = pltpu.get_barrier_semaphore()
    zpeers = [lax.rem(z + k, nz) for k in sorted(range(1, nz), key=lambda k: -min(k, nz - k))]
    apeers = [lax.rem(a + k, na) for k in range(1, na)]
    corners = [(up, left), (up, right), (down, left), (down, right)]
    greet = [(p, a) for p in zpeers] + [(z, p) for p in apeers] + corners
    loads = [pltpu.make_async_copy(s, d, insem.at[k]) for k, (s, d) in enumerate(
        [(ws, wv), (dc, dv), (on, ov), (ce, cv), (xhl, xhv), (yh, yhv), (yl, ylv), (exl, exlv), (exr, exrv), (ey, eyv)])]
    for load in loads:
        load.start()
    for who in greet:
        pl.semaphore_signal(barrier, inc=1, device_id=who, device_id_type=MESH)

    sends = []

    def send(src, dst, sem_index, recv, who):
        copy = pltpu.make_async_remote_copy(src_ref=src, dst_ref=dst, send_sem=ssem.at[sem_index], recv_sem=recv,
                                            device_id=who, device_id_type=MESH)
        copy.start()
        sends.append(copy)
        return copy

    for load in loads[:2]:
        load.wait()
    SUR, FX, FY, U, V, FXU, FXV, FYV = range(8)
    ACROSS = (SUR, FX, U, V, FXU, FXV)
    ALONG = (SUR, FY, U, V, FXV, FYV)

    def first(i, sums):
        rows = pl.ds(i * 16, 16)
        inner = pl.ds(i * 16 + FPAD, 16)
        kind = dv[rows, :]
        still = jnp.full((16, COLS), cd[0], F32)
        for k in range(1, CLASSES):
            still = jnp.where(kind == k, cd[k], still)
        surface, px, py = wv[0, rows, :], wv[1, rows, :], wv[2, rows, :]
        depth = still + surface
        u, v = px / depth, py / depth
        fields = [surface, px, py, u, v, px * u, px * v, py * v]
        for k, f in enumerate(fields):
            fld[k, inner, :] = f
        dep[rows, :] = depth
        c = depth * depth * (1.0 / 3.0)
        cext[pl.ds(i * 16 + HALO, 16), 0:COLS] = c
        for k, f in enumerate(ALONG):
            high, low = split_bf16(lane_source(fields[f]))
            syh[k, rows, :] = high
            syl[k, rows, :] = low
        energy = surface * surface + px * px + py * py
        return sums[0] + c * energy, sums[1] + energy

    nil = jnp.zeros((16, COLS), F32)
    stat = nil, nil
    for i in range(ROWS // 16):
        stat = first(i, stat)

    def across_sources(ref, which):
        for k, f in enumerate(which):
            for i in range(ROWS // 16):
                around = ref[f, i * 16 + FPAD:i * 16 + FPAD + 24, :]
                high, low = split_bf16(row_source(around))
                sxh[k, i * 16:i * 16 + 16, :] = high
                sxl[k, i * 16:i * 16 + 16, :] = low

    def solves(count):
        dot = functools.partial(jnp.dot, preferred_element_type=F32)
        high = syh[0:count].reshape(count * ROWS, COLS)
        low = syl[0:count].reshape(count * ROWS, COLS)
        solved = dot(high, yhv[...]) + (dot(low, yhv[...]) + dot(high, ylv[...]))
        hy[0:count] = solved.reshape(count, ROWS, COLS)
        for k in range(count):
            both = dot(xhv[...], sxh[k])
            hx[k] = both[0:ROWS] + (both[ROWS:] + dot(xhv[0:ROWS, :], sxl[k]))

    lane128 = iota((ROWS, 128), 1)

    def edges_out(ref, across, along, stage):
        for k, f in enumerate(across):
            for j in range(4):
                er[j, k:k + 1, :] = ref[f, FPAD + j:FPAD + j + 1, :]
                er[4 + j, k:k + 1, :] = ref[f, FPAD + ROWS - 1 - j:FPAD + ROWS - j, :]
            er[8, k:k + 1, :] = hx[k, 0:1, :]
            er[9, k:k + 1, :] = hx[k, ROWS - 1:ROWS, :]
        for k, f in enumerate(along):
            fl = ref[f, FPAD:FPAD + ROWS, 0:128]
            fr = ref[f, FPAD:FPAD + ROWS, COLS - 128:COLS]
            tile = jnp.where(lane128 < 32, fl, jnp.where(lane128 < 64, rolled(hy[k, :, 0:128], 32, 1), jnp.where(
                lane128 < 96, rolled(hy[k, :, COLS - 128:COLS], -32, 1), fr)))
            turned = tile.T
            for j in range(4):
                ec[j, k:k + 1, :] = turned[j:j + 1, :]
                ec[4 + j, k:k + 1, :] = turned[127 - j:128 - j, :]
            ec[8, k:k + 1, :] = turned[32:33, :]
            ec[9, k:k + 1, :] = turned[95:96, :]
        for e, msg in ((er, rowmsg), (ec, colmsg)):
            s0, s1 = edge_items([e[j] for j in range(4)])
            msg[stage, 0, 0] = e[0]
            msg[stage, 0, 1] = e[1]
            msg[stage, 0, 2] = e[8] + CORNER * s0 + NEXT * s1
            t0, t1 = edge_items([e[4 + j] for j in range(4)])
            msg[stage, 1, 0] = e[4]
            msg[stage, 1, 1] = e[5]
            msg[stage, 1, 2] = e[9] - CORNER * t0 - NEXT * t1

    def edges_send(stage):
        base = 4 * stage
        return [
            send(rowmsg.at[stage, 0], rowgot.at[stage, 1], base, rowsem.at[stage, 1], (up, a)),
            send(rowmsg.at[stage, 1], rowgot.at[stage, 0], base + 1, rowsem.at[stage, 0], (down, a)),
            send(colmsg.at[stage, 0], colgot.at[stage, 1], base + 2, colsem.at[stage, 1], (z, left)),
            send(colmsg.at[stage, 1], colgot.at[stage, 0], base + 3, colsem.at[stage, 0], (z, right)),
        ]

    def closing(e, got, keep_low, keep_high):
        f0, f1 = e[0], e[1]
        p1, p2, ph = got[0, 0] * keep_low, got[0, 1] * keep_low, got[0, 2]
        s0, s1 = edge_items([e[j] for j in range(4)])
        s0 = s0 - A2 * p1 - B4 * p2
        s1 = s1 - B4 * p1
        own = e[8] + CORNER * s0 + NEXT * s1
        theirs = ph + CORNER * (A2 * f0 + B4 * f1) + NEXT * (B4 * f0)
        gp = (theirs - LINK * own) * COUPLE * keep_low
        low, low_end = s0 - s1 * (1.0 / Q) - Q * gp, s1 * (1.0 / Q)
        l0, l1 = e[4], e[5]
        n1, n2, nh = got[1, 0] * keep_high, got[1, 1] * keep_high, got[1, 2]
        t0, t1 = edge_items([e[4 + j] for j in range(4)])
        t0 = A2 * n1 + B4 * n2 - t0
        t1 = B4 * n1 - t1
        own = e[9] + CORNER * t0 + NEXT * t1
        theirs = nh - CORNER * (A2 * l0 + B4 * l1) - NEXT * (B4 * l0)
        gn = (theirs - LINK * own) * COUPLE * keep_high
        return low, t0 - t1 * (1.0 / Q) - Q * gn, low_end, t1 * (1.0 / Q)

    def close_across(count, stage):
        low, high, low_end, high_end = closing(er, rowgot.at[stage], has_up, has_down)
        for k in range(count):
            hx[k, 0:1, :] = hx[k, 0:1, :] + low_end[k:k + 1, :]
            hx[k, ROWS - 1:ROWS, :] = hx[k, ROWS - 1:ROWS, :] + high_end[k:k + 1, :]
        return low, high

    def close_along(count, stage):
        terms = closing(ec, colgot.at[stage], 1.0, 1.0)
        block = jnp.concatenate(list(terms) + [jnp.zeros((96, 128), F32)], axis=0)
        turned = block.T
        for k in range(count):
            col = [jnp.broadcast_to(turned[:, 8 * j + k:8 * j + k + 1], (ROWS, 128)) for j in range(4)]
            hy[k, :, 0:128] = hy[k, :, 0:128] + col[0] * eyv[0:1, :] + jnp.where(lane128 == 0, col[2], 0.0)
            hy[k, :, COLS - 128:COLS] = (hy[k, :, COLS - 128:COLS] + col[1] * eyv[1:2, :]
                                         + jnp.where(lane128 == 127, col[3], 0.0))

    across_sources(fld, ACROSS)
    for load in loads[4:]:
        load.wait()
    solves(6)
    edges_out(fld, ACROSS, ALONG, 0)

    stat_c, stat_e = [t[0:8] + t[8:16] for t in stat]
    stat_c, stat_e = [sum(t[:, 128 * j:128 * (j + 1)] for j in range(4)) for t in (stat_c, stat_e)]
    sub8, lane8 = iota((8, 128), 0), iota((8, 128), 1)
    mixed = jnp.where(sub8 < 4, stat_c + rolled(stat_c, 4, 0), stat_e + rolled(stat_e, 4, 0))
    for s in (64, 32, 16, 8, 4, 2, 1):
        mixed = mixed + rolled(mixed, s, 1)
    mixed = mixed + jnp.where(sub8 % 4 < 2, rolled(mixed, -2, 0), rolled(mixed, 2, 0))
    mixed = mixed + jnp.where(sub8 % 2 < 1, rolled(mixed, -1, 0), rolled(mixed, 1, 0))
    stmsg[0] = mixed

    pl.semaphore_wait(barrier, len(greet))

    first_edges = edges_send(0)

    def spread(msg, slots, sem, peers, me, place):
        for p in peers:
            pltpu.make_async_remote_copy(src_ref=msg, dst_ref=slots.at[me], send_sem=sem.at[0], recv_sem=sem.at[1],
                                         device_id=place(p), device_id_type=MESH).start()
        slots[me] = msg[...]

    def spread_z(msg, slots, sem):
        spread(msg, slots, sem, zpeers, z, lambda p: (p, a))

    def spread_a(msg, slots, sem):
        spread(msg, slots, sem, apeers, a, lambda p: (z, p))

    def all_of(slots, sem, count):
        most = slots.at[pl.ds(0, count)]
        return pltpu.make_async_remote_copy(src_ref=most, dst_ref=most, send_sem=sem.at[0], recv_sem=sem.at[1],
                                            device_id=(z, right), device_id_type=MESH)

    spread_z(stmsg.at[0], stz, stzsem)

    top, bottom = pl.ds(0, HALO), pl.ds(EROWS - HALO, HALO)
    inner = pl.ds(HALO, ROWS)
    first_rows, last_rows = pl.ds(HALO, HALO), pl.ds(ROWS, HALO)
    low_cols, high_cols = pl.ds(0, 128), pl.ds(COLS - 128, 128)
    whole_cols = pl.ds(0, COLS)
    c_copies = [
        send(cext.at[first_rows, whole_cols], cext.at[bottom, whole_cols], 8, crowsem.at[1], (up, a)),
        send(cext.at[last_rows, whole_cols], cext.at[top, whole_cols], 9, crowsem.at[0], (down, a)),
        send(cext.at[inner, low_cols], cright.at[inner, :], 10, ccolsem.at[1], (z, left)),
        send(cext.at[inner, high_cols], cleft.at[inner, :], 11, ccolsem.at[0], (z, right)),
        send(cext.at[first_rows, low_cols], cright.at[bottom, :], 12, ccorsem.at[0], (up, left)),
        send(cext.at[first_rows, high_cols], cleft.at[bottom, :], 13, ccorsem.at[1], (up, right)),
        send(cext.at[last_rows, low_cols], cright.at[top, :], 14, ccorsem.at[2], (down, left)),
        send(cext.at[last_rows, high_cols], cleft.at[top, :], 15, ccorsem.at[3], (down, right)),
    ]

    for copy in first_edges:
        copy.wait_recv()
    xlow, xhigh = close_across(6, 0)
    close_along(6, 0)
    for load in loads[2:4]:
        load.wait()

    def wide(tile):
        return jnp.concatenate([tile] * 4, axis=1)

    er[0] = xlow
    er[1] = xhigh

    def second(i):
        rows = pl.ds(i * 16, 16)
        inner16 = pl.ds(i * 16 + FPAD, 16)
        wl, wr = wide(exlv[rows, :]), wide(exrv[rows, :])
        gx = [hx[k, rows, :] + (wl * er[0, k:k + 1, :] + wr * er[1, k:k + 1, :]) for k in range(6)]
        gy = [hy[k, rows, :] for k in range(6)]
        depth = dep[rows, :]
        rate = -(gx[1] + gy[1])
        active = (ov[rows, :] * (1 - cv[rows, :])).astype(F32)
        weight = BREAKING * active * depth * jnp.abs(rate) * depth
        sxx = 2.0 * weight * gx[2]
        sxy = weight * (gy[2] + gx[3])
        syy = 2.0 * weight * gy[3]
        ratev[rows, :] = -rate
        stress[0, inner16, :] = sxx
        stress[1, inner16, :] = sxy
        stress[2, inner16, :] = syy
        part[0, rows, :] = -gx[4] - gy[4] - depth * gx[0]
        part[1, rows, :] = -gx[5] - gy[5] - depth * gy[0]
        for k, f in enumerate((sxy, syy)):
            high, low = split_bf16(lane_source(f))
            syh[k, rows, :] = high
            syl[k, rows, :] = low

    for i in range(ROWS // 16):
        second(i)
    rate_out = pltpu.make_async_copy(ratev, out.at[0], outsem.at[0])
    rate_out.start()
    across_sources(stress, (0, 1))
    solves(2)
    edges_out(stress, (0, 1), (1, 2), 1)
    second_edges = edges_send(1)

    all_of(stz, stzsem, nz - 1).wait_recv()
    stmsg[1] = functools.reduce(lambda s, k: s + stz[k], range(1, nz), stz[0])
    spread_a(stmsg.at[1], sta, stasem)

    for copy in second_edges:
        copy.wait_recv()
    xlow, xhigh = close_across(2, 1)
    close_along(2, 1)
    er[0] = xlow
    er[1] = xhigh

    def third(i):
        rows = pl.ds(i * 16, 16)
        ext = pl.ds(i * 16 + HALO, 16)
        wl, wr = wide(exlv[rows, :]), wide(exrv[rows, :])
        gx = [hx[k, rows, :] + (wl * er[0, k:k + 1, :] + wr * er[1, k:k + 1, :]) for k in range(2)]
        fx = part[0, rows, :] + gx[0] + hy[0, rows, :]
        fy = part[1, rows, :] + gx[1] + hy[1, rows, :]
        bx[ext, 0:COLS] = fx
        by[ext, 0:COLS] = fy
        lane = iota((16, 128), 1)
        fmsg[0, rows, :] = jnp.where(lane < 64, fx[:, 0:128], rolled(fy[:, 0:128], 64, 1))
        fmsg[1, rows, :] = jnp.where(lane < 64, rolled(fy[:, COLS - 128:], 64, 1), fx[:, COLS - 128:])

    for i in range(ROWS // 16):
        third(i)
    lo8, hi8 = pl.ds(0, HALO), pl.ds(ROWS - HALO, HALO)
    f_copies = [
        send(bx.at[first_rows, whole_cols], bx.at[bottom, whole_cols], 16, frowsem.at[0], (up, a)),
        send(bx.at[last_rows, whole_cols], bx.at[top, whole_cols], 17, frowsem.at[1], (down, a)),
        send(by.at[first_rows, whole_cols], by.at[bottom, whole_cols], 18, frowsem.at[2], (up, a)),
        send(by.at[last_rows, whole_cols], by.at[top, whole_cols], 19, frowsem.at[3], (down, a)),
        send(fmsg.at[0], fright.at[inner, :], 20, fcolsem.at[1], (z, left)),
        send(fmsg.at[1], fleft.at[inner, :], 21, fcolsem.at[0], (z, right)),
        send(fmsg.at[0, lo8, :], fright.at[bottom, :], 22, fcorsem.at[0], (up, left)),
        send(fmsg.at[1, lo8, :], fleft.at[bottom, :], 23, fcorsem.at[1], (up, right)),
        send(fmsg.at[0, hi8, :], fright.at[top, :], 24, fcorsem.at[2], (down, left)),
        send(fmsg.at[1, hi8, :], fleft.at[top, :], 25, fcorsem.at[3], (down, right)),
    ]

    all_of(sta, stasem, na - 1).wait_recv()
    total = functools.reduce(lambda s, k: s + sta[k], range(1, na), sta[0])
    weight_c = jnp.broadcast_to(total[0:1, 0:1], (8, 128))
    weight_e = jnp.broadcast_to(total[4:5, 0:1], (8, 128))
    top_value = jnp.where(weight_e > 0.0, 10.0 * weight_c / weight_e, 100.0)
    half_top = 0.5 * top_value
    shrink = 1.0 / half_top
    for copy in c_copies:
        copy.wait_recv()

    def wide5(tile):
        return jnp.concatenate([tile] * 5, axis=1)

    sub = iota((8, ECOLS), 0)
    lanes = iota((8, 128), 1)
    shrink5 = wide5(shrink)

    def scaled_c(i, _):
        rows = pl.ds(pl.multiple_of(i * 8, 8), 8)
        side = jnp.where(lanes < 64, cright[rows, :], cleft[rows, :])
        c = jnp.concatenate([cext[rows, 0:COLS], side], axis=1) * shrink5
        c = c * jnp.where(i == 0, has_up, jnp.where(i == EROWS // 8 - 1, has_down, 1.0))
        cs[rows, :] = c
        crec[rows, :] = 1.0 / c
        return 0

    lax.fori_loop(0, EROWS // 8, scaled_c, 0)
    for copy in f_copies:
        copy.wait_recv()

    def sides(i, _):
        rows = pl.ds(pl.multiple_of(i * 8, 8), 8)
        from_right, from_left = fright[rows, :], fleft[rows, :]
        bx[rows, COLS:ECOLS] = jnp.where(lanes < 64, from_right, from_left)
        by[rows, COLS:ECOLS] = jnp.where(lanes < 64, rolled(from_right, 64, 1), rolled(from_left, 64, 1))
        return 0

    lax.fori_loop(0, EROWS // 8, sides, 0)
    bx[bottom, :] = bx[bottom, :] * has_down

    def tile_at(ref, i):
        return ref[8 * i:8 * i + 8, :]

    def below_of(x, nxt):
        return jnp.where(sub == 7, rolled(nxt, -1, 0), rolled(x, -1, 0))

    def above_of(x, prv):
        return jnp.where(sub == 0, rolled(prv, 1, 0), rolled(x, 1, 0))

    TILES = EROWS // 8

    def inside(t):
        return t[:, 0:COLS]

    nil8 = jnp.zeros((8, COLS), F32)
    norm, sums = nil8, nil8
    wx = tile_at(bx, 0)
    for i in range(TILES):
        nxt = tile_at(bx, min(i + 1, TILES - 1))
        wy = tile_at(by, i)
        t = tile_at(cs, i) * ((below_of(wx, nxt) - wx) + (rolled(wy, -1, 1) - wy))
        tau[0, 8 * i:8 * i + 8, :] = t
        if 0 < i < TILES - 1:
            norm = norm + (inside(wx) * inside(wx) + inside(wy) * inside(wy))
            sums = sums + inside(t) * (inside(t) * inside(tile_at(crec, i)))
        wx = nxt
    acc[0] = sums
    acc[15] = norm
    last_diag = jnp.where((sub == 7) & (z == nz - 1), 3.0, 4.0)

    def sweep(k, start):
        cross_sum, square_sum = nil8, nil8
        first_tile, stop = (1, TILES - 1) if start == 2 else (0, TILES)
        prv = tau[k, 8 * max(first_tile - 1, 0):8 * max(first_tile - 1, 0) + 8, :]
        x = tau[k, 8 * first_tile:8 * first_tile + 8, :]
        for i in range(first_tile, stop):
            j = min(i + 1, TILES - 1)
            nxt = tau[k, 8 * j:8 * j + 8, :]
            around = (above_of(x, prv) + below_of(x, nxt)) + (rolled(x, -1, 1) + rolled(x, 1, 1))
            diag = last_diag if i == TILES - 2 else 4.0
            t = tile_at(cs, i) * (diag * x - around) - x
            if start > 0:
                t = 2.0 * t - tau[k - 1, 8 * i:8 * i + 8, :]
            tau[k + 1, 8 * i:8 * i + 8, :] = t
            if 0 < i < TILES - 1:
                q = inside(t) * inside(tile_at(crec, i))
                cross_sum = cross_sum + inside(x) * q
                square_sum = square_sum + inside(t) * q
            prv, x = x, nxt
        acc[2 * k + 1] = cross_sum
        acc[2 * k + 2] = square_sum

    sweep(0, 0)

    def sweeps(k, _):
        sweep(k, 1)
        return 0

    lax.fori_loop(1, ITERS - 2, sweeps, 0)
    sweep(ITERS - 2, 2)
    dots = [acc[k] for k in range(16)]

    def fold(t):
        s0 = dd_add(two_sum(t[:, 0:128], t[:, 128:256]), two_sum(t[:, 256:384], t[:, 384:512]))
        return s0

    level = [fold(t) for t in dots]
    for width, span in ((8, 4), (4, 2), (2, 1)):
        mask = sub8 % (2 * span) < span

        def merge(p, q, mask=mask, span=span):
            def parts(g, h):
                w = jnp.where(mask, h, g)
                return jnp.where(mask, g, h), jnp.where(mask, rolled(w, -span, 0), rolled(w, span, 0))
            xh_, yh_ = parts(p[0], q[0])
            xl_, yl_ = parts(p[1], q[1])
            return dd_add((xh_, xl_), (yh_, yl_))

        level = [merge(level[i], level[i + width]) for i in range(width)]
    for s in (64, 32, 16, 8, 4, 2, 1):
        level = [dd_add(p, (rolled(p[0], s, 1), rolled(p[1], s, 1))) for p in level]
    even, odd = level

    dtmsg[0] = jnp.where(lane8 < 32, even[0], jnp.where(lane8 < 64, odd[0], jnp.where(lane8 < 96, even[1], odd[1])))
    spread_z(dtmsg.at[0], dtz, dtzsem)
    all_of(dtz, dtzsem, nz - 1).wait_recv()

    def gathered(slots, count):
        level = [(slots[k], rolled(slots[k], 64, 1)) for k in range(count)]
        while len(level) > 1:
            level = [dd_add(level[2 * i], level[2 * i + 1]) for i in range(len(level) // 2)]
        return level[0]

    sums = gathered(dtz, nz)
    dtmsg[1] = jnp.where(lane8 < 64, sums[0], rolled(sums[1], 64, 1))
    spread_a(dtmsg.at[1], dta, dtasem)
    all_of(dta, dtasem, na - 1).wait_recv()
    sums = gathered(dta, na)

    def pick(value, lane):
        return jnp.broadcast_to(value[:, lane:lane + 1], (8, 128))

    def row_of(value, r):
        return tuple(jnp.broadcast_to(part_[r:r + 1, :], (8, 128)) for part_ in value)

    even = pick(sums[0], 0), pick(sums[1], 0)
    odd = pick(sums[0], 32), pick(sums[1], 32)
    square = row_of(odd, 7)
    even = dd_add((2.0 * even[0], 2.0 * even[1]), dd_neg(row_of(even, 0)))
    odd = dd_add((2.0 * odd[0], 2.0 * odd[1]), dd_neg(row_of(odd, 0)))

    MOM, SEC, GRAM, MIX = range(4)
    nsc[...] = jnp.zeros(nsc.shape, F32)
    for part_ in range(2):
        for j in range(15):
            value = (even, odd)[j % 2][part_][j // 2:j // 2 + 1, :]
            nsc[MOM, part_, 8 + j:9 + j, :] = value
            if j == 1:
                nsc[MOM, part_, 7:8, :] = value

    def entries(which, start, count=8):
        return nsc[which, 0, start:start + count, :], nsc[which, 1, start:start + count, :]

    def widened(which, start):
        return dd_add(entries(which, start), dd_half(dd_add(entries(which, start + 1), entries(which, start - 1))))

    for start in (8, 16):
        value = widened(MOM, start)
        nsc[SEC, 0, start:start + 8, :], nsc[SEC, 1, start:start + 8, :] = value
        mix = dd_add(entries(MOM, start), dd_scale(value, half_top))
        nsc[MIX, 0, start:start + 8, :], nsc[MIX, 1, start:start + 8, :] = mix
    for part_ in range(2):
        nsc[SEC, part_, 7:8, :] = nsc[SEC, part_, 9:10, :]
    for start in (8, 16):
        value = dd_add(entries(SEC, start), dd_scale(widened(SEC, start), half_top))
        nsc[GRAM, 0, start:start + 8, :], nsc[GRAM, 1, start:start + 8, :] = value
    for part_ in range(2):
        for j in range(1, 8):
            nsc[GRAM, part_, 8 - j:9 - j, :] = nsc[GRAM, part_, 8 + j:9 + j, :]

    def with_first(value, head):
        return tuple(jnp.where(sub8 == 0, h, v) for v, h in zip(value, head))

    moment0 = row_of(entries(MOM, 8), 0)
    matrix = [with_first(entries(MIX, 7), dd_add(square, dd_scale(moment0, half_top)))]
    for l in range(ITERS - 1):
        column = dd_half(dd_add(entries(GRAM, 7 + l), entries(GRAM, 7 - l)))
        matrix.append(with_first(column, row_of(entries(MIX, 8 + l), 0)))
    right_side = with_first(entries(MOM, 7), square)
    diagonal = jnp.zeros((8, 128), F32)
    first_diagonal = [row_of(matrix[k], k)[0] for k in range(ITERS)]
    for k in range(ITERS):
        pivot = row_of(matrix[k], k)
        usable = pivot[0] > 1e-11 * first_diagonal[k]
        safe = jnp.where(usable, pivot[0], 1.0), jnp.where(usable, pivot[1], 0.0)
        factor = dd_div(matrix[k], safe)
        skip = (sub8 == k) | jnp.logical_not(usable)
        factor = tuple(jnp.where(skip, 0.0, f) for f in factor)
        diagonal = jnp.where((sub8 == k) & usable, pivot[0], diagonal)
        for l in range(k + 1, ITERS):
            matrix[l] = dd_add(matrix[l], dd_neg(dd_mul(factor, row_of(matrix[l], k))))
        right_side = dd_add(right_side, dd_neg(dd_mul(factor, row_of(right_side, k))))
    answer = jnp.where(diagonal > 0.0, right_side[0] / jnp.where(diagonal > 0.0, diagonal, 1.0), 0.0)
    nsc[MOM, 0, 0:8, :] = answer

    weights = [jnp.broadcast_to(nsc[MOM, 0, k:k + 1, :], (8, 128)) for k in range(ITERS)]

    def combined(j, w):
        return functools.reduce(lambda s, t: s + t, [w[l + 1] * tau[l, 8 * j:8 * j + 8, :] for l in range(ITERS - 1)])

    w5 = [wide5(w) for w in weights]
    gain = wide(weights[0])
    prv = combined(0, w5)
    for i in range(ROWS // 8):
        here = combined(i + 1, w5)
        solv[0, 8 * i:8 * i + 8, :] = inside(here - above_of(here, prv)) - gain * inside(tile_at(bx, i + 1))
        solv[1, 8 * i:8 * i + 8, :] = inside(here - rolled(here, 1, 1)) - gain * inside(tile_at(by, i + 1))
        prv = here
    solved_out = pltpu.make_async_copy(solv, out.at[pl.ds(1, 2)], outsem.at[1])
    solved_out.start()
    for copy in sends + [all_of(stz, stzsem, nz - 1), all_of(sta, stasem, na - 1), all_of(dtz, dtzsem, nz - 1), all_of(dta, dtasem, na - 1)]:
        copy.wait_send()
    rate_out.wait()
    solved_out.wait()


def per_device(nz, na, wave_state, depth_class, onset_flag, cessation, class_depth):
    across, along = tridiagonal_inverse(ROWS), tridiagonal_inverse(COLS)
    xhl = np.concatenate(halves(derivative_matrix(ROWS)), axis=0)
    yh, yl = halves(derivative_matrix(COLS).T)
    exl = np.repeat(across[:, :1], 128, axis=1).astype(np.float32)
    exr = np.repeat(across[:, -1:], 128, axis=1).astype(np.float32)
    ey = np.zeros((8, 128), np.float32)
    ey[0] = along[0, :128]
    ey[1] = along[-1, -128:]
    consts = [jnp.asarray(t) for t in (xhl, yh, yl, exl, exr, ey)]
    dma = pltpu.SemaphoreType.DMA

    def vm(*shape, dtype=F32):
        return pltpu.VMEM(shape, dtype)

    scratch = [
        vm(3, ROWS, COLS), vm(ROWS, COLS, dtype=jnp.int32), vm(ROWS, COLS, dtype=jnp.int32), vm(ROWS, COLS, dtype=jnp.int32),
        vm(2 * ROWS, ROWS, dtype=BF16), vm(COLS, COLS, dtype=BF16), vm(COLS, COLS, dtype=BF16),
        vm(ROWS, 128), vm(ROWS, 128), vm(8, 128),
        vm(8, ROWS + 2 * FPAD, COLS), vm(ROWS, COLS),
        vm(6, ROWS, COLS, dtype=BF16), vm(6, ROWS, COLS, dtype=BF16), vm(6, ROWS, COLS, dtype=BF16), vm(6, ROWS, COLS, dtype=BF16),
        vm(6, ROWS, COLS), vm(6, ROWS, COLS), vm(10, 8, COLS), vm(10, 8, 128),
        vm(3, ROWS + 2 * FPAD, COLS), vm(2, ROWS, COLS), vm(ROWS, COLS), vm(2, ROWS, COLS),
        vm(2, 2, 3, 8, COLS), vm(2, 2, 3, 8, COLS), vm(2, 2, 3, 8, 128), vm(2, 2, 3, 8, 128),
        vm(EROWS, ECOLS), vm(EROWS, ECOLS), vm(EROWS, ECOLS), vm(EROWS, ECOLS),
        vm(EROWS, 128), vm(EROWS, 128), vm(EROWS, 128), vm(EROWS, 128), vm(2, ROWS, 128),
        vm(ITERS, EROWS, ECOLS), vm(EROWS, ECOLS), vm(16, 8, COLS),
        vm(2, 8, 128), vm(nz, 8, 128), vm(na, 8, 128), vm(2, 8, 128), vm(nz, 8, 128), vm(na, 8, 128), vm(4, 2, 32, 128),
        dma((10,)), dma((2,)), dma((26,)), dma((2, 2)), dma((2, 2)), dma((2,)), dma((2,)), dma((4,)), dma((4,)), dma((2,)), dma((4,)),
        dma((2,)), dma((2,)), dma((2,)), dma((2,)),
    ]
    anywhere = pl.BlockSpec(memory_space=pl.ANY)
    negated = pl.pallas_call(
        functools.partial(kernel, nz, na),
        out_shape=jax.ShapeDtypeStruct((3, ROWS, COLS), F32),
        in_specs=[anywhere] * 4 + [pl.BlockSpec(memory_space=pltpu.SMEM)] + [anywhere] * 6,
        out_specs=anywhere,
        scratch_shapes=scratch,
        compiler_params=pltpu.CompilerParams(collective_id=0, has_side_effects=True, vmem_limit_bytes=VMEM_BYTES),
    )(wave_state, depth_class, onset_flag, cessation, class_depth, *consts)
    return -negated


def solution(mesh):
    sizes = dict(mesh.shape)
    in_specs = (P(None, "xs", "al"), P("xs", "al"), P("xs", "al"), P("xs", "al"), P())
    return jax.shard_map(
        functools.partial(per_device, sizes["xs"], sizes["al"]),
        mesh=mesh, in_specs=in_specs, out_specs=P(None, "xs", "al"), check_vma=False,
    )
```

```python
import functools

import jax
import jax.numpy as jnp
import numpy as np
from jax import lax
from jax.experimental import pallas as pl
from jax.experimental.pallas import tpu as pltpu
from jax.sharding import PartitionSpec as P

MESH = pl.DeviceIdType.MESH
CLASSES = 8
ITERS = 8
ROWS, COLS = 128, 512
HALO = 8
EROWS, ECOLS = ROWS + 2 * HALO, COLS + 128
FPAD = 16
Q = 1.0 / 3.0
A2 = 0.5 * 14.0 / 9.0
B4 = 0.25 / 9.0
BREAKING = 0.05
VMEM_BYTES = 63 * 2**20
F32, BF16 = jnp.float32, jnp.bfloat16


def tridiagonal_inverse(length):
    band = np.eye(length) + Q * (np.eye(length, k=1) + np.eye(length, k=-1))
    return np.linalg.inv(band)


CORNER = float(tridiagonal_inverse(ROWS)[0, 0])
NEXT = (1.0 - CORNER) / Q
LINK = Q * CORNER
COUPLE = 1.0 / (1.0 - LINK * LINK)


def halves(matrix):
    matrix = matrix.astype(np.float32)
    high = matrix.astype(jnp.bfloat16)
    low = (matrix - high.astype(np.float32)).astype(jnp.bfloat16)
    return high, low


def split_bf16(value):
    high = value.astype(BF16)
    return high, (value - high.astype(F32)).astype(BF16)


def two_sum(a, b):
    s = a + b
    t = s - a
    return s, (a - (s - t)) + (b - t)


def quick_sum(a, b):
    s = a + b
    return s, b - (s - a)


def cut(a):
    t = 4097.0 * a
    high = t - (t - a)
    return high, a - high


def two_prod(a, b):
    p = a * b
    ah, al = cut(a)
    bh, bl = cut(b)
    return p, ((ah * bh - p) + ah * bl + al * bh) + al * bl


def dd_add(a, b):
    s, e = two_sum(a[0], b[0])
    t, f = two_sum(a[1], b[1])
    s, e = quick_sum(s, e + t)
    return quick_sum(s, e + f)


def dd_neg(a):
    return -a[0], -a[1]


def dd_mul(a, b):
    p, e = two_prod(a[0], b[0])
    return quick_sum(p, e + (a[0] * b[1] + a[1] * b[0]))


def dd_scale(a, b):
    p, e = two_prod(a[0], b)
    return quick_sum(p, e + a[1] * b)


def dd_half(a):
    return 0.5 * a[0], 0.5 * a[1]


def dd_div(a, b):
    inverse = 1.0 / b[0]
    first = a[0] * inverse
    rest = dd_add(a, dd_neg(dd_scale(b, first)))
    return quick_sum(first, rest[0] * inverse)


def rolled(value, shift, axis):
    size = value.shape[axis]
    return pltpu.roll(value, shift % size, axis)


def iota(shape, axis):
    return lax.broadcasted_iota(jnp.int32, shape, axis)


def lane_source(field):
    return rolled(field, -1, 1) - field


def row_source(around):
    return (rolled(around, -1, 0) - around)[0:16]


def derivative_matrix(length):
    eye, shift = np.eye(length), functools.partial(np.eye, length)
    near = A2 * (eye + shift(k=-1))
    far = B4 * (shift(k=1) + eye + shift(k=-1) + shift(k=-2))
    inside = np.zeros((length, 1))
    inside[2:length - 2] = 1.0
    return tridiagonal_inverse(length) @ (inside * (near + far))


def edge_items(f):
    return A2 * f[1] + B4 * f[2], A2 * (f[2] - f[0]) + B4 * f[3]


def kernel(nz, na, ws, dc, on, ce, cd, xhl, yh, yl, exl, exr, ey, out,
           wv, dv, ov, cv, xhv, yhv, ylv, exlv, exrv, eyv,
           fld, dep, sxh, sxl, syh, syl, hx, hy, er, ec, stress, part, ratev, solv,
           rowmsg, rowgot, colmsg, colgot, rown, roth, rst, cown, coth, cst, bx2, by2, bx, by, cext, cs, cright, cleft, fright, fleft, fmsg, tau, crec, acc,
           stmsg, stz, sta, dtmsg, dtz, dta, nsc,
           insem, outsem, ssem, rowsem, colsem, crowsem, ccolsem, ccorsem, msem,
           stzsem, stasem, dtzsem, dtasem):
    z, a = lax.axis_index("xs"), lax.axis_index("al")
    up, down = lax.rem(z + nz - 1, nz), lax.rem(z + 1, nz)
    left, right = lax.rem(a + na - 1, na), lax.rem(a + 1, na)
    has_up = (z > 0).astype(F32)
    has_down = (z < nz - 1).astype(F32)

    barrier = pltpu.get_barrier_semaphore()
    zpeers = [lax.rem(z + k, nz) for k in sorted(range(1, nz), key=lambda k: -min(k, nz - k))]
    px, py, core = a // 8, (a % 8) // 2, a % 2
    steps = sorted([(i, j, k) for i in range(4) for j in range(4) for k in range(2)][1:],
                   key=lambda t: -(min(t[0], 4 - t[0]) + min(t[1], 4 - t[1])))
    apeers = [lax.rem(px + i, 4) * 8 + lax.rem(py + j, 4) * 2 + (core + k - 2 * core * k) for i, j, k in steps]
    corners = [(up, left), (up, right), (down, left), (down, right)]
    greet = [(p, a) for p in zpeers] + [(z, p) for p in apeers] + corners
    loads = [pltpu.make_async_copy(s, d, insem.at[k]) for k, (s, d) in enumerate(
        [(ws, wv), (dc, dv), (on, ov), (ce, cv), (xhl, xhv), (yh, yhv), (yl, ylv), (exl, exlv), (exr, exrv), (ey, eyv)])]
    for load in loads:
        load.start()
    for who in greet:
        pl.semaphore_signal(barrier, inc=1, device_id=who, device_id_type=MESH)

    sends = []

    def send(src, dst, sem_index, recv, who):
        copy = pltpu.make_async_remote_copy(src_ref=src, dst_ref=dst, send_sem=ssem.at[sem_index], recv_sem=recv,
                                            device_id=who, device_id_type=MESH)
        copy.start()
        sends.append(copy)
        return copy

    for load in loads[:2]:
        load.wait()
    SUR, FX, FY, U, V, FXU, FXV, FYV = range(8)
    ACROSS = (SUR, FX, U, V, FXU, FXV)
    ALONG = (SUR, FY, U, V, FXV, FYV)

    def first(i, sums):
        rows = pl.ds(i * 16, 16)
        inner = pl.ds(i * 16 + FPAD, 16)
        kind = dv[rows, :]
        still = jnp.full((16, COLS), cd[0], F32)
        for k in range(1, CLASSES):
            still = jnp.where(kind == k, cd[k], still)
        surface, px, py = wv[0, rows, :], wv[1, rows, :], wv[2, rows, :]
        depth = still + surface
        u, v = px / depth, py / depth
        fields = [surface, px, py, u, v, px * u, px * v, py * v]
        for k, f in enumerate(fields):
            fld[k, inner, :] = f
        dep[rows, :] = depth
        c = depth * depth * (1.0 / 3.0)
        cext[pl.ds(i * 16 + HALO, 16), 0:COLS] = c
        for k, f in enumerate(ALONG):
            high, low = split_bf16(lane_source(fields[f]))
            syh[k, rows, :] = high
            syl[k, rows, :] = low
        energy = surface * surface + px * px + py * py
        return sums[0] + c * energy, sums[1] + energy

    nil = jnp.zeros((16, COLS), F32)
    stat = nil, nil
    for i in range(ROWS // 16):
        stat = first(i, stat)

    def across_sources(ref, which):
        for k, f in enumerate(which):
            for i in range(ROWS // 16):
                around = ref[f, i * 16 + FPAD:i * 16 + FPAD + 24, :]
                high, low = split_bf16(row_source(around))
                sxh[k, i * 16:i * 16 + 16, :] = high
                sxl[k, i * 16:i * 16 + 16, :] = low

    def solves(count):
        dot = functools.partial(jnp.dot, preferred_element_type=F32)
        high = syh[0:count].reshape(count * ROWS, COLS)
        low = syl[0:count].reshape(count * ROWS, COLS)
        solved = dot(high, yhv[...]) + (dot(low, yhv[...]) + dot(high, ylv[...]))
        hy[0:count] = solved.reshape(count, ROWS, COLS)
        for k in range(count):
            both = dot(xhv[...], sxh[k])
            hx[k] = both[0:ROWS] + (both[ROWS:] + dot(xhv[0:ROWS, :], sxl[k]))

    lane128 = iota((ROWS, 128), 1)

    def edges_in(ref, across, along):
        for k, f in enumerate(across):
            for j in range(4):
                er[j, k:k + 1, :] = ref[f, FPAD + j:FPAD + j + 1, :]
                er[4 + j, k:k + 1, :] = ref[f, FPAD + ROWS - 1 - j:FPAD + ROWS - j, :]
            er[8, k:k + 1, :] = hx[k, 0:1, :]
            er[9, k:k + 1, :] = hx[k, ROWS - 1:ROWS, :]
        for k, f in enumerate(along):
            fl = ref[f, FPAD:FPAD + ROWS, 0:128]
            fr = ref[f, FPAD:FPAD + ROWS, COLS - 128:COLS]
            tile = jnp.where(lane128 < 32, fl, jnp.where(lane128 < 64, rolled(hy[k, :, 0:128], 32, 1), jnp.where(
                lane128 < 96, rolled(hy[k, :, COLS - 128:COLS], -32, 1), fr)))
            turned = tile.T
            for j in range(4):
                ec[j, k:k + 1, :] = turned[j:j + 1, :]
                ec[4 + j, k:k + 1, :] = turned[127 - j:128 - j, :]
            ec[8, k:k + 1, :] = turned[32:33, :]
            ec[9, k:k + 1, :] = turned[95:96, :]

    def edges_out():
        for e, msg in ((er, rowmsg), (ec, colmsg)):
            s0, s1 = edge_items([e[j] for j in range(4)])
            t0, t1 = edge_items([e[4 + j] for j in range(4)])
            items = ((e[0], e[1], e[8] + CORNER * s0 + NEXT * s1), (e[4], e[5], e[9] - CORNER * t0 - NEXT * t1))
            for end in range(2):
                for j in range(3):
                    msg[end, j] = items[end][j]

    def edges_send():
        return [
            send(rowmsg.at[0], rowgot.at[1], 0, rowsem.at[1], (up, a)),
            send(rowmsg.at[1], rowgot.at[0], 1, rowsem.at[0], (down, a)),
            send(colmsg.at[0], colgot.at[1], 2, colsem.at[1], (z, left)),
            send(colmsg.at[1], colgot.at[0], 3, colsem.at[0], (z, right)),
        ]

    def closing(e, got, keep_low, keep_high):
        f0, f1 = e[0], e[1]
        p1, p2, ph = got[0][0] * keep_low, got[0][1] * keep_low, got[0][2]
        s0, s1 = edge_items([e[j] for j in range(4)])
        s0 = s0 - A2 * p1 - B4 * p2
        s1 = s1 - B4 * p1
        own = e[8] + CORNER * s0 + NEXT * s1
        theirs = ph + CORNER * (A2 * f0 + B4 * f1) + NEXT * (B4 * f0)
        gp = (theirs - LINK * own) * COUPLE * keep_low
        low, low_end = s0 - s1 * (1.0 / Q) - Q * gp, s1 * (1.0 / Q)
        l0, l1 = e[4], e[5]
        n1, n2, nh = got[1][0] * keep_high, got[1][1] * keep_high, got[1][2]
        t0, t1 = edge_items([e[4 + j] for j in range(4)])
        t0 = A2 * n1 + B4 * n2 - t0
        t1 = B4 * n1 - t1
        own = e[9] + CORNER * t0 + NEXT * t1
        theirs = nh - CORNER * (A2 * l0 + B4 * l1) - NEXT * (B4 * l0)
        gn = (theirs - LINK * own) * COUPLE * keep_high
        return low, t0 - t1 * (1.0 / Q) - Q * gn, low_end, t1 * (1.0 / Q)

    def close_across(count):
        low, high, low_end, high_end = closing(er, rowgot, has_up, has_down)
        for k in range(count):
            hx[k, 0:1, :] = hx[k, 0:1, :] + low_end[k:k + 1, :]
            hx[k, ROWS - 1:ROWS, :] = hx[k, ROWS - 1:ROWS, :] + high_end[k:k + 1, :]
        return low, high

    def close_along(count):
        terms = closing(ec, colgot, 1.0, 1.0)
        block = jnp.concatenate(list(terms) + [jnp.zeros((96, 128), F32)], axis=0)
        turned = block.T
        for k in range(count):
            col = [jnp.broadcast_to(turned[:, 8 * j + k:8 * j + k + 1], (ROWS, 128)) for j in range(4)]
            hy[k, :, 0:128] = hy[k, :, 0:128] + col[0] * eyv[0:1, :] + jnp.where(lane128 == 0, col[2], 0.0)
            hy[k, :, COLS - 128:COLS] = (hy[k, :, COLS - 128:COLS] + col[1] * eyv[1:2, :]
                                         + jnp.where(lane128 == 127, col[3], 0.0))

    across_sources(fld, ACROSS)
    for load in loads[4:]:
        load.wait()
    solves(6)
    edges_in(fld, ACROSS, ALONG)
    edges_out()

    stat_c, stat_e = [t[0:8] + t[8:16] for t in stat]
    stat_c, stat_e = [sum(t[:, 128 * j:128 * (j + 1)] for j in range(4)) for t in (stat_c, stat_e)]
    sub8, lane8 = iota((8, 128), 0), iota((8, 128), 1)
    mixed = jnp.where(sub8 < 4, stat_c + rolled(stat_c, 4, 0), stat_e + rolled(stat_e, 4, 0))
    for s in (64, 32, 16, 8, 4, 2, 1):
        mixed = mixed + rolled(mixed, s, 1)
    mixed = mixed + jnp.where(sub8 % 4 < 2, rolled(mixed, -2, 0), rolled(mixed, 2, 0))
    mixed = mixed + jnp.where(sub8 % 2 < 1, rolled(mixed, -1, 0), rolled(mixed, 1, 0))
    stmsg[0] = mixed

    pl.semaphore_wait(barrier, len(greet))

    first_edges = edges_send()

    def spread(msg, slots, sem, peers, me, place):
        for p in peers:
            pltpu.make_async_remote_copy(src_ref=msg, dst_ref=slots.at[me], send_sem=sem.at[0], recv_sem=sem.at[1],
                                         device_id=place(p), device_id_type=MESH).start()
        slots[me] = msg[...]

    def spread_z(msg, slots, sem):
        spread(msg, slots, sem, zpeers, z, lambda p: (p, a))

    def spread_a(msg, slots, sem):
        spread(msg, slots, sem, apeers, a, lambda p: (z, p))

    def all_of(slots, sem, count):
        most = slots.at[pl.ds(0, count)]
        return pltpu.make_async_remote_copy(src_ref=most, dst_ref=most, send_sem=sem.at[0], recv_sem=sem.at[1],
                                            device_id=(z, right), device_id_type=MESH)

    spread_z(stmsg.at[0], stz, stzsem)

    top, bottom = pl.ds(0, HALO), pl.ds(EROWS - HALO, HALO)
    inner = pl.ds(HALO, ROWS)
    first_rows, last_rows = pl.ds(HALO, HALO), pl.ds(ROWS, HALO)
    low_cols, high_cols = pl.ds(0, 128), pl.ds(COLS - 128, 128)
    whole_cols = pl.ds(0, COLS)
    c_copies = [
        send(cext.at[first_rows, whole_cols], cext.at[bottom, whole_cols], 4, crowsem.at[1], (up, a)),
        send(cext.at[last_rows, whole_cols], cext.at[top, whole_cols], 5, crowsem.at[0], (down, a)),
        send(cext.at[inner, low_cols], cright.at[inner, :], 6, ccolsem.at[1], (z, left)),
        send(cext.at[inner, high_cols], cleft.at[inner, :], 7, ccolsem.at[0], (z, right)),
        send(cext.at[first_rows, low_cols], cright.at[bottom, :], 8, ccorsem.at[0], (up, left)),
        send(cext.at[first_rows, high_cols], cleft.at[bottom, :], 9, ccorsem.at[1], (up, right)),
        send(cext.at[last_rows, low_cols], cright.at[top, :], 10, ccorsem.at[2], (down, left)),
        send(cext.at[last_rows, high_cols], cleft.at[top, :], 11, ccorsem.at[3], (down, right)),
    ]

    for copy in first_edges:
        copy.wait_recv()
    xlow, xhigh = close_across(6)
    close_along(6)
    for load in loads[2:4]:
        load.wait()

    def wide(tile):
        return jnp.concatenate([tile] * 4, axis=1)

    er[0] = xlow
    er[1] = xhigh

    def second(i):
        rows = pl.ds(i * 16, 16)
        inner16 = pl.ds(i * 16 + FPAD, 16)
        wl, wr = wide(exlv[rows, :]), wide(exrv[rows, :])
        gx = [hx[k, rows, :] + (wl * er[0, k:k + 1, :] + wr * er[1, k:k + 1, :]) for k in range(6)]
        gy = [hy[k, rows, :] for k in range(6)]
        depth = dep[rows, :]
        rate = -(gx[1] + gy[1])
        active = (ov[rows, :] * (1 - cv[rows, :])).astype(F32)
        weight = BREAKING * active * depth * jnp.abs(rate) * depth
        sxx = 2.0 * weight * gx[2]
        sxy = weight * (gy[2] + gx[3])
        syy = 2.0 * weight * gy[3]
        ratev[rows, :] = -rate
        stress[0, inner16, :] = sxx
        stress[1, inner16, :] = sxy
        stress[2, inner16, :] = syy
        part[0, rows, :] = -gx[4] - gy[4] - depth * gx[0]
        part[1, rows, :] = -gx[5] - gy[5] - depth * gy[0]
        for k, f in enumerate((sxy, syy)):
            high, low = split_bf16(lane_source(f))
            syh[k, rows, :] = high
            syl[k, rows, :] = low

    for i in range(ROWS // 16):
        second(i)
    rate_out = pltpu.make_async_copy(ratev, out.at[0], outsem.at[0])
    rate_out.start()
    all_of(stz, stzsem, nz - 1).wait_recv()
    stmsg[1] = functools.reduce(lambda s, k: s + stz[k], range(1, nz), stz[0])
    spread_a(stmsg.at[1], sta, stasem)

    across_sources(stress, (0, 1))
    solves(2)
    edges_in(stress, (0, 1), (1, 2))

    def packed(items):
        row = iota(items[0].shape, 0)
        return jnp.where(row < 2, items[0], jnp.where(row < 4, rolled(items[1], 2, 0), jnp.where(
            row < 6, rolled(items[2], 4, 0), rolled(items[3], 6, 0)))), items[4]

    for e, own in ((er, rown), (ec, cown)):
        for end in range(2):
            cells = [e[4 * end + j] for j in range(4)]
            own[end, 0], own[end, 1] = packed((cells[0], cells[1], *edge_items(cells), e[8 + end]))

    def third(i):
        rows = pl.ds(i * 16, 16)
        ext = pl.ds(i * 16 + HALO, 16)
        fx = part[0, rows, :] + hx[0, rows, :] + hy[0, rows, :]
        fy = part[1, rows, :] + hx[1, rows, :] + hy[1, rows, :]
        bx[ext, 0:COLS] = fx
        by[ext, 0:COLS] = fy
        lane = iota((16, 128), 1)
        fmsg[0, rows, :] = jnp.where(lane < 64, fx[:, 0:128], rolled(fy[:, 0:128], 64, 1))
        fmsg[1, rows, :] = jnp.where(lane < 64, rolled(fy[:, COLS - 128:], 64, 1), fx[:, COLS - 128:])

    for i in range(ROWS // 16):
        third(i)
    lo8, hi8 = pl.ds(0, HALO), pl.ds(ROWS - HALO, HALO)
    ends = pl.ds(0, 2)
    exchanges = []
    for who, side in (((z, left), 0), ((z, right), 1)):
        exchanges.append((fmsg.at[side], (fleft if side else fright).at[inner, :], who))
    for who, low, vert in (((up, left), 1, 0), ((up, right), 0, 0), ((down, left), 1, 1), ((down, right), 0, 1)):
        cols = low_cols if low else high_cols
        side = 0 if low else 1
        exchanges += [
            (rown.at[vert, ends, :, cols], rst.at[side, 3 - vert], who),
            (cown.at[1 - low], cst.at[vert, 2 + low], who),
            (fmsg.at[side, hi8 if vert else lo8, :], (fright if low else fleft).at[top if vert else bottom, :], who),
        ]
    for who, side in (((z, left), 0), ((z, right), 1)):
        cols = high_cols if side else low_cols
        exchanges += [
            (cown.at[side], coth.at[1 - side], who),
            (rown.at[ends, ends, :, cols], rst.at[side, ends], who),
        ]
    for who, vert in (((up, a), 0), ((down, a), 1)):
        rows, place = (last_rows, top) if vert else (first_rows, bottom)
        exchanges += [
            (rown.at[vert], roth.at[1 - vert], who),
            (cown, cst.at[vert, ends], who),
            (bx.at[rows, whole_cols], bx.at[place, whole_cols], who),
            (by.at[rows, whole_cols], by.at[place, whole_cols], who),
        ]
    f_copies = [send(src, dst, 12 + n, msem.at[n], who) for n, (src, dst, who) in enumerate(exchanges)]

    for copy in c_copies:
        copy.wait_recv()

    def wide5(tile):
        return jnp.concatenate([tile] * 5, axis=1)

    sub = iota((8, ECOLS), 0)
    lanes = iota((8, 128), 1)

    def gathered_c(i):
        rows = pl.ds(i * 8, 8)
        side = jnp.where(lanes < 64, cright[rows, :], cleft[rows, :])
        c = jnp.concatenate([cext[rows, 0:COLS], side], axis=1)
        if i == 0:
            c = c * has_up
        if i == EROWS // 8 - 1:
            c = c * has_down
        cs[rows, :] = c
        crec[rows, :] = 1.0 / c

    for i in range(EROWS // 8):
        gathered_c(i)
    all_of(sta, stasem, na - 1).wait_recv()
    total = functools.reduce(lambda s, k: s + sta[k], range(1, na), sta[0])
    weight_c = jnp.broadcast_to(total[0:1, 0:1], (8, 128))
    weight_e = jnp.broadcast_to(total[4:5, 0:1], (8, 128))
    top_value = jnp.where(weight_e > 0.0, 10.0 * weight_c / weight_e, 100.0)
    half_top = 0.5 * top_value
    shrink = 1.0 / half_top
    shrink5 = wide5(shrink)

    for copy in f_copies:
        copy.wait_recv()

    def unpacked(tiles):
        return [rolled(tiles[0], -2 * j, 0) for j in range(4)] + [tiles[1]]

    def interface(before, after, keep):
        l0, l1, t0, t1, hl = before
        f0, f1, s0, s1, hf = after
        inflow, inflow1 = A2 * l0 + B4 * l1, B4 * l0
        outflow, outflow1 = A2 * f0 + B4 * f1, B4 * f0
        low0, low1 = s0 - keep * inflow, s1 - keep * inflow1
        high0, high1 = keep * outflow - t0, keep * outflow1 - t1
        own_low = hf + CORNER * low0 + NEXT * low1
        own_high = hl + CORNER * high0 + NEXT * high1
        bare_high = hl - CORNER * t0 - NEXT * t1 + CORNER * outflow + NEXT * outflow1
        bare_low = hf + CORNER * s0 + NEXT * s1 - CORNER * inflow - NEXT * inflow1
        gp = (bare_high - LINK * own_low) * COUPLE * keep
        gn = (bare_low - LINK * own_high) * COUPLE * keep
        return (low0 - low1 * (1.0 / Q) - Q * gp, low1 * (1.0 / Q), high0 - high1 * (1.0 / Q) - Q * gn, high1 * (1.0 / Q))

    def extended(body, stage_, slot):
        return unpacked([jnp.concatenate([body[t], jnp.where(lanes < 64, stage_[0, slot, t], stage_[1, slot, t])], axis=1)
                         for t in range(2)])

    tops = interface(extended(roth.at[0], rst, 2), extended(rown.at[0], rst, 0), has_up)
    bottoms = interface(extended(rown.at[1], rst, 1), extended(roth.at[1], rst, 3), has_down)
    lefts = interface(extended(coth.at[0], cst, 2), extended(cown.at[0], cst, 0), 1.0)
    rights = interface(extended(cown.at[1], cst, 1), extended(coth.at[1], cst, 3), 1.0)
    stacked = jnp.concatenate(list(lefts) + list(rights) + [jnp.zeros((64, 256), F32)], axis=0)
    turned_own, turned_side = stacked[:, 0:128].T, stacked[:, 128:256].T
    ey0, ey1 = eyv[0:1, :], eyv[1:2, :]

    def closed(i):
        rows = pl.ds(8 * i, 8)
        r = 8 * (i - 1)
        from_right, from_left = fright[rows, :], fleft[rows, :]
        side = (jnp.where(lanes < 64, from_right, from_left),
                jnp.where(lanes < 64, rolled(from_right, 64, 1), rolled(from_left, 64, 1)))
        block = turned_side[120:128] if i == 0 else turned_side[0:8] if i == EROWS // 8 - 1 else turned_own[r:r + 8]
        for k, (src, dst) in enumerate(((bx, bx2), (by, by2))):
            def term(which):
                return which[k:k + 1, :]

            def col(c):
                return jnp.broadcast_to(block[:, 8 * c + k:8 * c + k + 1], (8, 128))

            if i == 0:
                across = wide5(exrv[120:128, :]) * term(tops[2]) + jnp.where(sub == 7, term(tops[3]), 0.0)
            elif i == EROWS // 8 - 1:
                across = wide5(exlv[0:8, :]) * term(bottoms[0]) + jnp.where(sub == 0, term(bottoms[1]), 0.0)
            else:
                across = wide5(exlv[r:r + 8, :]) * term(tops[0]) + wide5(exrv[r:r + 8, :]) * term(bottoms[2])
                if i == 1:
                    across = across + jnp.where(sub == 0, term(tops[1]), 0.0)
                if i == EROWS // 8 - 2:
                    across = across + jnp.where(sub == 7, term(bottoms[3]), 0.0)
            low = col(0) * ey0 + jnp.where(lanes == 0, col(1), 0.0)
            high = col(6) * ey1 + jnp.where(lanes == 127, col(7), 0.0)
            beyond = jnp.where(lanes < 64, col(4) * ey0 + jnp.where(lanes == 0, col(5), 0.0),
                               col(2) * ey1 + jnp.where(lanes == 127, col(3), 0.0))
            nothing = jnp.zeros((8, 128), F32)
            along = jnp.concatenate([low, nothing, nothing, high, beyond], axis=1)
            value = jnp.concatenate([src[rows, 0:COLS], side[k]], axis=1) + (across + along)
            if k == 0 and i == EROWS // 8 - 1:
                value = value * has_down
            dst[rows, :] = value

    for i in range(EROWS // 8):
        closed(i)

    def tile_at(ref, i):
        return ref[8 * i:8 * i + 8, :]

    def below_of(x, nxt):
        return jnp.where(sub == 7, rolled(nxt, -1, 0), rolled(x, -1, 0))

    def above_of(x, prv):
        return jnp.where(sub == 0, rolled(prv, 1, 0), rolled(x, 1, 0))

    TILES = EROWS // 8

    def inside(t):
        return t[:, 0:COLS]

    nil8 = jnp.zeros((8, COLS), F32)
    norm, sums = nil8, nil8
    wx = tile_at(bx2, 0)
    for i in range(TILES):
        nxt = tile_at(bx2, min(i + 1, TILES - 1))
        wy = tile_at(by2, i)
        c = tile_at(cs, i) * shrink5
        cs[8 * i:8 * i + 8, :] = c
        t = c * ((below_of(wx, nxt) - wx) + (rolled(wy, -1, 1) - wy))
        tau[0, 8 * i:8 * i + 8, :] = t
        if 0 < i < TILES - 1:
            norm = norm + (inside(wx) * inside(wx) + inside(wy) * inside(wy))
            sums = sums + inside(t) * (inside(t) * inside(tile_at(crec, i)))
        wx = nxt
    acc[0] = sums
    acc[15] = norm
    last_diag = jnp.where((sub == 7) & (z == nz - 1), 3.0, 4.0)

    def sweep(k, start):
        cross_sum, square_sum = nil8, nil8
        first_tile, stop = (1, TILES - 1) if start == 2 else (0, TILES)
        prv = tau[k, 8 * max(first_tile - 1, 0):8 * max(first_tile - 1, 0) + 8, :]
        x = tau[k, 8 * first_tile:8 * first_tile + 8, :]
        for i in range(first_tile, stop):
            j = min(i + 1, TILES - 1)
            nxt = tau[k, 8 * j:8 * j + 8, :]
            around = (above_of(x, prv) + below_of(x, nxt)) + (rolled(x, -1, 1) + rolled(x, 1, 1))
            diag = last_diag if i == TILES - 2 else 4.0
            t = tile_at(cs, i) * (diag * x - around) - x
            if start > 0:
                t = 2.0 * t - tau[k - 1, 8 * i:8 * i + 8, :]
            tau[k + 1, 8 * i:8 * i + 8, :] = t
            if 0 < i < TILES - 1:
                q = inside(t) * inside(tile_at(crec, i))
                cross_sum = cross_sum + inside(x) * q
                square_sum = square_sum + inside(t) * q
            prv, x = x, nxt
        acc[2 * k + 1] = cross_sum
        acc[2 * k + 2] = square_sum

    sweep(0, 0)

    def sweeps(k, _):
        sweep(k, 1)
        return 0

    lax.fori_loop(1, ITERS - 2, sweeps, 0)
    sweep(ITERS - 2, 2)
    dots = [acc[k] for k in range(16)]

    def fold(t):
        s0 = dd_add(two_sum(t[:, 0:128], t[:, 128:256]), two_sum(t[:, 256:384], t[:, 384:512]))
        return s0

    level = [fold(t) for t in dots]
    for width, span in ((8, 4), (4, 2), (2, 1)):
        mask = sub8 % (2 * span) < span

        def merge(p, q, mask=mask, span=span):
            def parts(g, h):
                w = jnp.where(mask, h, g)
                return jnp.where(mask, g, h), jnp.where(mask, rolled(w, -span, 0), rolled(w, span, 0))
            xh_, yh_ = parts(p[0], q[0])
            xl_, yl_ = parts(p[1], q[1])
            return dd_add((xh_, xl_), (yh_, yl_))

        level = [merge(level[i], level[i + width]) for i in range(width)]
    for s in (64, 32, 16, 8, 4, 2, 1):
        level = [dd_add(p, (rolled(p[0], s, 1), rolled(p[1], s, 1))) for p in level]
    even, odd = level

    dtmsg[0] = jnp.where(lane8 < 32, even[0], jnp.where(lane8 < 64, odd[0], jnp.where(lane8 < 96, even[1], odd[1])))
    spread_z(dtmsg.at[0], dtz, dtzsem)
    all_of(dtz, dtzsem, nz - 1).wait_recv()

    def gathered(slots, count):
        level = [(slots[k], rolled(slots[k], 64, 1)) for k in range(count)]
        while len(level) > 1:
            level = [dd_add(level[2 * i], level[2 * i + 1]) for i in range(len(level) // 2)]
        return level[0]

    sums = gathered(dtz, nz)
    dtmsg[1] = jnp.where(lane8 < 64, sums[0], rolled(sums[1], 64, 1))
    spread_a(dtmsg.at[1], dta, dtasem)
    all_of(dta, dtasem, na - 1).wait_recv()
    sums = gathered(dta, na)

    def pick(value, lane):
        return jnp.broadcast_to(value[:, lane:lane + 1], (8, 128))

    def row_of(value, r):
        return tuple(jnp.broadcast_to(part_[r:r + 1, :], (8, 128)) for part_ in value)

    even = pick(sums[0], 0), pick(sums[1], 0)
    odd = pick(sums[0], 32), pick(sums[1], 32)
    square = row_of(odd, 7)
    even, odd = dd_scale(even, half_top), dd_scale(odd, half_top)
    even = dd_add((2.0 * even[0], 2.0 * even[1]), dd_neg(row_of(even, 0)))
    odd = dd_add((2.0 * odd[0], 2.0 * odd[1]), dd_neg(row_of(odd, 0)))

    MOM, SEC, GRAM, MIX = range(4)
    nsc[...] = jnp.zeros(nsc.shape, F32)
    for part_ in range(2):
        for j in range(15):
            value = (even, odd)[j % 2][part_][j // 2:j // 2 + 1, :]
            nsc[MOM, part_, 8 + j:9 + j, :] = value
            if j == 1:
                nsc[MOM, part_, 7:8, :] = value

    def entries(which, start, count=8):
        return nsc[which, 0, start:start + count, :], nsc[which, 1, start:start + count, :]

    def widened(which, start):
        return dd_add(entries(which, start), dd_half(dd_add(entries(which, start + 1), entries(which, start - 1))))

    for start in (8, 16):
        value = widened(MOM, start)
        nsc[SEC, 0, start:start + 8, :], nsc[SEC, 1, start:start + 8, :] = value
        mix = dd_add(entries(MOM, start), dd_scale(value, half_top))
        nsc[MIX, 0, start:start + 8, :], nsc[MIX, 1, start:start + 8, :] = mix
    for part_ in range(2):
        nsc[SEC, part_, 7:8, :] = nsc[SEC, part_, 9:10, :]
    for start in (8, 16):
        value = dd_add(entries(SEC, start), dd_scale(widened(SEC, start), half_top))
        nsc[GRAM, 0, start:start + 8, :], nsc[GRAM, 1, start:start + 8, :] = value
    for part_ in range(2):
        for j in range(1, 8):
            nsc[GRAM, part_, 8 - j:9 - j, :] = nsc[GRAM, part_, 8 + j:9 + j, :]

    def with_first(value, head):
        return tuple(jnp.where(sub8 == 0, h, v) for v, h in zip(value, head))

    moment0 = row_of(entries(MOM, 8), 0)
    matrix = [with_first(entries(MIX, 7), dd_add(square, dd_scale(moment0, half_top)))]
    for l in range(ITERS - 1):
        column = dd_half(dd_add(entries(GRAM, 7 + l), entries(GRAM, 7 - l)))
        matrix.append(with_first(column, row_of(entries(MIX, 8 + l), 0)))
    right_side = with_first(entries(MOM, 7), square)
    diagonal = jnp.zeros((8, 128), F32)
    first_diagonal = [row_of(matrix[k], k)[0] for k in range(ITERS)]
    for k in range(ITERS):
        pivot = row_of(matrix[k], k)
        usable = pivot[0] > 1e-11 * first_diagonal[k]
        safe = jnp.where(usable, pivot[0], 1.0), jnp.where(usable, pivot[1], 0.0)
        factor = dd_div(matrix[k], safe)
        skip = (sub8 == k) | jnp.logical_not(usable)
        factor = tuple(jnp.where(skip, 0.0, f) for f in factor)
        diagonal = jnp.where((sub8 == k) & usable, pivot[0], diagonal)
        for l in range(k + 1, ITERS):
            matrix[l] = dd_add(matrix[l], dd_neg(dd_mul(factor, row_of(matrix[l], k))))
        right_side = dd_add(right_side, dd_neg(dd_mul(factor, row_of(right_side, k))))
    answer = jnp.where(diagonal > 0.0, right_side[0] / jnp.where(diagonal > 0.0, diagonal, 1.0), 0.0)
    nsc[MOM, 0, 0:8, :] = answer

    weights = [jnp.broadcast_to(nsc[MOM, 0, k:k + 1, :], (8, 128)) for k in range(ITERS)]

    def combined(j, w):
        return functools.reduce(lambda s, t: s + t, [w[l + 1] * tau[l, 8 * j:8 * j + 8, :] for l in range(ITERS - 1)])

    w5 = [wide5(w) for w in weights]
    gain = wide(weights[0])
    solved_out = []
    prv = combined(0, w5)
    for i in range(ROWS // 8):
        here = combined(i + 1, w5)
        solv[0, 8 * i:8 * i + 8, :] = inside(here - above_of(here, prv)) - gain * inside(tile_at(bx2, i + 1))
        solv[1, 8 * i:8 * i + 8, :] = inside(here - rolled(here, 1, 1)) - gain * inside(tile_at(by2, i + 1))
        prv = here
        if i % 4 == 3:
            piece = pl.ds(8 * (i - 3), 32)
            solved_out.append(pltpu.make_async_copy(solv.at[:, piece, :], out.at[pl.ds(1, 2), piece, :], outsem.at[1 + i // 4]))
            solved_out[-1].start()
    for copy in sends + [all_of(stz, stzsem, nz - 1), all_of(sta, stasem, na - 1), all_of(dtz, dtzsem, nz - 1), all_of(dta, dtasem, na - 1)]:
        copy.wait_send()
    rate_out.wait()
    for copy in solved_out:
        copy.wait()


def per_device(nz, na, wave_state, depth_class, onset_flag, cessation, class_depth):
    across, along = tridiagonal_inverse(ROWS), tridiagonal_inverse(COLS)
    xhl = np.concatenate(halves(derivative_matrix(ROWS)), axis=0)
    yh, yl = halves(derivative_matrix(COLS).T)
    exl = np.repeat(across[:, :1], 128, axis=1).astype(np.float32)
    exr = np.repeat(across[:, -1:], 128, axis=1).astype(np.float32)
    ey = np.zeros((8, 128), np.float32)
    ey[0] = along[0, :128]
    ey[1] = along[-1, -128:]
    consts = [jnp.asarray(t) for t in (xhl, yh, yl, exl, exr, ey)]
    dma = pltpu.SemaphoreType.DMA

    def vm(*shape, dtype=F32):
        return pltpu.VMEM(shape, dtype)

    scratch = [
        vm(3, ROWS, COLS), vm(ROWS, COLS, dtype=jnp.int32), vm(ROWS, COLS, dtype=jnp.int32), vm(ROWS, COLS, dtype=jnp.int32),
        vm(2 * ROWS, ROWS, dtype=BF16), vm(COLS, COLS, dtype=BF16), vm(COLS, COLS, dtype=BF16),
        vm(ROWS, 128), vm(ROWS, 128), vm(8, 128),
        vm(8, ROWS + 2 * FPAD, COLS), vm(ROWS, COLS),
        vm(6, ROWS, COLS, dtype=BF16), vm(6, ROWS, COLS, dtype=BF16), vm(6, ROWS, COLS, dtype=BF16), vm(6, ROWS, COLS, dtype=BF16),
        vm(6, ROWS, COLS), vm(6, ROWS, COLS), vm(10, 8, COLS), vm(10, 8, 128),
        vm(3, ROWS + 2 * FPAD, COLS), vm(2, ROWS, COLS), vm(ROWS, COLS), vm(2, ROWS, COLS),
        vm(2, 3, 8, COLS), vm(2, 3, 8, COLS), vm(2, 3, 8, 128), vm(2, 3, 8, 128),
        vm(2, 2, 8, COLS), vm(2, 2, 8, COLS), vm(2, 4, 2, 8, 128), vm(2, 2, 8, 128), vm(2, 2, 8, 128), vm(2, 4, 2, 8, 128),
        vm(EROWS, ECOLS), vm(EROWS, ECOLS),
        vm(EROWS, ECOLS), vm(EROWS, ECOLS), vm(EROWS, ECOLS), vm(EROWS, ECOLS),
        vm(EROWS, 128), vm(EROWS, 128), vm(EROWS, 128), vm(EROWS, 128), vm(2, ROWS, 128),
        vm(ITERS, EROWS, ECOLS), vm(EROWS, ECOLS), vm(16, 8, COLS),
        vm(2, 8, 128), vm(nz, 8, 128), vm(na, 8, 128), vm(2, 8, 128), vm(nz, 8, 128), vm(na, 8, 128), vm(4, 2, 32, 128),
        dma((10,)), dma((5,)), dma((38,)), dma((2,)), dma((2,)), dma((2,)), dma((2,)), dma((4,)), dma((26,)),
        dma((2,)), dma((2,)), dma((2,)), dma((2,)),
    ]
    anywhere = pl.BlockSpec(memory_space=pl.ANY)
    negated = pl.pallas_call(
        functools.partial(kernel, nz, na),
        out_shape=jax.ShapeDtypeStruct((3, ROWS, COLS), F32),
        in_specs=[anywhere] * 4 + [pl.BlockSpec(memory_space=pltpu.SMEM)] + [anywhere] * 6,
        out_specs=anywhere,
        scratch_shapes=scratch,
        compiler_params=pltpu.CompilerParams(collective_id=0, has_side_effects=True, vmem_limit_bytes=VMEM_BYTES),
    )(wave_state, depth_class, onset_flag, cessation, class_depth, *consts)
    return -negated


def solution(mesh):
    sizes = dict(mesh.shape)
    in_specs = (P(None, "xs", "al"), P("xs", "al"), P("xs", "al"), P("xs", "al"), P())
    return jax.shard_map(
        functools.partial(per_device, sizes["xs"], sizes["al"]),
        mesh=mesh, in_specs=in_specs, out_specs=P(None, "xs", "al"), check_vma=False,
    )
```

```python
import functools

import jax
import jax.numpy as jnp
import numpy as np
from jax import lax
from jax.experimental import pallas as pl
from jax.experimental.pallas import tpu as pltpu
from jax.sharding import PartitionSpec as P

MESH = pl.DeviceIdType.MESH
CLASSES = 8
ITERS = 8
ROWS, COLS = 128, 512
HALO = 8
EROWS, ECOLS = ROWS + 2 * HALO, COLS + 128
FPAD = 16
Q = 1.0 / 3.0
A2 = 0.5 * 14.0 / 9.0
B4 = 0.25 / 9.0
BREAKING = 0.05
VMEM_BYTES = 63 * 2**20
F32, BF16 = jnp.float32, jnp.bfloat16


def tridiagonal_inverse(length):
    band = np.eye(length) + Q * (np.eye(length, k=1) + np.eye(length, k=-1))
    return np.linalg.inv(band)


CORNER = float(tridiagonal_inverse(ROWS)[0, 0])
NEXT = (1.0 - CORNER) / Q
LINK = Q * CORNER
COUPLE = 1.0 / (1.0 - LINK * LINK)


def halves(matrix):
    matrix = matrix.astype(np.float32)
    high = matrix.astype(jnp.bfloat16)
    low = (matrix - high.astype(np.float32)).astype(jnp.bfloat16)
    return high, low


def split_bf16(value):
    high = value.astype(BF16)
    return high, (value - high.astype(F32)).astype(BF16)


def two_sum(a, b):
    s = a + b
    t = s - a
    return s, (a - (s - t)) + (b - t)


def quick_sum(a, b):
    s = a + b
    return s, b - (s - a)


def cut(a):
    t = 4097.0 * a
    high = t - (t - a)
    return high, a - high


def two_prod(a, b):
    p = a * b
    ah, al = cut(a)
    bh, bl = cut(b)
    return p, ((ah * bh - p) + ah * bl + al * bh) + al * bl


def dd_add(a, b):
    s, e = two_sum(a[0], b[0])
    return quick_sum(s, e + (a[1] + b[1]))


def dd_gather(a, b):
    s, e = two_sum(a[0], b[0])
    return s, e + (a[1] + b[1])


def dd_neg(a):
    return -a[0], -a[1]


def dd_mul(a, b):
    p, e = two_prod(a[0], b[0])
    return quick_sum(p, e + (a[0] * b[1] + a[1] * b[0]))


def dd_scale(a, b):
    p, e = two_prod(a[0], b)
    return quick_sum(p, e + a[1] * b)


def dd_half(a):
    return 0.5 * a[0], 0.5 * a[1]


def dd_div(a, b):
    inverse = 1.0 / b[0]
    first = a[0] * inverse
    rest = dd_add(a, dd_neg(dd_scale(b, first)))
    return quick_sum(first, rest[0] * inverse)


def rolled(value, shift, axis):
    size = value.shape[axis]
    return pltpu.roll(value, shift % size, axis)


def iota(shape, axis):
    return lax.broadcasted_iota(jnp.int32, shape, axis)


def lane_source(field):
    return rolled(field, -1, 1) - field


def row_source(around):
    return (rolled(around, -1, 0) - around)[0:16]


def derivative_matrix(length):
    eye, shift = np.eye(length), functools.partial(np.eye, length)
    near = A2 * (eye + shift(k=-1))
    far = B4 * (shift(k=1) + eye + shift(k=-1) + shift(k=-2))
    inside = np.zeros((length, 1))
    inside[2:length - 2] = 1.0
    return tridiagonal_inverse(length) @ (inside * (near + far))


def edge_items(f):
    return A2 * f[1] + B4 * f[2], A2 * (f[2] - f[0]) + B4 * f[3]


def kernel(nz, na, ws, dc, on, ce, cd, xhl, yh, yl, exl, exr, ey, out,
           wv, dv, ov, cv, xhv, yhv, ylv, exlv, exrv, eyv,
           fld, dep, sxh, sxl, syh, syl, hx, hy, er, ec, stress, part, ratev, solv,
           rowmsg, rowgot, colmsg, colgot, rown, roth, rst, cown, coth, cst, bx2, by2, bx, by, cext, cs, cright, cleft, fright, fleft, fmsg, tau, crec, acc,
           stmsg, stz, sta, dtmsg, dtz, dta, nsc,
           insem, outsem, ssem, rsem,
           stzsem, stasem, dtzsem, dtasem):
    z, a = lax.axis_index("xs"), lax.axis_index("al")
    up, down = lax.rem(z + nz - 1, nz), lax.rem(z + 1, nz)
    left, right = lax.rem(a + na - 1, na), lax.rem(a + 1, na)
    has_up = (z > 0).astype(F32)
    has_down = (z < nz - 1).astype(F32)

    barrier = pltpu.get_barrier_semaphore()
    zpeers = [lax.rem(z + k, nz) for k in sorted(range(1, nz), key=lambda k: -min(k, nz - k))]
    px, py, core = a // 8, (a % 8) // 2, a % 2
    steps = sorted([(i, j, k) for i in range(4) for j in range(4) for k in range(2)][1:],
                   key=lambda t: -(min(t[0], 4 - t[0]) + min(t[1], 4 - t[1])))
    apeers = [lax.rem(px + i, 4) * 8 + lax.rem(py + j, 4) * 2 + (core + k - 2 * core * k) for i, j, k in steps]
    corners = [(up, left), (up, right), (down, left), (down, right)]
    greet = [(p, a) for p in zpeers] + [(z, p) for p in apeers] + corners
    loads = [pltpu.make_async_copy(s, d, insem.at[k]) for k, (s, d) in enumerate(
        [(ws, wv), (dc, dv), (on, ov), (ce, cv), (xhl, xhv), (yh, yhv), (yl, ylv), (exl, exlv), (exr, exrv), (ey, eyv)])]
    for load in loads:
        load.start()
    for who in greet:
        pl.semaphore_signal(barrier, inc=1, device_id=who, device_id_type=MESH)


    def send(src, dst, stage, who):
        pltpu.make_async_remote_copy(src_ref=src, dst_ref=dst, send_sem=ssem.at[stage], recv_sem=rsem.at[stage],
                                     device_id=who, device_id_type=MESH).start()

    def exchanged(stage):
        bulk = (tau.at[0, pl.ds(0, 48), :], tau.at[0, pl.ds(0, 88), pl.ds(0, COLS)], tau.at[:, pl.ds(0, 104), pl.ds(0, 128)])[stage]
        return pltpu.make_async_remote_copy(src_ref=bulk, dst_ref=bulk, send_sem=ssem.at[stage], recv_sem=rsem.at[stage],
                                            device_id=(z, right), device_id_type=MESH)

    for load in loads[:2]:
        load.wait()
    SUR, FX, FY, U, V, FXU, FXV, FYV = range(8)
    ACROSS = (SUR, FX, U, V, FXU, FXV)
    ALONG = (SUR, FY, U, V, FXV, FYV)

    def first(i, sums):
        rows = pl.ds(i * 16, 16)
        inner = pl.ds(i * 16 + FPAD, 16)
        kind = dv[rows, :]
        still = jnp.full((16, COLS), cd[0], F32)
        for k in range(1, CLASSES):
            still = jnp.where(kind == k, cd[k], still)
        surface, px, py = wv[0, rows, :], wv[1, rows, :], wv[2, rows, :]
        depth = still + surface
        u, v = px / depth, py / depth
        fields = [surface, px, py, u, v, px * u, px * v, py * v]
        for k, f in enumerate(fields):
            fld[k, inner, :] = f
        dep[rows, :] = depth
        c = depth * depth * (1.0 / 3.0)
        cext[pl.ds(i * 16 + HALO, 16), 0:COLS] = c
        for k, f in enumerate(ALONG):
            high, low = split_bf16(lane_source(fields[f]))
            syh[k, rows, :] = high
            syl[k, rows, :] = low
        energy = surface * surface + px * px + py * py
        return sums[0] + c * energy, sums[1] + energy

    nil = jnp.zeros((16, COLS), F32)
    stat = nil, nil
    for i in range(ROWS // 16):
        stat = first(i, stat)

    def across_sources(ref, which):
        for k, f in enumerate(which):
            for i in range(ROWS // 16):
                around = ref[f, i * 16 + FPAD:i * 16 + FPAD + 24, :]
                high, low = split_bf16(row_source(around))
                sxh[k, i * 16:i * 16 + 16, :] = high
                sxl[k, i * 16:i * 16 + 16, :] = low

    def solves(count):
        dot = functools.partial(jnp.dot, preferred_element_type=F32)
        high = syh[0:count].reshape(count * ROWS, COLS)
        low = syl[0:count].reshape(count * ROWS, COLS)
        solved = dot(high, yhv[...]) + (dot(low, yhv[...]) + dot(high, ylv[...]))
        hy[0:count] = solved.reshape(count, ROWS, COLS)
        for k in range(count):
            both = dot(xhv[...], sxh[k])
            hx[k] = both[0:ROWS] + (both[ROWS:] + dot(xhv[0:ROWS, :], sxl[k]))

    lane128 = iota((ROWS, 128), 1)

    def edges_in(ref, across, along):
        for k, f in enumerate(across):
            for j in range(4):
                er[j, k:k + 1, :] = ref[f, FPAD + j:FPAD + j + 1, :]
                er[4 + j, k:k + 1, :] = ref[f, FPAD + ROWS - 1 - j:FPAD + ROWS - j, :]
            er[8, k:k + 1, :] = hx[k, 0:1, :]
            er[9, k:k + 1, :] = hx[k, ROWS - 1:ROWS, :]
        for k, f in enumerate(along):
            fl = ref[f, FPAD:FPAD + ROWS, 0:128]
            fr = ref[f, FPAD:FPAD + ROWS, COLS - 128:COLS]
            tile = jnp.where(lane128 < 32, fl, jnp.where(lane128 < 64, rolled(hy[k, :, 0:128], 32, 1), jnp.where(
                lane128 < 96, rolled(hy[k, :, COLS - 128:COLS], -32, 1), fr)))
            turned = tile.T
            for j in range(4):
                ec[j, k:k + 1, :] = turned[j:j + 1, :]
                ec[4 + j, k:k + 1, :] = turned[127 - j:128 - j, :]
            ec[8, k:k + 1, :] = turned[32:33, :]
            ec[9, k:k + 1, :] = turned[95:96, :]

    def edges_out():
        for e, msg in ((er, rowmsg), (ec, colmsg)):
            s0, s1 = edge_items([e[j] for j in range(4)])
            t0, t1 = edge_items([e[4 + j] for j in range(4)])
            items = ((e[0], e[1], e[8] + CORNER * s0 + NEXT * s1), (e[4], e[5], e[9] - CORNER * t0 - NEXT * t1))
            for end in range(2):
                for j in range(3):
                    msg[end, j] = items[end][j]

    def edges_send():
        send(colmsg.at[0], colgot.at[1], 0, (z, left))
        send(colmsg.at[1], colgot.at[0], 0, (z, right))
        send(rowmsg.at[0], rowgot.at[1], 0, (up, a))
        send(rowmsg.at[1], rowgot.at[0], 0, (down, a))

    def closing(e, got, keep_low, keep_high):
        f0, f1 = e[0], e[1]
        p1, p2, ph = got[0][0] * keep_low, got[0][1] * keep_low, got[0][2]
        s0, s1 = edge_items([e[j] for j in range(4)])
        s0 = s0 - A2 * p1 - B4 * p2
        s1 = s1 - B4 * p1
        own = e[8] + CORNER * s0 + NEXT * s1
        theirs = ph + CORNER * (A2 * f0 + B4 * f1) + NEXT * (B4 * f0)
        gp = (theirs - LINK * own) * COUPLE * keep_low
        low, low_end = s0 - s1 * (1.0 / Q) - Q * gp, s1 * (1.0 / Q)
        l0, l1 = e[4], e[5]
        n1, n2, nh = got[1][0] * keep_high, got[1][1] * keep_high, got[1][2]
        t0, t1 = edge_items([e[4 + j] for j in range(4)])
        t0 = A2 * n1 + B4 * n2 - t0
        t1 = B4 * n1 - t1
        own = e[9] + CORNER * t0 + NEXT * t1
        theirs = nh - CORNER * (A2 * l0 + B4 * l1) - NEXT * (B4 * l0)
        gn = (theirs - LINK * own) * COUPLE * keep_high
        return low, t0 - t1 * (1.0 / Q) - Q * gn, low_end, t1 * (1.0 / Q)

    def close_across(count):
        low, high, low_end, high_end = closing(er, rowgot, has_up, has_down)
        for k in range(count):
            hx[k, 0:1, :] = hx[k, 0:1, :] + low_end[k:k + 1, :]
            hx[k, ROWS - 1:ROWS, :] = hx[k, ROWS - 1:ROWS, :] + high_end[k:k + 1, :]
        return low, high

    def close_along(count):
        terms = closing(ec, colgot, 1.0, 1.0)
        block = jnp.concatenate(list(terms) + [jnp.zeros((96, 128), F32)], axis=0)
        turned = block.T
        for k in range(count):
            col = [jnp.broadcast_to(turned[:, 8 * j + k:8 * j + k + 1], (ROWS, 128)) for j in range(4)]
            hy[k, :, 0:128] = hy[k, :, 0:128] + col[0] * eyv[0:1, :] + jnp.where(lane128 == 0, col[2], 0.0)
            hy[k, :, COLS - 128:COLS] = (hy[k, :, COLS - 128:COLS] + col[1] * eyv[1:2, :]
                                         + jnp.where(lane128 == 127, col[3], 0.0))

    across_sources(fld, ACROSS)
    for load in loads[4:]:
        load.wait()
    solves(6)
    edges_in(fld, ACROSS, ALONG)
    edges_out()

    stat_c, stat_e = [t[0:8] + t[8:16] for t in stat]
    stat_c, stat_e = [sum(t[:, 128 * j:128 * (j + 1)] for j in range(4)) for t in (stat_c, stat_e)]
    sub8, lane8 = iota((8, 128), 0), iota((8, 128), 1)
    mixed = jnp.where(sub8 < 4, stat_c + rolled(stat_c, 4, 0), stat_e + rolled(stat_e, 4, 0))
    for s in (64, 32, 16, 8, 4, 2, 1):
        mixed = mixed + rolled(mixed, s, 1)
    mixed = mixed + jnp.where(sub8 % 4 < 2, rolled(mixed, -2, 0), rolled(mixed, 2, 0))
    mixed = mixed + jnp.where(sub8 % 2 < 1, rolled(mixed, -1, 0), rolled(mixed, 1, 0))
    stmsg[0] = mixed

    pl.semaphore_wait(barrier, len(greet))

    edges_send()

    def spread(msg, slots, sem, peers, me, place):
        for p in peers:
            pltpu.make_async_remote_copy(src_ref=msg, dst_ref=slots.at[me], send_sem=sem.at[0], recv_sem=sem.at[1],
                                         device_id=place(p), device_id_type=MESH).start()
        slots[me] = msg[...]

    def spread_z(msg, slots, sem):
        spread(msg, slots, sem, zpeers, z, lambda p: (p, a))

    def spread_a(msg, slots, sem):
        spread(msg, slots, sem, apeers, a, lambda p: (z, p))

    def all_of(slots, sem, count):
        most = slots.at[pl.ds(0, count)]
        return pltpu.make_async_remote_copy(src_ref=most, dst_ref=most, send_sem=sem.at[0], recv_sem=sem.at[1],
                                            device_id=(z, right), device_id_type=MESH)

    spread_z(stmsg.at[0], stz, stzsem)

    top, bottom = pl.ds(0, HALO), pl.ds(EROWS - HALO, HALO)
    inner = pl.ds(HALO, ROWS)
    first_rows, last_rows = pl.ds(HALO, HALO), pl.ds(ROWS, HALO)
    low_cols, high_cols = pl.ds(0, 128), pl.ds(COLS - 128, 128)
    whole_cols = pl.ds(0, COLS)
    send(cext.at[first_rows, whole_cols], cext.at[bottom, whole_cols], 1, (up, a))
    send(cext.at[last_rows, whole_cols], cext.at[top, whole_cols], 1, (down, a))
    send(cext.at[inner, low_cols], cright.at[inner, :], 1, (z, left))
    send(cext.at[inner, high_cols], cleft.at[inner, :], 1, (z, right))
    send(cext.at[first_rows, low_cols], cright.at[bottom, :], 1, (up, left))
    send(cext.at[first_rows, high_cols], cleft.at[bottom, :], 1, (up, right))
    send(cext.at[last_rows, low_cols], cright.at[top, :], 1, (down, left))
    send(cext.at[last_rows, high_cols], cleft.at[top, :], 1, (down, right))

    exchanged(0).wait_recv()
    xlow, xhigh = close_across(6)
    close_along(6)
    for load in loads[2:4]:
        load.wait()

    def wide(tile):
        return jnp.concatenate([tile] * 4, axis=1)

    er[0] = xlow
    er[1] = xhigh

    def second(i):
        rows = pl.ds(i * 16, 16)
        inner16 = pl.ds(i * 16 + FPAD, 16)
        wl, wr = wide(exlv[rows, :]), wide(exrv[rows, :])
        gx = [hx[k, rows, :] + (wl * er[0, k:k + 1, :] + wr * er[1, k:k + 1, :]) for k in range(6)]
        gy = [hy[k, rows, :] for k in range(6)]
        depth = dep[rows, :]
        rate = -(gx[1] + gy[1])
        active = (ov[rows, :] * (1 - cv[rows, :])).astype(F32)
        weight = BREAKING * active * depth * jnp.abs(rate) * depth
        sxx = 2.0 * weight * gx[2]
        sxy = weight * (gy[2] + gx[3])
        syy = 2.0 * weight * gy[3]
        ratev[rows, :] = -rate
        stress[0, inner16, :] = sxx
        stress[1, inner16, :] = sxy
        stress[2, inner16, :] = syy
        part[0, rows, :] = -gx[4] - gy[4] - depth * gx[0]
        part[1, rows, :] = -gx[5] - gy[5] - depth * gy[0]
        for k, f in enumerate((sxy, syy)):
            high, low = split_bf16(lane_source(f))
            syh[k, rows, :] = high
            syl[k, rows, :] = low

    for i in range(ROWS // 16):
        second(i)
    rate_out = pltpu.make_async_copy(ratev, out.at[0], outsem.at[0])
    rate_out.start()
    all_of(stz, stzsem, nz - 1).wait_recv()
    stmsg[1] = functools.reduce(lambda s, k: s + stz[k], range(1, nz), stz[0])
    spread_a(stmsg.at[1], sta, stasem)

    across_sources(stress, (0, 1))
    solves(2)
    edges_in(stress, (0, 1), (1, 2))

    def packed(items):
        row = iota(items[0].shape, 0)
        return jnp.where(row < 2, items[0], jnp.where(row < 4, rolled(items[1], 2, 0), jnp.where(
            row < 6, rolled(items[2], 4, 0), rolled(items[3], 6, 0)))), items[4]

    for e, own in ((er, rown), (ec, cown)):
        for end in range(2):
            cells = [e[4 * end + j] for j in range(4)]
            own[end, 0], own[end, 1] = packed((cells[0], cells[1], *edge_items(cells), e[8 + end]))

    def third(i):
        rows = pl.ds(i * 16, 16)
        ext = pl.ds(i * 16 + HALO, 16)
        fx = part[0, rows, :] + hx[0, rows, :] + hy[0, rows, :]
        fy = part[1, rows, :] + hx[1, rows, :] + hy[1, rows, :]
        bx[ext, 0:COLS] = fx
        by[ext, 0:COLS] = fy
        lane = iota((16, 128), 1)
        fmsg[0, rows, :] = jnp.where(lane < 64, fx[:, 0:128], rolled(fy[:, 0:128], 64, 1))
        fmsg[1, rows, :] = jnp.where(lane < 64, rolled(fy[:, COLS - 128:], 64, 1), fx[:, COLS - 128:])

    for i in range(ROWS // 16):
        third(i)
    lo8, hi8 = pl.ds(0, HALO), pl.ds(ROWS - HALO, HALO)
    ends = pl.ds(0, 2)
    exchanges = []
    for who, side in (((z, left), 0), ((z, right), 1)):
        exchanges.append((fmsg.at[side], (fleft if side else fright).at[inner, :], who))
    for who, low, vert in (((up, left), 1, 0), ((up, right), 0, 0), ((down, left), 1, 1), ((down, right), 0, 1)):
        cols = low_cols if low else high_cols
        side = 0 if low else 1
        exchanges += [
            (rown.at[vert, ends, :, cols], rst.at[side, 3 - vert], who),
            (cown.at[1 - low], cst.at[vert, 2 + low], who),
            (fmsg.at[side, hi8 if vert else lo8, :], (fright if low else fleft).at[top if vert else bottom, :], who),
        ]
    for who, side in (((z, left), 0), ((z, right), 1)):
        cols = high_cols if side else low_cols
        exchanges += [
            (cown.at[side], coth.at[1 - side], who),
            (rown.at[ends, ends, :, cols], rst.at[side, ends], who),
        ]
    for who, vert in (((up, a), 0), ((down, a), 1)):
        rows, place = (last_rows, top) if vert else (first_rows, bottom)
        exchanges += [
            (rown.at[vert], roth.at[1 - vert], who),
            (cown, cst.at[vert, ends], who),
            (bx.at[rows, whole_cols], bx.at[place, whole_cols], who),
            (by.at[rows, whole_cols], by.at[place, whole_cols], who),
        ]
    for src, dst, who in exchanges:
        send(src, dst, 2, who)

    exchanged(1).wait_recv()

    def wide5(tile):
        return jnp.concatenate([tile] * 5, axis=1)

    sub = iota((8, ECOLS), 0)
    lanes = iota((8, 128), 1)

    def gathered_c(i):
        rows = pl.ds(i * 8, 8)
        side = jnp.where(lanes < 64, cright[rows, :], cleft[rows, :])
        c = jnp.concatenate([cext[rows, 0:COLS], side], axis=1)
        if i == 0:
            c = c * has_up
        if i == EROWS // 8 - 1:
            c = c * has_down
        cs[rows, :] = c
        crec[rows, :] = 1.0 / c

    for i in range(EROWS // 8):
        gathered_c(i)
    all_of(sta, stasem, na - 1).wait_recv()
    total = functools.reduce(lambda s, k: s + sta[k], range(1, na), sta[0])
    weight_c = jnp.broadcast_to(total[0:1, 0:1], (8, 128))
    weight_e = jnp.broadcast_to(total[4:5, 0:1], (8, 128))
    top_value = jnp.where(weight_e > 0.0, 10.0 * weight_c / weight_e, 100.0)
    half_top = 0.5 * top_value
    shrink = 1.0 / half_top
    shrink5 = wide5(shrink)

    exchanged(2).wait_recv()

    def unpacked(tiles):
        return [rolled(tiles[0], -2 * j, 0) for j in range(4)] + [tiles[1]]

    def interface(before, after, keep):
        l0, l1, t0, t1, hl = before
        f0, f1, s0, s1, hf = after
        inflow, inflow1 = A2 * l0 + B4 * l1, B4 * l0
        outflow, outflow1 = A2 * f0 + B4 * f1, B4 * f0
        low0, low1 = s0 - keep * inflow, s1 - keep * inflow1
        high0, high1 = keep * outflow - t0, keep * outflow1 - t1
        own_low = hf + CORNER * low0 + NEXT * low1
        own_high = hl + CORNER * high0 + NEXT * high1
        bare_high = hl - CORNER * t0 - NEXT * t1 + CORNER * outflow + NEXT * outflow1
        bare_low = hf + CORNER * s0 + NEXT * s1 - CORNER * inflow - NEXT * inflow1
        gp = (bare_high - LINK * own_low) * COUPLE * keep
        gn = (bare_low - LINK * own_high) * COUPLE * keep
        return (low0 - low1 * (1.0 / Q) - Q * gp, low1 * (1.0 / Q), high0 - high1 * (1.0 / Q) - Q * gn, high1 * (1.0 / Q))

    def extended(body, stage_, slot):
        return unpacked([jnp.concatenate([body[t], jnp.where(lanes < 64, stage_[0, slot, t], stage_[1, slot, t])], axis=1)
                         for t in range(2)])

    tops = interface(extended(roth.at[0], rst, 2), extended(rown.at[0], rst, 0), has_up)
    bottoms = interface(extended(rown.at[1], rst, 1), extended(roth.at[1], rst, 3), has_down)
    lefts = interface(extended(coth.at[0], cst, 2), extended(cown.at[0], cst, 0), 1.0)
    rights = interface(extended(cown.at[1], cst, 1), extended(coth.at[1], cst, 3), 1.0)
    stacked = jnp.concatenate(list(lefts) + list(rights) + [jnp.zeros((64, 256), F32)], axis=0)
    turned_own, turned_side = stacked[:, 0:128].T, stacked[:, 128:256].T
    ey0, ey1 = eyv[0:1, :], eyv[1:2, :]

    def closed(i):
        rows = pl.ds(8 * i, 8)
        r = 8 * (i - 1)
        from_right, from_left = fright[rows, :], fleft[rows, :]
        side = (jnp.where(lanes < 64, from_right, from_left),
                jnp.where(lanes < 64, rolled(from_right, 64, 1), rolled(from_left, 64, 1)))
        block = turned_side[120:128] if i == 0 else turned_side[0:8] if i == EROWS // 8 - 1 else turned_own[r:r + 8]
        for k, (src, dst) in enumerate(((bx, bx2), (by, by2))):
            def term(which):
                return which[k:k + 1, :]

            def col(c):
                return jnp.broadcast_to(block[:, 8 * c + k:8 * c + k + 1], (8, 128))

            if i == 0:
                across = wide5(exrv[120:128, :]) * term(tops[2]) + jnp.where(sub == 7, term(tops[3]), 0.0)
            elif i == EROWS // 8 - 1:
                across = wide5(exlv[0:8, :]) * term(bottoms[0]) + jnp.where(sub == 0, term(bottoms[1]), 0.0)
            else:
                across = wide5(exlv[r:r + 8, :]) * term(tops[0]) + wide5(exrv[r:r + 8, :]) * term(bottoms[2])
                if i == 1:
                    across = across + jnp.where(sub == 0, term(tops[1]), 0.0)
                if i == EROWS // 8 - 2:
                    across = across + jnp.where(sub == 7, term(bottoms[3]), 0.0)
            low = col(0) * ey0 + jnp.where(lanes == 0, col(1), 0.0)
            high = col(6) * ey1 + jnp.where(lanes == 127, col(7), 0.0)
            beyond = jnp.where(lanes < 64, col(4) * ey0 + jnp.where(lanes == 0, col(5), 0.0),
                               col(2) * ey1 + jnp.where(lanes == 127, col(3), 0.0))
            nothing = jnp.zeros((8, 128), F32)
            along = jnp.concatenate([low, nothing, nothing, high, beyond], axis=1)
            value = jnp.concatenate([src[rows, 0:COLS], side[k]], axis=1) + (across + along)
            if k == 0 and i == EROWS // 8 - 1:
                value = value * has_down
            dst[rows, :] = value

    for i in range(EROWS // 8):
        closed(i)

    def tile_at(ref, i):
        return ref[8 * i:8 * i + 8, :]

    def below_of(x, nxt):
        return jnp.where(sub == 7, rolled(nxt, -1, 0), rolled(x, -1, 0))

    def above_of(x, prv):
        return jnp.where(sub == 0, rolled(prv, 1, 0), rolled(x, 1, 0))

    TILES = EROWS // 8

    def inside(t):
        return t[:, 0:COLS]

    nil8 = jnp.zeros((8, COLS), F32)
    norm, sums = nil8, nil8
    wx = tile_at(bx2, 0)
    for i in range(TILES):
        nxt = tile_at(bx2, min(i + 1, TILES - 1))
        wy = tile_at(by2, i)
        c = tile_at(cs, i) * shrink5
        cs[8 * i:8 * i + 8, :] = c
        t = c * ((below_of(wx, nxt) - wx) + (rolled(wy, -1, 1) - wy))
        tau[0, 8 * i:8 * i + 8, :] = t
        if 0 < i < TILES - 1:
            norm = norm + (inside(wx) * inside(wx) + inside(wy) * inside(wy))
            sums = sums + inside(t) * (inside(t) * inside(tile_at(crec, i)))
        wx = nxt
    acc[0] = sums
    acc[15] = norm
    last_diag = jnp.where((sub == 7) & (z == nz - 1), 3.0, 4.0)

    def sweep(k, start):
        cross_sum, square_sum = nil8, nil8
        first_tile, stop = (1, TILES - 1) if start == 2 else (0, TILES)
        prv = tau[k, 8 * max(first_tile - 1, 0):8 * max(first_tile - 1, 0) + 8, :]
        x = tau[k, 8 * first_tile:8 * first_tile + 8, :]
        for i in range(first_tile, stop):
            j = min(i + 1, TILES - 1)
            nxt = tau[k, 8 * j:8 * j + 8, :]
            around = (above_of(x, prv) + below_of(x, nxt)) + (rolled(x, -1, 1) + rolled(x, 1, 1))
            diag = last_diag if i == TILES - 2 else 4.0
            t = tile_at(cs, i) * (diag * x - around) - x
            if start > 0:
                t = 2.0 * t - tau[k - 1, 8 * i:8 * i + 8, :]
            tau[k + 1, 8 * i:8 * i + 8, :] = t
            if 0 < i < TILES - 1:
                q = inside(t) * inside(tile_at(crec, i))
                cross_sum = cross_sum + inside(x) * q
                square_sum = square_sum + inside(t) * q
            prv, x = x, nxt
        acc[2 * k + 1] = cross_sum
        acc[2 * k + 2] = square_sum

    sweep(0, 0)

    def sweeps(k, _):
        sweep(k, 1)
        return 0

    lax.fori_loop(1, ITERS - 2, sweeps, 0)
    sweep(ITERS - 2, 2)
    dots = [acc[k] for k in range(16)]

    def fold(t):
        s0 = dd_gather(two_sum(t[:, 0:128], t[:, 128:256]), two_sum(t[:, 256:384], t[:, 384:512]))
        return s0

    level = [fold(t) for t in dots]
    for width, span in ((8, 4), (4, 2), (2, 1)):
        mask = sub8 % (2 * span) < span

        def merge(p, q, mask=mask, span=span):
            def parts(g, h):
                w = jnp.where(mask, h, g)
                return jnp.where(mask, g, h), jnp.where(mask, rolled(w, -span, 0), rolled(w, span, 0))
            xh_, yh_ = parts(p[0], q[0])
            xl_, yl_ = parts(p[1], q[1])
            return dd_gather((xh_, xl_), (yh_, yl_))

        level = [merge(level[i], level[i + width]) for i in range(width)]
    for s in (64, 32, 16, 8, 4, 2, 1):
        level = [dd_gather(p, (rolled(p[0], s, 1), rolled(p[1], s, 1))) for p in level]
    even, odd = [quick_sum(*p) for p in level]

    dtmsg[0] = jnp.where(lane8 < 32, even[0], jnp.where(lane8 < 64, odd[0], jnp.where(lane8 < 96, even[1], odd[1])))
    spread_z(dtmsg.at[0], dtz, dtzsem)
    all_of(dtz, dtzsem, nz - 1).wait_recv()

    def gathered(slots, count):
        level = [(slots[k], rolled(slots[k], 64, 1)) for k in range(count)]
        while len(level) > 1:
            level = [dd_gather(level[2 * i], level[2 * i + 1]) for i in range(len(level) // 2)]
        return quick_sum(*level[0])

    sums = gathered(dtz, nz)
    dtmsg[1] = jnp.where(lane8 < 64, sums[0], rolled(sums[1], 64, 1))
    spread_a(dtmsg.at[1], dta, dtasem)
    all_of(dta, dtasem, na - 1).wait_recv()
    sums = gathered(dta, na)

    def pick(value, lane):
        return jnp.broadcast_to(value[:, lane:lane + 1], (8, 128))

    def row_of(value, r):
        return tuple(jnp.broadcast_to(part_[r:r + 1, :], (8, 128)) for part_ in value)

    even = pick(sums[0], 0), pick(sums[1], 0)
    odd = pick(sums[0], 32), pick(sums[1], 32)
    square = row_of(odd, 7)
    even, odd = dd_scale(even, half_top), dd_scale(odd, half_top)
    even = dd_add((2.0 * even[0], 2.0 * even[1]), dd_neg(row_of(even, 0)))
    odd = dd_add((2.0 * odd[0], 2.0 * odd[1]), dd_neg(row_of(odd, 0)))

    MOM, SEC, GRAM, MIX = range(4)
    nsc[...] = jnp.zeros(nsc.shape, F32)
    for part_ in range(2):
        for j in range(15):
            value = (even, odd)[j % 2][part_][j // 2:j // 2 + 1, :]
            nsc[MOM, part_, 8 + j:9 + j, :] = value
            if j == 1:
                nsc[MOM, part_, 7:8, :] = value

    def entries(which, start, count=8):
        return nsc[which, 0, start:start + count, :], nsc[which, 1, start:start + count, :]

    def widened(which, start):
        return dd_add(entries(which, start), dd_half(dd_add(entries(which, start + 1), entries(which, start - 1))))

    for start in (8, 16):
        value = widened(MOM, start)
        nsc[SEC, 0, start:start + 8, :], nsc[SEC, 1, start:start + 8, :] = value
        mix = dd_add(entries(MOM, start), dd_scale(value, half_top))
        nsc[MIX, 0, start:start + 8, :], nsc[MIX, 1, start:start + 8, :] = mix
    for part_ in range(2):
        nsc[SEC, part_, 7:8, :] = nsc[SEC, part_, 9:10, :]
    for start in (8, 16):
        value = dd_add(entries(SEC, start), dd_scale(widened(SEC, start), half_top))
        nsc[GRAM, 0, start:start + 8, :], nsc[GRAM, 1, start:start + 8, :] = value
    for part_ in range(2):
        for j in range(1, 8):
            nsc[GRAM, part_, 8 - j:9 - j, :] = nsc[GRAM, part_, 8 + j:9 + j, :]

    def with_first(value, head):
        return tuple(jnp.where(sub8 == 0, h, v) for v, h in zip(value, head))

    moment0 = row_of(entries(MOM, 8), 0)
    matrix = [with_first(entries(MIX, 7), dd_add(square, dd_scale(moment0, half_top)))]
    for l in range(ITERS - 1):
        column = dd_half(dd_add(entries(GRAM, 7 + l), entries(GRAM, 7 - l)))
        matrix.append(with_first(column, row_of(entries(MIX, 8 + l), 0)))
    right_side = with_first(entries(MOM, 7), square)
    diagonal = jnp.zeros((8, 128), F32)
    first_diagonal = [row_of(matrix[k], k)[0] for k in range(ITERS)]
    for k in range(ITERS):
        pivot = row_of(matrix[k], k)
        usable = pivot[0] > 1e-11 * first_diagonal[k]
        safe = jnp.where(usable, pivot[0], 1.0), jnp.where(usable, pivot[1], 0.0)
        factor = dd_div(matrix[k], safe)
        skip = (sub8 == k) | jnp.logical_not(usable)
        factor = tuple(jnp.where(skip, 0.0, f) for f in factor)
        diagonal = jnp.where((sub8 == k) & usable, pivot[0], diagonal)
        for l in range(k + 1, ITERS):
            matrix[l] = dd_add(matrix[l], dd_neg(dd_mul(factor, row_of(matrix[l], k))))
        right_side = dd_add(right_side, dd_neg(dd_mul(factor, row_of(right_side, k))))
    answer = jnp.where(diagonal > 0.0, right_side[0] / jnp.where(diagonal > 0.0, diagonal, 1.0), 0.0)
    nsc[MOM, 0, 0:8, :] = answer

    weights = [jnp.broadcast_to(nsc[MOM, 0, k:k + 1, :], (8, 128)) for k in range(ITERS)]

    def combined(j, w):
        return functools.reduce(lambda s, t: s + t, [w[l + 1] * tau[l, 8 * j:8 * j + 8, :] for l in range(ITERS - 1)])

    w5 = [wide5(w) for w in weights]
    gain = wide(weights[0])
    solved_out = []
    prv = combined(0, w5)
    for i in range(ROWS // 8):
        here = combined(i + 1, w5)
        solv[0, 8 * i:8 * i + 8, :] = inside(here - above_of(here, prv)) - gain * inside(tile_at(bx2, i + 1))
        solv[1, 8 * i:8 * i + 8, :] = inside(here - rolled(here, 1, 1)) - gain * inside(tile_at(by2, i + 1))
        prv = here
        if i % 4 == 3:
            piece = pl.ds(8 * (i - 3), 32)
            solved_out.append(pltpu.make_async_copy(solv.at[:, piece, :], out.at[pl.ds(1, 2), piece, :], outsem.at[1 + i // 4]))
            solved_out[-1].start()
    for copy in [exchanged(0), exchanged(1), exchanged(2), all_of(stz, stzsem, nz - 1), all_of(sta, stasem, na - 1), all_of(dtz, dtzsem, nz - 1), all_of(dta, dtasem, na - 1)]:
        copy.wait_send()
    rate_out.wait()
    for copy in solved_out:
        copy.wait()


def per_device(nz, na, wave_state, depth_class, onset_flag, cessation, class_depth):
    across, along = tridiagonal_inverse(ROWS), tridiagonal_inverse(COLS)
    xhl = np.concatenate(halves(derivative_matrix(ROWS)), axis=0)
    yh, yl = halves(derivative_matrix(COLS).T)
    exl = np.repeat(across[:, :1], 128, axis=1).astype(np.float32)
    exr = np.repeat(across[:, -1:], 128, axis=1).astype(np.float32)
    ey = np.zeros((8, 128), np.float32)
    ey[0] = along[0, :128]
    ey[1] = along[-1, -128:]
    consts = [jnp.asarray(t) for t in (xhl, yh, yl, exl, exr, ey)]
    dma = pltpu.SemaphoreType.DMA

    def vm(*shape, dtype=F32):
        return pltpu.VMEM(shape, dtype)

    scratch = [
        vm(3, ROWS, COLS), vm(ROWS, COLS, dtype=jnp.int32), vm(ROWS, COLS, dtype=jnp.int32), vm(ROWS, COLS, dtype=jnp.int32),
        vm(2 * ROWS, ROWS, dtype=BF16), vm(COLS, COLS, dtype=BF16), vm(COLS, COLS, dtype=BF16),
        vm(ROWS, 128), vm(ROWS, 128), vm(8, 128),
        vm(8, ROWS + 2 * FPAD, COLS), vm(ROWS, COLS),
        vm(6, ROWS, COLS, dtype=BF16), vm(6, ROWS, COLS, dtype=BF16), vm(6, ROWS, COLS, dtype=BF16), vm(6, ROWS, COLS, dtype=BF16),
        vm(6, ROWS, COLS), vm(6, ROWS, COLS), vm(10, 8, COLS), vm(10, 8, 128),
        vm(3, ROWS + 2 * FPAD, COLS), vm(2, ROWS, COLS), vm(ROWS, COLS), vm(2, ROWS, COLS),
        vm(2, 3, 8, COLS), vm(2, 3, 8, COLS), vm(2, 3, 8, 128), vm(2, 3, 8, 128),
        vm(2, 2, 8, COLS), vm(2, 2, 8, COLS), vm(2, 4, 2, 8, 128), vm(2, 2, 8, 128), vm(2, 2, 8, 128), vm(2, 4, 2, 8, 128),
        vm(EROWS, ECOLS), vm(EROWS, ECOLS),
        vm(EROWS, ECOLS), vm(EROWS, ECOLS), vm(EROWS, ECOLS), vm(EROWS, ECOLS),
        vm(EROWS, 128), vm(EROWS, 128), vm(EROWS, 128), vm(EROWS, 128), vm(2, ROWS, 128),
        vm(ITERS, EROWS, ECOLS), vm(EROWS, ECOLS), vm(16, 8, COLS),
        vm(2, 8, 128), vm(nz, 8, 128), vm(na, 8, 128), vm(2, 8, 128), vm(nz, 8, 128), vm(na, 8, 128), vm(4, 2, 32, 128),
        dma((10,)), dma((5,)), dma((3,)), dma((3,)),
        dma((2,)), dma((2,)), dma((2,)), dma((2,)),
    ]
    anywhere = pl.BlockSpec(memory_space=pl.ANY)
    negated = pl.pallas_call(
        functools.partial(kernel, nz, na),
        out_shape=jax.ShapeDtypeStruct((3, ROWS, COLS), F32),
        in_specs=[anywhere] * 4 + [pl.BlockSpec(memory_space=pltpu.SMEM)] + [anywhere] * 6,
        out_specs=anywhere,
        scratch_shapes=scratch,
        compiler_params=pltpu.CompilerParams(collective_id=0, has_side_effects=True, vmem_limit_bytes=VMEM_BYTES),
    )(wave_state, depth_class, onset_flag, cessation, class_depth, *consts)
    return -negated


def solution(mesh):
    sizes = dict(mesh.shape)
    in_specs = (P(None, "xs", "al"), P("xs", "al"), P("xs", "al"), P("xs", "al"), P())
    return jax.shard_map(
        functools.partial(per_device, sizes["xs"], sizes["al"]),
        mesh=mesh, in_specs=in_specs, out_specs=P(None, "xs", "al"), check_vma=False,
    )
```
